32 devices in a mesh: section: 2 (over y), tensor: 4 (over x, core), dp: 4 (over z).
Axes of the slice: x: 2, y: 2, z: 4, core: 2. Of those that a mesh axis runs over, the one named last changes fastest.
Arguments:
- tokens: bfloat16 [8, 512, 1024], P('dp', 'tensor'), may hold values from -6 to 6
- segment: int32 [8, 512], P('dp'), may hold values from -1 to 15, as said below
- score_grad: float32 [64, 4], P('dp'), may hold values from -96 to 96
- qkv_weight: bfloat16 [2, 1024, 3, 1024], P('section', None, None, 'tensor'), may hold values from -0.1875 to 0.1875
- qkv_bias: bfloat16 [2, 3, 1024], P('section', None, 'tensor'), may hold values from -4 to 4
- out_weight: bfloat16 [2, 1024, 1024], P('section', 'tensor'), may hold values from -3 to 3
- up_weight: bfloat16 [2, 1024, 4096], P('section', None, 'tensor'), may hold values from -0.1875 to 0.1875
- up_bias: bfloat16 [2, 4096], P('section', 'tensor'), may hold values from -4 to 4
- down_weight: bfloat16 [2, 4096, 1024], P('section', 'tensor'), may hold values from -0.09375 to 0.09375
- out_bias: bfloat16 [2, 2, 1024], P('section'), may hold values from -4 to 4
- norm_gain: bfloat16 [2, 2, 1024], P('section'), may hold values from 0.5 to 1.5
- norm_shift: bfloat16 [2, 2, 1024], P('section'), may hold values from -4 to 4
- proj_weight: bfloat16 [1024, 128], replicated, may hold values from -0.1875 to 0.1875
Outputs:
- scores: float32 [64, 4], P('dp', 'section')
- input_grad: float32 [8, 512, 1024], P('dp', 'tensor', 'section')
- qkv_weight_grad: float32 [2, 1024, 3, 1024], P('section', None, None, 'tensor')
- qkv_bias_grad: float32 [2, 3, 1024], P('section', None, 'tensor')
- out_weight_grad: float32 [2, 1024, 1024], P('section', 'tensor')
- up_weight_grad: float32 [2, 1024, 4096], P('section', None, 'tensor')
- up_bias_grad: float32 [2, 4096], P('section', 'tensor')
- down_weight_grad: float32 [2, 4096, 1024], P('section', 'tensor')
- out_bias_grad: float32 [2, 2, 1024], P('section')
- norm_gain_grad: float32 [2, 2, 1024], P('section')
- norm_shift_grad: float32 [2, 2, 1024], P('section')
- proj_weight_grad: float32 [1024, 128], P('section')
The draws below stay inside these ranges and needn't reach their ends.
Inputs may be any that keep to these rules, and one draw needn't show every extreme that they name: `segment`: block 2g is group g's document: its first L positions are 0 and the rest -1, with 384 < L <= 512; L = 512 in some group and L is the least allowed value in another. Block 2g + 1 is group g's queries: its first c query slots are live, 8 <= c (and c >= 1), c = 16 in some group; live query q marks positions q * 32 to q * 32 + l - 1 with q, where 32 // 2 <= l; every other position is -1.
All inputs are finite; a program needn't handle non-finite values.
Results may differ from the reference program's by a relative error of at most 0.015.
Values may be sent and summed in bfloat16 or wider, within the bound.
No kernel may reach another device: no remote copies, remote signals or barrier semaphores. Data moves between devices by JAX's collectives and lax.ppermute only.
A program may use at most 192 MiB of HBM per device.

```python
import jax
import jax.numpy as jnp
from jax import lax

D = 1024
HEADS = 16
HD = 64
FF = 4096
PROJ = 128
QLEN = 32
MB_TOK = 512
SLOTS = 8
QB = 16
QUERIES = 64
N_SECTION = 2
N_TENSOR = 4
N_DP = 4


def draw_segment(key, part):
    key = jax.random.fold_in(key, 7)
    keys = jax.random.split(key, 5)
    groups = SLOTS // 2
    query_slots = MB_TOK // QLEN
    shortest = MB_TOK - MB_TOK // N_TENSOR + 1
    group_index = jnp.arange(groups)
    lengths = jax.random.randint(keys[0], (groups,), shortest, MB_TOK + 1)
    longest = jax.random.randint(keys[1], (), 0, groups)
    lengths = jnp.where(group_index == longest, MB_TOK, lengths)
    lengths = jnp.where(group_index == (longest + 1) % groups, shortest, lengths)
    live_count = jax.random.randint(keys[2], (groups,), max(query_slots // 2, 1), query_slots + 1)
    fullest = jax.random.randint(keys[3], (), 0, groups)
    live_count = jnp.where(group_index == fullest, query_slots, live_count)
    query_lengths = jax.random.randint(keys[4], (groups, query_slots), QLEN // 2, QLEN + 1)
    position = jnp.arange(MB_TOK)
    documents = jnp.where(position[None, :] < lengths[:, None], 0, -1)
    query_owner = position // QLEN
    within = position % QLEN
    query_alive = (query_owner[None, :] < live_count[:, None]) & (within[None, :] < query_lengths[:, query_owner])
    queries = jnp.where(query_alive, query_owner[None, :], -1)
    return jnp.stack([documents, queries], axis=1).reshape(SLOTS, MB_TOK).astype(jnp.int32)


def block_scale(stream_key, extent, shards, smallest, top_value):
    gain = 1.0
    for dim, shards_of in shards:
        draws = jax.random.uniform(jax.random.fold_in(jax.random.fold_in(stream_key, 6), dim), (shards_of,), jnp.float32, smallest / len(shards), top_value / len(shards))
        gain = gain * jnp.repeat(jnp.exp(draws), extent[dim] // shards_of).reshape((-1,) + (1,) * (len(extent) - 1 - dim))
    return gain


def normal_values(own_key, shape, deviation, bound, cuts=(), kind=jnp.bfloat16):
    factor_of = block_scale(own_key, shape, cuts, -0.22, 0.18) if cuts else 1.0
    array = jax.random.normal(own_key, shape, jnp.float32) * deviation * factor_of
    return jnp.minimum(jnp.maximum(array, -bound), bound).astype(kind)


def setup_inputs(seed: int = 0) -> dict:
    streams_of = jax.random.split(jax.random.key(seed), 14)
    tokens = normal_values(streams_of[0], (SLOTS, MB_TOK, D), 1.0, 6.0, ((0, 4), (1, 4)))
    segment = draw_segment(jax.random.fold_in(streams_of[13], 71), 0)
    score_grad = normal_values(streams_of[2], (QUERIES, N_DP), 16.0, 96.0, ((0, 4),), jnp.float32)
    qkv_weight = normal_values(streams_of[3], (N_SECTION, D, 3, D), D ** -0.5, 0.1875, ((0, 2), (3, 4)))
    qkv_bias = normal_values(streams_of[4], (N_SECTION, 3, D), 0.3, 4.0, ((0, 2), (2, 4)))
    out_weight = normal_values(streams_of[5], (N_SECTION, D, D), (max(D // 256, 1)) ** -0.5, 3.0, ((0, 2), (1, 4)))
    up_weight = normal_values(streams_of[6], (N_SECTION, D, FF), D ** -0.5, 0.1875, ((0, 2), (2, 4)))
    up_bias = normal_values(streams_of[7], (N_SECTION, FF), 0.3, 4.0, ((0, 2), (1, 4)))
    down_weight = normal_values(streams_of[8], (N_SECTION, FF, D), FF ** -0.5, 0.09375, ((0, 2), (1, 4)))
    out_bias = normal_values(streams_of[9], (N_SECTION, 2, D), 0.3, 4.0, ((0, 2),))
    norm_gain = jnp.clip(1.0 + 0.1 * jax.random.normal(streams_of[10], (N_SECTION, 2, D), jnp.float32), 0.5, 1.5).astype(jnp.bfloat16)
    norm_shift = normal_values(streams_of[11], (N_SECTION, 2, D), 0.3, 4.0, ((0, 2),))
    proj_weight = normal_values(streams_of[12], (D, PROJ), D ** -0.5, 0.1875)
    return dict(tokens=tokens, segment=segment, score_grad=score_grad, qkv_weight=qkv_weight, qkv_bias=qkv_bias, out_weight=out_weight, up_weight=up_weight, up_bias=up_bias, down_weight=down_weight, out_bias=out_bias, norm_gain=norm_gain, norm_shift=norm_shift, proj_weight=proj_weight)


norm_eps = 1e-05
unit_eps = 1e-06
softness_factor = 0.0625
rope_base = 10000.0
hidden_score = -1000000000.0
highest = lax.Precision.HIGHEST

@jax.custom_vjp
def low(v):
    return lax.optimization_barrier(v.astype(jnp.bfloat16)).astype(jnp.float32)

@jax.custom_vjp
def low_back(v):
    return v

def low_keep(v):
    return (low(v), None)

def low_pass(kept, grad):
    return (grad,)

def back_keep(v):
    return (v, None)

def back_low(kept, grad):
    return (low(grad),)
low.defvjp(low_keep, low_pass)
low_back.defvjp(back_keep, back_low)

def rope_tables(positions, head_size):
    half_size = head_size // 2
    frequency = jnp.power(rope_base, -2.0 * jnp.arange(half_size, dtype=jnp.float32) / head_size)
    angles = positions.astype(jnp.float32)[:, None] * frequency[None, :]
    return (jnp.cos(angles)[:, None, :], jnp.sin(angles)[:, None, :])

def rotate(vectors, cosine_table, sine_table):
    half_size = vectors.shape[-1] // 2
    lower_half = vectors[..., :half_size]
    upper_half = vectors[..., half_size:]
    return jnp.concatenate([lower_half * cosine_table - upper_half * sine_table, upper_half * cosine_table + lower_half * sine_table], axis=-1)

def layer_norm(values, norm_gains, shifts):
    centred = values - lax.optimization_barrier(jnp.mean(values, axis=-1, keepdims=True))
    inverse = lax.rsqrt(lax.optimization_barrier(jnp.mean(centred * centred, axis=-1, keepdims=True)) + norm_eps)
    return centred * inverse * norm_gains + shifts

def encoder_block(hidden, seg_ids, cosine_table, sine_table, qkv_weight, qkv_bias, out_weight, up_weight, up_bias, down_weight, out_bias, norm_gain, norm_shift):
    block_rows, model_width = hidden.shape
    projected = low_back(jnp.dot(hidden, qkv_weight.reshape(model_width, 3 * model_width), precision=highest)) + qkv_bias.reshape(3 * model_width)
    projected = projected.reshape(block_rows, 3, HEADS, HD)
    queries = low(rotate(projected[:, 0], cosine_table, sine_table))
    key_rows = low(rotate(projected[:, 1], cosine_table, sine_table))
    value_rows = low(projected[:, 2])
    scores = low_back(jnp.einsum('qhd,khd->hqk', queries, key_rows, precision=highest) * HD ** (-0.5))
    allowed = seg_ids[:, None] == seg_ids[None, :]
    softmax = low(jax.nn.softmax(jnp.where(allowed[None], scores, hidden_score), axis=-1))
    mixed_heads = jnp.einsum('hqk,khd->qhd', softmax, value_rows, precision=highest).reshape(block_rows, model_width)
    mixed_heads = low(low_back(mixed_heads))
    first_sum = hidden + low_back(jnp.dot(mixed_heads, out_weight, precision=highest)) + out_bias[0]
    normed = layer_norm(first_sum, norm_gain[0], norm_shift[0])
    hidden_pre = low_back(jnp.dot(low(normed), up_weight, precision=highest)) + up_bias
    activated = low(jax.nn.gelu(hidden_pre, approximate=False))
    second_sum = normed + low_back(jnp.dot(activated, down_weight, precision=highest)) + out_bias[1]
    return layer_norm(second_sum, norm_gain[1], norm_shift[1])

def reference(tokens, segment, score_grad, qkv_weight, qkv_bias, out_weight, up_weight, up_bias, down_weight, out_bias, norm_gain, norm_shift, proj_weight):
    token_index = jnp.arange(MB_TOK)
    doc_tables = rope_tables(token_index, HD)
    query_tables = rope_tables(token_index % QLEN, HD)
    cosine_all = jnp.tile(jnp.stack([doc_tables[0], query_tables[0]]), (N_DP, 1, 1, 1))
    sine_all = jnp.tile(jnp.stack([doc_tables[1], query_tables[1]]), (N_DP, 1, 1, 1))
    members = (segment[1::2][:, :, None] == jnp.arange(QB)[None, None, :]).astype(jnp.float32)
    doc_alive = segment[0::2] == 0

    def forward(hidden, *params):

        def run(layer_index, states):
            chosen = [weight[layer_index] for weight in params[:9]]

            def one_block(entry_value):
                return encoder_block(entry_value[0], entry_value[1], entry_value[2], entry_value[3], *chosen)
            return lax.map(jax.checkpoint(one_block), (states, segment, cosine_all, sine_all))
        states = run(0, hidden)
        states = run(1, low(low_back(states)))
        projected = low_back(jnp.einsum('smd,dp->smp', low(states), params[9], precision=highest))
        unit_rows = low(projected * lax.rsqrt(lax.optimization_barrier(jnp.sum(projected * projected, axis=-1, keepdims=True)) + unit_eps))
        unit_rows = unit_rows.reshape(N_DP, 2, MB_TOK, PROJ)
        query_units = unit_rows[:, 1]

        def per_document(entry_value):
            similarity_matrix = low_back(jnp.einsum('gtp,kp->gtk', query_units, entry_value[0], precision=highest))
            score_logits = jnp.where(entry_value[1][None, None, :], similarity_matrix / softness_factor, hidden_score)
            smooth_maxima = softness_factor * jax.nn.logsumexp(score_logits, axis=-1)
            return jnp.einsum('gt,gtq->gq', smooth_maxima, members, precision=highest)
        columns = lax.map(jax.checkpoint(per_document), (unit_rows[:, 0], doc_alive))
        return jnp.transpose(columns, (1, 2, 0)).reshape(N_DP * QB, N_DP)
    floats = tuple((argument.astype(jnp.float32) for argument in (tokens, qkv_weight, qkv_bias, out_weight, up_weight, up_bias, down_weight, out_bias, norm_gain, norm_shift, proj_weight)))
    scores, pullback = jax.vjp(forward, *floats)
    gradients = pullback(score_grad)
    return (scores, gradients[0], gradients[1], gradients[2], gradients[3], gradients[4], gradients[5], gradients[6], gradients[7], gradients[8], gradients[9], gradients[10])
```

```python
import jax
import jax.numpy as jnp
import numpy as np
from jax import lax
from jax.sharding import PartitionSpec as P

HD = 64
QLEN = 32

norm_eps = 1e-05
unit_eps = 1e-06
softness_factor = 0.0625
rope_base = 10000.0
hidden_score = -1000000000.0
contract_rows = (((0,), (0,)), ((), ()))
contract_cols = (((1,), (1,)), ((), ()))
bf16 = jnp.bfloat16
f32 = jnp.float32


def dot(left, right, contraction=(((1,), (0,)), ((), ()))):
    return lax.dot_general(left, right, contraction, preferred_element_type=f32)


def flip(value, bit):
    count = lax.axis_size("tensor")
    return lax.ppermute(value, "tensor", [(i, i ^ (1 << bit)) for i in range(count)])


def chip_bits():
    return range(1, lax.axis_size("tensor").bit_length() - 1)


def core_other(value):
    return flip(value, 0)


def chips_gather(value, chip):
    for bit in chip_bits():
        other = flip(value, bit)
        upper = (chip >> (bit - 1)) % 2 == 1
        value = jnp.concatenate([jnp.where(upper, other, value), jnp.where(upper, value, other)], axis=0)
    return value


def chips_sum(value):
    for bit in chip_bits():
        low = value.astype(bf16)
        value = low.astype(f32) + flip(low, bit).astype(f32)
    return value


def to_section(value, pairs):
    return lax.ppermute(value, "section", pairs)


def rope_tables(positions):
    half = HD // 2
    frequency = np.power(np.float32(rope_base), (-2.0 * np.arange(half) / HD).astype(np.float32)).astype(np.float32)
    angles = (positions.astype(np.float32)[:, None] * frequency[None, :]).astype(np.float32)
    cosine, sine = np.cos(angles), np.sin(angles)
    return np.concatenate([cosine, cosine], 1).astype(np.float32), np.concatenate([-sine, sine], 1).astype(np.float32)


def halves_swapped(v):
    half = HD // 2
    return jnp.concatenate([v[..., half:], v[..., :half]], axis=-1)


def rotate(v, tables):
    return v * tables[0][:, None, :] + halves_swapped(v) * tables[1][:, None, :]


def rotate_back(v, tables):
    return v * tables[0][:, None, :] - halves_swapped(v) * tables[1][:, None, :]


def norm(values):
    centred = values - jnp.mean(values, axis=-1, keepdims=True)
    inverse = lax.rsqrt(jnp.mean(centred * centred, axis=-1, keepdims=True) + norm_eps)
    return centred * inverse, inverse


def norm_back(gradient, normed, inverse):
    return inverse * (
        gradient
        - jnp.mean(gradient, axis=-1, keepdims=True)
        - normed * jnp.mean(gradient * normed, axis=-1, keepdims=True)
    )


def gelu_slope(values):
    return 0.5 * (1.0 + lax.erf(values * 0.7071067811865476)) + values * jnp.exp(-0.5 * values * values) * 0.3989422804014327


def sum_over_tensor(rows_in, weight, contraction, half):
    other_part = dot(rows_in[half:], weight, contraction).astype(bf16)
    arrived = core_other(other_part)
    own_part = dot(rows_in[:half], weight, contraction) + arrived.astype(f32)
    return chips_sum(own_part)


def both_cores(rows):
    return jnp.concatenate([rows, core_other(rows)], axis=0)


def attend(h_all, w, seg_ids, tables):
    rows = h_all.shape[0]
    width = w["qkv"].shape[-1]
    shape = (rows, width // HD, HD)
    projected = dot(h_all, w["qkv"].reshape(h_all.shape[1], 3 * width)) + w["qkv_b"].reshape(3 * width)
    q = rotate(projected[:, :width].reshape(shape), tables).astype(bf16)
    k = rotate(projected[:, width : 2 * width].reshape(shape), tables).astype(bf16)
    v = projected[:, 2 * width :].reshape(shape).astype(bf16)
    scores = jnp.einsum("qhd,khd->hqk", q, k, preferred_element_type=f32) * HD ** (-0.5)
    allowed = seg_ids[:, None] == seg_ids[None, :]
    a = jax.nn.softmax(jnp.where(allowed[None], scores, hidden_score), axis=-1)
    a_low = a.astype(bf16)
    o = jnp.einsum("hqk,khd->qhd", a_low, v, preferred_element_type=f32).reshape(rows, width).astype(bf16)
    return q, k, v, a, a_low, o


def forward(h_own, w, seg_ids, tables):
    half = h_own.shape[0]
    h_all = both_cores(h_own)
    heads = attend(h_all, w, seg_ids, tables)
    s1 = h_own.astype(f32) + sum_over_tensor(heads[5], w["out"], (((1,), (0,)), ((), ())), half) + w["out_b"][0]
    n1, r1 = norm(s1)
    h1 = n1 * w["gain"][0] + w["shift"][0]
    h1_all = both_cores(h1.astype(bf16))
    u = dot(h1_all, w["up"]) + w["up_b"]
    g = jax.nn.gelu(u, approximate=False).astype(bf16)
    s2 = h1 + sum_over_tensor(g, w["down"], (((1,), (0,)), ((), ())), half) + w["out_b"][1]
    n2, r2 = norm(s2)
    y = n2 * w["gain"][1] + w["shift"][1]
    return y, (h_all, heads, n1, r1, h1_all, u, g, n2, r2)


def backward(dy, w, tables, record):
    h_all, (q, k, v, a, a_low, o), n1, r1, h1_all, u, g, n2, r2 = record
    half = dy.shape[0]
    rows, width = o.shape
    shape = (rows, width // HD, HD)
    gain2, shift2 = jnp.sum(dy * n2, axis=0), jnp.sum(dy, axis=0)
    ds2 = norm_back(dy * w["gain"][1], n2, r2)
    bias2 = jnp.sum(ds2, axis=0)
    f_all = both_cores(ds2.astype(bf16))
    du = dot(f_all, w["down"], contract_cols) * gelu_slope(u)
    u_low = du.astype(bf16)
    dh1 = ds2 + sum_over_tensor(u_low, w["up"], contract_cols, half)
    d_down = dot(g, f_all, contract_rows)
    d_up = dot(h1_all, u_low, contract_rows)
    d_up_b = jnp.sum(du, axis=0)
    gain1, shift1 = jnp.sum(dh1 * n1, axis=0), jnp.sum(dh1, axis=0)
    ds1 = norm_back(dh1 * w["gain"][0], n1, r1)
    bias1 = jnp.sum(ds1, axis=0)
    o_all = both_cores(ds1.astype(bf16))
    do = dot(o_all, w["out"], contract_cols).astype(bf16).reshape(shape)
    d_out = dot(o, o_all, contract_rows)
    da = jnp.einsum("qhd,khd->hqk", do, v, preferred_element_type=f32)
    dv = jnp.einsum("hqk,qhd->khd", a_low, do, preferred_element_type=f32)
    ds = a * (da - jnp.sum(da * a, axis=-1, keepdims=True))
    ds = ds.astype(bf16) * jnp.asarray(HD ** (-0.5), bf16)
    dq = rotate_back(jnp.einsum("hqk,khd->qhd", ds, k, preferred_element_type=f32), tables)
    dk = rotate_back(jnp.einsum("hqk,qhd->khd", ds, q, preferred_element_type=f32), tables)
    dp = jnp.concatenate([part.reshape(rows, width) for part in (dq, dk, dv)], axis=1)
    d_qkv_b = jnp.sum(dp, axis=0)
    dp_low = dp.astype(bf16)
    dh = ds1 + sum_over_tensor(dp_low, w["qkv"].reshape(w["qkv"].shape[0], 3 * width), contract_cols, half)
    d_qkv = dot(h_all, dp_low, contract_rows)
    return dh, (d_down, d_up, d_out, d_qkv), (d_up_b, d_qkv_b), jnp.stack([bias1, bias2, gain1, gain2, shift1, shift2])


def on_device(tokens, segment, score_grad, qkv_weight, qkv_bias, out_weight, up_weight, up_bias, down_weight, out_bias, norm_gain, norm_shift, proj_weight):
    w = dict(
        qkv=qkv_weight[0], qkv_b=qkv_bias[0].astype(f32), out=out_weight[0], up=up_weight[0], up_b=up_bias[0].astype(f32),
        down=down_weight[0], out_b=out_bias[0].astype(f32), gain=norm_gain[0].astype(f32), shift=norm_shift[0].astype(f32),
    )
    first = lax.axis_index("section") == 0
    device = lax.axis_index("tensor")
    core, chip = device % 2, device // 2
    blocks, share, model = tokens.shape
    chips = lax.axis_size("tensor") // 2
    groups = lax.axis_size("dp")
    half = share * chips
    rows = 2 * half
    proj = proj_weight.shape[1]

    def own_first(by_token):
        parts = by_token.reshape((chips, 2, share) + by_token.shape[1:])
        even = parts[:, 0].reshape((half,) + by_token.shape[1:])
        odd = parts[:, 1].reshape((half,) + by_token.shape[1:])
        return jnp.concatenate([jnp.where(core == 0, even, odd), jnp.where(core == 0, odd, even)], axis=0)

    index = np.arange(rows)
    tables = [tuple(own_first(jnp.asarray(part)) for part in rope_tables(p)) for p in (index, index % QLEN)]
    segments = [own_first(segment[b]) for b in range(2)]
    entering = [chips_gather(tokens[b], chip) for b in range(2)]

    def pick(zero, one):
        return (
            jnp.where(first, segments[zero], segments[one]),
            tuple(jnp.where(first, x, y) for x, y in zip(tables[zero], tables[one])),
        )

    contexts = [pick(0, 0), pick(1, 0), pick(1, 1)]
    received = jnp.zeros((half, model), bf16)
    records, outputs = [], []
    for tick in range(3):
        h_own = jnp.where(first, entering[min(tick, 1)], received)
        y, record = forward(h_own, w, *contexts[tick])
        records.append(record)
        outputs.append(y)
        if tick < 2:
            received = to_section(y.astype(bf16), [(0, 1)])

    def embed(y):
        low = y.astype(bf16)
        z = dot(low, proj_weight)
        inverse = lax.rsqrt(jnp.sum(z * z, axis=-1, keepdims=True) + unit_eps)
        return low, inverse, z * inverse

    def embed_back(low, inverse, units, gradient):
        dz = (inverse * (gradient - units * jnp.sum(gradient * units, axis=-1, keepdims=True))).astype(bf16)
        return dot(dz, proj_weight, contract_cols), dot(low, dz, contract_rows)

    doc = embed(outputs[1])
    query = embed(outputs[2])
    units_own = lax.all_gather(doc[2].astype(bf16), "dp", axis=0)
    units = jnp.stack([units_own, core_other(units_own)], axis=1).reshape(groups * rows, proj)
    alive_all = lax.all_gather((segments[0] == 0).astype(f32), "dp", axis=0).reshape(1, groups * rows)
    slots = score_grad.shape[0]
    member = (segments[1][:half, None] == jnp.arange(slots)[None, :]).astype(f32)
    token_grad = jnp.dot(member, score_grad, precision=lax.Precision.HIGHEST)
    query_low = query[2].astype(bf16)
    logits = jnp.where(alive_all > 0, dot(query_low, units, contract_cols) / softness_factor, hidden_score)
    logits = logits.reshape(half, groups, rows)
    peak = jnp.max(logits, axis=-1, keepdims=True)
    exps = jnp.exp(logits - peak)
    total = jnp.sum(exps, axis=-1, keepdims=True)
    smooth = softness_factor * (peak + jnp.log(total))[:, :, 0]
    board = lax.dot_general(member, smooth, contract_rows, precision=lax.Precision.HIGHEST, preferred_element_type=f32)
    pull = (exps / total * token_grad[:, :, None]).astype(bf16).reshape(half, groups * rows)
    query_grad = dot(pull, units)
    doc_terms = dot(pull, query_low, contract_rows).reshape(groups, 2, half, proj)
    doc_terms = doc_terms[:, 0] + core_other(doc_terms[:, 1])
    doc_grad = lax.psum_scatter(doc_terms, "dp", scatter_dimension=0)
    doc_back, doc_proj = embed_back(*doc, doc_grad)
    query_back, query_proj = embed_back(*query, query_grad)
    proj_grad = doc_proj + query_proj
    own = (query_back, doc_back, jnp.zeros_like(doc_back))
    received = jnp.zeros((half, model), bf16)
    totals, biases, small = None, None, None
    input_grads = [None, None]
    for step in range(3):
        dy = jnp.where(first, received.astype(f32), own[step])
        dh, weights, bias, vectors = backward(dy, w, contexts[2 - step][1], records[2 - step])
        totals = weights if totals is None else [p + q for p, q in zip(totals, weights)]
        biases = bias if biases is None else [p + q for p, q in zip(biases, bias)]
        small = vectors if small is None else small + vectors
        if step < 2:
            received = to_section(dh.astype(bf16), [(1, 0)])
        if step >= 1:
            input_grads[2 - step] = lax.dynamic_slice_in_dim(dh, chip * share, share, 0)
    totals = [lax.psum(part.astype(bf16), "dp").astype(f32) for part in totals]
    small = small + core_other(small)
    proj_grad = proj_grad + core_other(proj_grad)
    board = board + core_other(board)
    d_up_b, d_qkv_b, small, proj_grad = lax.psum((biases[0], biases[1], small, proj_grad), "dp")
    stack = jnp.stack(input_grads)
    swap = [(0, 1), (1, 0)]
    mid, docs = model // 2, groups // 2
    sent_input = to_section(stack[:, :, mid:], swap)
    sent_board, sent_proj = to_section((board[:, :docs], proj_grad[:mid]), swap)
    d_down, d_up, d_out, d_qkv = totals
    width = qkv_weight.shape[-1]
    return (
        jnp.where(first, sent_board, board[:, docs:]),
        jnp.where(first, stack[:, :, :mid], sent_input),
        d_qkv.reshape(1, model, 3, width),
        d_qkv_b.reshape(1, 3, width),
        d_out[None],
        d_up[None],
        d_up_b[None],
        d_down[None],
        small[0:2][None],
        small[2:4][None],
        small[4:6][None],
        jnp.where(first, sent_proj, proj_grad[mid:]),
    )


def solution(mesh):
    return jax.shard_map(
        on_device,
        mesh=mesh,
        in_specs=(
            P("dp", "tensor", None),
            P("dp", None),
            P("dp", None),
            P("section", None, None, "tensor"),
            P("section", None, "tensor"),
            P("section", "tensor", None),
            P("section", None, "tensor"),
            P("section", "tensor"),
            P("section", "tensor", None),
            P("section", None, None),
            P("section", None, None),
            P("section", None, None),
            P(),
        ),
        out_specs=(
            P("dp", "section"),
            P("dp", "tensor", "section"),
            P("section", None, None, "tensor"),
            P("section", None, "tensor"),
            P("section", "tensor", None),
            P("section", None, "tensor"),
            P("section", "tensor"),
            P("section", "tensor", None),
            P("section", None, None),
            P("section", None, None),
            P("section", None, None),
            P("section", None),
        ),
        check_vma=False,
    )
```

```python
import functools

import jax
import jax.numpy as jnp
import numpy as np
from jax import lax
from jax.experimental import pallas as pl
from jax.experimental.pallas import tpu as pltpu
from jax.sharding import PartitionSpec as P

HD = 64
QLEN = 32
LANES = 128

norm_eps = 1e-05
unit_eps = 1e-06
softness_factor = 0.0625
rope_base = 10000.0
hidden_score = -1000000000.0
contract_rows = (((0,), (0,)), ((), ()))
contract_cols = (((1,), (1,)), ((), ()))
contract_inner = (((1,), (0,)), ((), ()))
bf16 = jnp.bfloat16
f32 = jnp.float32


def dot(left, right, contraction=contract_inner):
    return lax.dot_general(left, right, contraction, preferred_element_type=f32)


def flip(value, bit):
    count = lax.axis_size("tensor")
    return lax.ppermute(value, "tensor", [(i, i ^ (1 << bit)) for i in range(count)])


def chip_bits():
    return range(1, lax.axis_size("tensor").bit_length() - 1)


def core_other(value):
    return flip(value, 0)


def chips_gather(value, chip):
    for bit in chip_bits():
        other = flip(value, bit)
        upper = (chip >> (bit - 1)) % 2 == 1
        value = jnp.concatenate([jnp.where(upper, other, value), jnp.where(upper, value, other)], axis=0)
    return value


def chips_other(low):
    bits = list(chip_bits())
    if not bits:
        return low, jnp.zeros_like(low)
    for bit in bits[:-1]:
        low = (low.astype(f32) + flip(low, bit).astype(f32)).astype(bf16)
    return low, flip(low, bits[-1])


def to_section(value, pairs):
    return lax.ppermute(value, "section", pairs)


def dp_gather(value):
    count = lax.axis_size("dp")
    me = lax.axis_index("dp")
    value = value[None]
    step = 1
    while step < count:
        other = lax.ppermute(value, "dp", [(i, i ^ step) for i in range(count)])
        upper = (me // step) % 2 == 1
        value = jnp.concatenate([jnp.where(upper, other, value), jnp.where(upper, value, other)], axis=0)
        step *= 2
    return value


def dp_sum(value):
    count = lax.axis_size("dp")
    step = 1
    while step < count:
        value = value + lax.ppermute(value, "dp", [(i, i ^ step) for i in range(count)])
        step *= 2
    return value


def add_kernel(x, y, *refs):
    refs[-1][...] = (x[...].astype(f32) + y[...].astype(f32)).astype(bf16)


def add_step(x, y, following=None, after=()):
    extra = ([following] if following is not None else []) + list(after)

    def body(x_ref, y_ref, *refs):
        add_kernel(x_ref, y_ref, refs[-1])

    handed = [jax.ShapeDtypeStruct(following.shape, following.dtype)] if following is not None else []
    out = pl.pallas_call(
        body,
        in_specs=[VMEM, VMEM] + [ANY] * len(extra),
        out_specs=[ANY] * len(handed) + [VMEM],
        out_shape=handed + [jax.ShapeDtypeStruct(x.shape, bf16)],
        input_output_aliases={2: 0} if handed else {},
        compiler_params=pltpu.CompilerParams(vmem_limit_bytes=16 * 1024 * 1024),
    )(x, y, *extra)
    return out[-1], (out[0] if handed else None)


class LineSum:

    def __init__(self):
        self.waiting, self.flying, self.side, self.results, self.last = [], [], None, [], ()

    def put(self, chunks):
        self.waiting += chunks
        while len(self.flying) < 2 and self.waiting:
            self.launch(self.waiting.pop(0))

    def launch(self, chunk):
        self.flying.append((chunk, lax.ppermute(chunk, "dp", [(0, 1), (3, 2)])))

    def step(self, after=()):
        before = self.side
        after = tuple(after) + tuple(back for _, back in self.results[-2:-1])
        if self.flying:
            chunk, arrived = self.flying.pop(0)
            following = self.waiting.pop(0) if self.waiting else None
            side, following = add_step(chunk, arrived, following, tuple(after) + self.last)
            self.last = (side,)
            if following is not None:
                self.launch(following)
            self.side = (side, lax.ppermute(side, "dp", [(1, 2), (2, 1)]))
        else:
            self.side = None
        if before is not None:
            total, _ = add_step(*before, None, self.last)
            self.last = (total,)
            self.results.append((total, lax.ppermute(total, "dp", [(1, 0), (2, 3)])))
        return self.last

    def busy(self):
        return bool(self.flying or self.side is not None)


def gathered_line(results):
    me = lax.axis_index("dp")
    totals = jnp.concatenate([t for t, _ in results], axis=0)
    backs = jnp.concatenate([r for _, r in results], axis=0)
    return jnp.where((me == 0) | (me == 3), backs, totals).astype(f32)


def rope_tables(positions):
    half = HD // 2
    frequency = np.power(np.float32(rope_base), (-2.0 * np.arange(half) / HD).astype(np.float32)).astype(np.float32)
    angles = (positions.astype(np.float32)[:, None] * frequency[None, :]).astype(np.float32)
    cosine, sine = np.cos(angles), np.sin(angles)
    head = (np.concatenate([cosine, cosine], 1), np.concatenate([-sine, sine], 1))
    return tuple(np.tile(part, (1, LANES // HD)).astype(np.float32) for part in head)


VMEM = pl.BlockSpec(memory_space=pltpu.VMEM)
ANY = pl.BlockSpec(memory_space=pl.ANY)
SMEM = pl.BlockSpec(memory_space=pltpu.SMEM)


def held(x):
    return pltpu.with_memory_space_constraint(x, pltpu.HBM)


def call(kernel, ins, outs, scratch=(), after=(), smem=(), keep=(), limit=16):
    n = len(ins)

    def body(*refs):
        kernel(*refs[:n], *refs[n + len(after) :])

    return pl.pallas_call(
        body,
        in_specs=[SMEM if i in smem else VMEM for i in range(n)] + [ANY] * len(after),
        out_specs=[VMEM] * len(outs),
        out_shape=[pltpu.HBM(*out) if i in keep else jax.ShapeDtypeStruct(*out) for i, out in enumerate(outs)],
        scratch_shapes=list(scratch),
        compiler_params=pltpu.CompilerParams(vmem_limit_bytes=limit * 1024 * 1024),
    )(*ins, *after)


def load_kernel(own, oth, out, sem, axis):
    size = own.shape[axis]
    places = [out.at[:, :size], out.at[:, size:]] if axis else [out.at[:size], out.at[size:]]
    copies = [pltpu.make_async_copy(x, place, sem.at[i]) for i, (x, place) in enumerate(zip((own, oth), places))]
    for copy in copies:
        copy.start()
    for copy in copies:
        copy.wait()


def chip_weight(own, axis):
    other = core_other(own)
    shape = tuple(2 * n if i == axis else n for i, n in enumerate(own.shape))
    return pl.pallas_call(
        functools.partial(load_kernel, axis=axis),
        in_specs=[ANY, ANY],
        out_specs=VMEM,
        out_shape=pltpu.VMEM(shape, own.dtype),
        scratch_shapes=[pltpu.SemaphoreType.DMA((2,))],
        compiler_params=pltpu.CompilerParams(vmem_limit_bytes=16 * 1024 * 1024),
    )(own, other)


def half_rows(ref, c):
    size = ref.shape[0] // 2
    return ref[c * size : (c + 1) * size, :]


def half_lanes(ref, c):
    size = ref.shape[1] // 2
    return ref[:, c * size : (c + 1) * size]


def merge(out, before, value):
    size = value.shape[0]
    out[:size, :] = before[...]
    out[size:, :] = value


def swap_halves(tile):
    lane = lax.broadcasted_iota(jnp.int32, tile.shape, 1)
    return jnp.where(lane % HD < HD // 2, pltpu.roll(tile, LANES - HD // 2, 1), pltpu.roll(tile, HD // 2, 1))


def qkv_kernel(flag, entering, received_a, received_b, w, b, cos, sin, h_ref, q_ref, kv_ref):
    received = jnp.concatenate([received_a[...], received_b[...]], axis=0)
    h = jnp.where(flag[0, 0] == 1, entering[...], received)
    h_ref[...] = h
    width = w.shape[1] // 6
    c, s = cos[...], sin[...]
    for place in range(2):
        at = slice(place * 3 * width, (place + 1) * 3 * width)
        p = dot(h, w[:, at]) + b[:, at]
        for t in range(0, width, LANES):
            at = slice(place * width + t, place * width + t + LANES)
            tile = p[:, t : t + LANES]
            q_ref[:, at] = (tile * c + swap_halves(tile) * s).astype(bf16)
            tile = p[:, width + t : width + t + LANES]
            kv_ref[:, at] = (tile * c + swap_halves(tile) * s).astype(bf16)
        kv_ref[:, 2 * width + place * width : 2 * width + (place + 1) * width] = p[:, 2 * width :].astype(bf16)


def qkv_step(flag, entering, received, w, tables, after=()):
    rows, model = entering.shape
    features = w["qkv"].shape[1] // 3
    return call(
        qkv_kernel,
        [flag, entering, *received, w["qkv"], w["qkv_b"], *tables],
        [((rows, model), bf16), ((rows, features), bf16), ((rows, 2 * features), bf16)],
        after=after,
        smem=(0,),
        keep=(0, 1, 2),
    )


def head_rows(tile, place):
    row = lax.broadcasted_iota(jnp.int32, tile.shape, 0)
    return jnp.where(row // HD == place, tile, 0.0).astype(bf16)


def head_lanes(tile, place):
    lane = lax.broadcasted_iota(jnp.int32, tile.shape, 1)
    return jnp.where(lane // HD == place, tile, 0.0).astype(bf16)


def tile_at(j, features, base=0):
    return slice(base + j * LANES, base + (j + 1) * LANES)


def partner_tile(j, features):
    tiles = features // LANES
    return (j + tiles // 2) % tiles


def partner_base(j, features, base=0):
    return tile_at(partner_tile(j, features), features, base)


def attend_kernel(*refs, c):
    q_ref, kv_own, kv_oth, bias_ref, w = refs[:5]
    if c:
        o_before, v_t, refs = refs[5], refs[6], refs[7:]
        o_own, o_oth, lse_ref, low_ref, o_t, s_all = refs
    else:
        o_first, k_t, v_t, lse_ref, low_ref, o_t, s_all = refs[5:]
    features = q_ref.shape[1]
    rows = kv_own.shape[0]
    some = rows // 2
    q_half = half_rows(q_ref, c)
    for j in range(features // LANES):
        at = tile_at(j, features)
        q_t = q_half[:, at].astype(f32).T * HD ** (-0.5)
        k_here, k_there = kv_own[:, at], kv_oth[:, partner_base(j, features)]
        for place in range(2):
            q_one = head_rows(q_t, place)
            s_all[2 * j + place, :rows, :] = dot(k_here, q_one)
            s_all[2 * j + place, rows:, :] = dot(k_there, q_one)
        if not c:
            v_here, v_there = kv_own[:, tile_at(j, features, features)], kv_oth[:, partner_base(j, features, features)]
            v_t[at, :rows] = v_here.astype(f32).T.astype(bf16)
            v_t[at, rows:] = v_there.astype(f32).T.astype(bf16)
            k_t[at, :rows] = k_here.astype(f32).T.astype(bf16)
            k_t[at, rows:] = k_there.astype(f32).T.astype(bf16)
    bias = bias_ref[:, c * some : (c + 1) * some]
    for h in range(features // HD):
        s = s_all[h] + bias
        peak = jnp.max(s, axis=0, keepdims=True)
        e = jnp.exp(s - peak)
        total = jnp.sum(e, axis=0, keepdims=True)
        s_all[h] = e * (1.0 / total)
        lse_ref[h : h + 1, :] = peak + jnp.log(total)
    for h in range(features // HD):
        o_t[h * HD : (h + 1) * HD, :] = dot(v_t[h * HD : (h + 1) * HD, :], s_all[h].astype(bf16))
    o = o_t[...].T.astype(bf16)
    half = features // 2
    if c:
        merge(o_own, o_before[:, :half], o[:, :half])
        merge(o_oth, o_before[:, half:], o[:, half:])
    else:
        o_first[...] = o
    low_ref[...] = dot(o, w[...]).astype(bf16)


def attend_step(c, q, kv, kv_other, bias, w, before=(), after=()):
    rows, features = q.shape
    model = w["out"].shape[1]
    some = rows // 2
    heads = features // HD
    if c:
        kept = [((rows, features // 2), bf16)] * 2
    else:
        kept = [((some, features), bf16), ((features, 2 * rows), bf16), ((features, 2 * rows), bf16)]
    return call(
        functools.partial(attend_kernel, c=c),
        [q, kv, kv_other, bias, w["out"], *before],
        kept + [((heads, some), f32), ((some, model), bf16)],
        scratch=[pltpu.VMEM((features, some), f32), pltpu.VMEM((heads, 2 * rows, some), f32)],
        after=after,
        keep=(0, 1, 2) if c else (0, 1, 2, 3),
    )


def normed(values):
    centred = values - jnp.mean(values, axis=-1, keepdims=True)
    inverse = lax.rsqrt(jnp.mean(centred * centred, axis=-1, keepdims=True) + norm_eps)
    return centred * inverse, inverse


def norm_back(gradient, n, inverse):
    return inverse * (gradient - jnp.mean(gradient, axis=-1, keepdims=True) - n * jnp.mean(gradient * n, axis=-1, keepdims=True))


def feed_kernel(*refs, c):
    h, low, recv, vec, up, b, down = refs[:7]
    before, refs = (refs[7:10], refs[10:]) if c else (None, refs[7:])
    n_ref, r_ref, sl_ref, low_ref, h1_ref, g_own, g_oth = refs
    s1 = half_rows(h, c).astype(f32) + (low[...].astype(f32) + recv[...].astype(f32)) + vec[0:1, :]
    n, r = normed(s1)
    n_ref[...] = n
    r_ref[...] = r
    h1 = (n * vec[1:2, :] + vec[2:3, :]).astype(bf16)
    u = dot(h1, up[...]) + b[...]
    phi = 0.5 * (1.0 + lax.erf(u * 0.7071067811865476))
    g = (u * phi).astype(bf16)
    sl_ref[...] = (phi + u * jnp.exp(-0.5 * u * u) * 0.3989422804014327).astype(bf16)
    low_ref[...] = dot(g, down[...]).astype(bf16)
    units = up.shape[1] // 2
    for place, value in enumerate((h1, g[:, :units], g[:, units:])):
        out = (h1_ref, g_own, g_oth)[place]
        if c:
            merge(out, before[place], value)
        else:
            out[...] = value


def feed_step(c, h, low, recv, vec, w, before=(), after=()):
    rows, model = h.shape
    units = w["up"].shape[1]
    some = rows // 2
    kept = rows if c else some
    return call(
        functools.partial(feed_kernel, c=c),
        [h, low, recv, vec, w["up"], w["up_b"], w["down"], *before],
        [
            ((some, model), f32), ((some, 1), f32), ((some, units), bf16), ((some, model), bf16),
            ((kept, model), bf16), ((kept, units // 2), bf16), ((kept, units // 2), bf16),
        ],
        after=after,
        keep=(0, 1, 2, 4, 5, 6),
    )


def output_kernel(n1, low, recv, vec, n_ref, r_ref, y_ref):
    s2 = n1[...] * vec[0:1, :] + vec[1:2, :] + (low[...].astype(f32) + recv[...].astype(f32)) + vec[2:3, :]
    n, r = normed(s2)
    n_ref[...] = n
    r_ref[...] = r
    y_ref[...] = (n * vec[3:4, :] + vec[4:5, :]).astype(bf16)


def output_step(n1, low, recv, vec, after=()):
    return call(output_kernel, [n1, low, recv, vec], [(n1.shape, f32), ((n1.shape[0], 1), f32), (n1.shape, bf16)], after=after, keep=(0, 1))


def feed_back_kernel(*refs, c):
    flag, received, own, n2, r2, gain, up, down, sl = refs[:9]
    before, refs = (refs[9:12], refs[12:]) if c else (None, refs[9:])
    ds_ref, low_ref, vec_ref, ub_ref, f_ref, u_own, u_oth = refs
    dy = jnp.where(flag[0, 0] == 1, received[...].astype(f32), half_rows(own, c))
    n = n2[...]
    ds = norm_back(dy * gain[...], n, r2[...])
    ds_ref[...] = ds
    vec_ref[0:1, :] = jnp.sum(ds, axis=0, keepdims=True)
    vec_ref[1:2, :] = jnp.sum(dy * n, axis=0, keepdims=True)
    vec_ref[2:3, :] = jnp.sum(dy, axis=0, keepdims=True)
    f = ds.astype(bf16)
    du = dot(f, down[...], contract_cols) * sl[...].astype(f32)
    ub_ref[...] = jnp.sum(du, axis=0, keepdims=True)
    u = du.astype(bf16)
    low_ref[...] = dot(u, up[...], contract_cols).astype(bf16)
    units = up.shape[1] // 2
    for place, value in enumerate((f, u[:, :units], u[:, units:])):
        out = (f_ref, u_own, u_oth)[place]
        if c:
            merge(out, before[place], value)
        else:
            out[...] = value


def feed_back_step(c, flag, received, own, n2, r2, gain, w, sl, before=(), after=()):
    some, model = n2.shape
    units = w["up"].shape[1]
    kept = 2 * some if c else some
    return call(
        functools.partial(feed_back_kernel, c=c),
        [flag, received, own, n2, r2, gain, w["up"], w["down"], sl, *before],
        [
            ((some, model), f32), ((some, model), bf16), ((3, model), f32), ((1, units), f32),
            ((kept, model), bf16), ((kept, units // 2), bf16), ((kept, units // 2), bf16),
        ],
        after=after,
        smem=(0,),
        keep=(0, 2, 3, 4, 5, 6),
    )


def attend_back_kernel(*refs, c):
    (ds2, low, recv, n1, r1, gain, w, q_ref, kv_own, kv_oth, k_t, bias_ref, lse_ref), refs = refs[:13], refs[13:]
    if c:
        (own_before, oth_before, out_before), refs = refs[:3], refs[3:]
    ds_ref, dq_ref, vec_ref, dkv_ref, dkv_send, out_ref, dq_t, s_all, d_all, a_all, slopes = refs
    features = q_ref.shape[1]
    rows = kv_own.shape[0]
    some = rows // 2
    dh1 = ds2[...] + (low[...].astype(f32) + recv[...].astype(f32))
    n = n1[...]
    ds1 = norm_back(dh1 * gain[...], n, r1[...])
    ds_ref[...] = ds1
    vec_ref[0:1, :] = jnp.sum(ds1, axis=0, keepdims=True)
    vec_ref[1:2, :] = jnp.sum(dh1 * n, axis=0, keepdims=True)
    vec_ref[2:3, :] = jnp.sum(dh1, axis=0, keepdims=True)
    spread = ds1.astype(bf16)
    if c:
        merge(out_ref, out_before, spread)
    else:
        out_ref[...] = spread
    q_half = half_rows(q_ref, c)
    for j in range(features // LANES):
        at = tile_at(j, features)
        q_t = q_half[:, at].astype(f32).T * HD ** (-0.5)
        k_here, k_there = kv_own[:, at], kv_oth[:, partner_base(j, features)]
        for place in range(2):
            q_one = head_rows(q_t, place)
            s_all[2 * j + place, :rows, :] = dot(k_here, q_one)
            s_all[2 * j + place, rows:, :] = dot(k_there, q_one)
    mixed = dot(spread, w[...], contract_cols).astype(bf16).astype(f32)
    for j in range(features // LANES):
        do_t = mixed[:, tile_at(j, features)].T
        v_here, v_there = kv_own[:, tile_at(j, features, features)], kv_oth[:, partner_base(j, features, features)]
        for place in range(2):
            do_one = head_rows(do_t, place)
            d_all[2 * j + place, :rows, :] = dot(v_here, do_one)
            d_all[2 * j + place, rows:, :] = dot(v_there, do_one)
    bias = bias_ref[:, c * some : (c + 1) * some]
    for h in range(features // HD):
        a = jnp.exp(s_all[h] + bias - lse_ref[h : h + 1, :])
        da = d_all[h]
        slope = a * (da - jnp.sum(da * a, axis=0, keepdims=True))
        slopes[h] = slope.astype(bf16) * jnp.asarray(HD ** (-0.5), bf16)
        a_all[h] = a.astype(bf16)
    for h in range(features // HD):
        dq_t[h * HD : (h + 1) * HD, :] = dot(k_t[h * HD : (h + 1) * HD, :], slopes[h])
    for j in range(features // LANES):
        at, v_at = tile_at(j, features), tile_at(j, features, features)
        theirs, v_theirs = partner_base(j, features), partner_base(j, features, features)
        q, do = q_half[:, at].astype(f32), mixed[:, at]
        dk = dot(slopes[2 * j], head_lanes(q, 0)) + dot(slopes[2 * j + 1], head_lanes(q, 1))
        dv = dot(a_all[2 * j], head_lanes(do, 0)) + dot(a_all[2 * j + 1], head_lanes(do, 1))
        if c:
            dkv_ref[:, at] = dk[:rows] + own_before[:, at]
            dkv_ref[:, v_at] = dv[:rows] + own_before[:, v_at]
            dkv_send[:, theirs] = (dk[rows:] + oth_before[:, theirs]).astype(bf16)
            dkv_send[:, v_theirs] = (dv[rows:] + oth_before[:, v_theirs]).astype(bf16)
        else:
            dkv_ref[:, at] = dk[:rows]
            dkv_ref[:, v_at] = dv[:rows]
            dkv_send[:, theirs] = dk[rows:]
            dkv_send[:, v_theirs] = dv[rows:]
    dq_ref[...] = dq_t[...].T


def attend_back_step(c, ds2, low, recv, n1, r1, gain, w, q, kv, kv_other, k_t, bias, lse, before=(), after=()):
    some, model = ds2.shape
    features = q.shape[1]
    rows = 2 * some
    heads = features // HD
    all_heads = (heads, 2 * rows, some)
    return call(
        functools.partial(attend_back_kernel, c=c),
        [ds2, low, recv, n1, r1, gain, w["out"], q, kv, kv_other, k_t, bias, lse, *before],
        [
            ((some, model), f32), ((some, features), f32), ((3, model), f32),
            ((rows, 2 * features), f32), ((rows, 2 * features), bf16 if c else f32), ((rows if c else some, model), bf16),
        ],
        scratch=[
            pltpu.VMEM((features, some), f32), pltpu.VMEM(all_heads, f32), pltpu.VMEM(all_heads, f32), pltpu.VMEM(all_heads, bf16),
            pltpu.VMEM(all_heads, bf16),
        ],
        after=after,
        keep=(0, 1, 2, 3, 5) if c else (0, 1, 2, 3, 4, 5),
        limit=24,
    )


def qkv_back_kernel(*refs, c):
    dq, dkv_ref, arrived_ref, cos, sin, w = refs[:6]
    before, refs = (refs[6:8], refs[8:]) if c else (None, refs[6:])
    low_ref, b_ref, p_own, p_oth = refs
    some, features = dq.shape
    width = features // 2
    cosine, sine = half_rows(cos, c), half_rows(sin, c)
    dkv = half_rows(dkv_ref, c) + half_rows(arrived_ref, c).astype(f32)
    total = None
    for place, p_ref in enumerate((p_own, p_oth)):
        base = place * 3 * width
        rows_at = slice(some, 2 * some) if c else slice(0, some)
        for t in range(0, width, LANES):
            at = slice(place * width + t, place * width + t + LANES)
            v_at = slice(features + place * width + t, features + place * width + t + LANES)
            gq, gk, gv = dq[:, at], dkv[:, at], dkv[:, v_at]
            gq = gq * cosine - swap_halves(gq) * sine
            gk = gk * cosine - swap_halves(gk) * sine
            for part, g in enumerate((gq, gk, gv)):
                to = part * width + t
                p_ref[rows_at, to : to + LANES] = g.astype(bf16)
                b_ref[0:1, base + to : base + to + LANES] = jnp.sum(g, axis=0, keepdims=True)
        if c:
            p_ref[:some, :] = before[place][...]
        part = dot(p_ref[rows_at, :], w[:, base : base + 3 * width], contract_cols)
        total = part if total is None else total + part
    low_ref[...] = total.astype(bf16)


def qkv_back_step(c, dq, dkv, arrived, tables, w, before=(), after=()):
    some, features = dq.shape
    model, wide = w["qkv"].shape
    kept = 2 * some if c else some
    return call(
        functools.partial(qkv_back_kernel, c=c),
        [dq, dkv, arrived, *tables, w["qkv"], *before],
        [((some, model), bf16), ((1, wide), f32), ((kept, wide // 2), bf16), ((kept, wide // 2), bf16)],
        after=after,
        keep=(1, 2, 3),
    )


def whole(x):
    return x, pl.BlockSpec(x.shape, lambda *i: (0,) * len(x.shape))


def steps_of_rows(x, steps):
    return x, pl.BlockSpec((x.shape[0] // steps, x.shape[1]), lambda i: (i, 0))


def steps_of_lanes(x, steps):
    return x, pl.BlockSpec((x.shape[0], x.shape[1] // steps), lambda i: (0, i))


def weight_kernel(*refs, pieces, before, chunks):
    lefts, rights, refs = refs[:pieces], refs[pieces : 2 * pieces], refs[2 * pieces :]
    left = jnp.concatenate([x[...] for x in lefts], axis=0)
    right = jnp.concatenate([x[...] for x in rights], axis=0)
    total = dot(left, right, contract_rows)
    if before:
        total = total + refs[0][...]
    outs = refs[before:]
    if not chunks:
        outs[0][...] = total.astype(outs[0].dtype)
        return
    for i, out in enumerate(outs):

        @pl.when(pl.program_id(0) == i)
        def _(out=out):
            out[...] = total.astype(out.dtype)


def weight_step(lefts, rights, before=None, chunks=False, steps=2, after=()):
    shape = (lefts[0].shape[1], rights[0].shape[1])
    steps = min(steps, shape[0] // LANES)
    ins = [steps_of_lanes(held(x), steps) for x in lefts] + [whole(held(x)) for x in rights]
    if before is not None:
        ins.append(steps_of_rows(held(before), steps))
    n = len(ins)
    some = (shape[0] // steps, shape[1])
    kernel = functools.partial(weight_kernel, pieces=len(lefts), before=int(before is not None), chunks=chunks)

    def body(*refs):
        kernel(*refs[:n], *refs[n + len(after) :])

    return pl.pallas_call(
        body,
        grid=(steps,),
        in_specs=[spec for _, spec in ins] + [ANY] * len(after),
        out_specs=[pl.BlockSpec(some, lambda i: (0, 0))] * steps if chunks else pl.BlockSpec(some, lambda i: (i, 0)),
        out_shape=[jax.ShapeDtypeStruct(some, bf16)] * steps if chunks else pltpu.HBM(shape, f32),
        compiler_params=pltpu.CompilerParams(vmem_limit_bytes=24 * 1024 * 1024),
    )(*[x for x, _ in ins], *after)


def scores_kernel(y_a, y_b, proj, units, alive, grad_t, z_ref, m_ref, dy_ref, terms_ref, groups):
    low = jnp.concatenate([y_a[...], y_b[...]], axis=0)
    z = dot(low, proj[...])
    inverse = lax.rsqrt(jnp.sum(z * z, axis=-1, keepdims=True) + unit_eps)
    e = z * inverse
    e_low = e.astype(bf16)
    e_t = e_low.astype(f32).T.astype(bf16)
    block = units.shape[0] // groups
    back = None
    for d in range(groups):
        at = slice(d * block, (d + 1) * block)
        docs = units[at, :]
        logits = jnp.where(alive[at, :] > 0, dot(docs, e_t) / softness_factor, hidden_score)
        peak = jnp.max(logits, axis=0, keepdims=True)
        x = jnp.exp(logits - peak)
        total = jnp.sum(x, axis=0, keepdims=True)
        m_ref[d : d + 1, :] = softness_factor * (peak + jnp.log(total))
        pull = (x * (grad_t[d : d + 1, :] / total)).astype(bf16)
        terms_ref[at, :] = dot(pull, e_low)
        part = dot(docs.astype(f32).T.astype(bf16), pull)
        back = part if back is None else back + part
    de = back.T
    dz = (inverse * (de - e * jnp.sum(de * e, axis=-1, keepdims=True))).astype(bf16)
    z_ref[...] = dz
    dy_ref[...] = dot(dz, proj[...], contract_cols)


def scores_step(y, proj, units, alive, grad_t):
    rows, model = 2 * y[0].shape[0], y[0].shape[1]
    groups, width = grad_t.shape[0], proj.shape[1]
    return call(
        functools.partial(scores_kernel, groups=groups),
        [*y, proj, units, alive, grad_t],
        [((rows, width), bf16), ((groups, rows), f32), ((rows, model), f32), ((units.shape[0], width), f32)],
        limit=32,
    )


def forward(flag, entering, received, w, bias, tables, after=()):
    h, q, kv = qkv_step(flag, entering, received, w, tables, after)
    kv_other = held(core_other(kv))
    h_here, q, kv = held(h), held(q), held(kv)
    o_a, k_t, v_t, lse_a, low_a = attend_step(0, q, kv, kv_other, bias, w)
    sum_a = chips_other(low_a)
    o, o_o, lse_b, low_b = attend_step(1, q, kv, kv_other, bias, w, (held(o_a), held(v_t)))
    sum_b = chips_other(low_b)
    n1_a, r1_a, sl_a, low_a, *before = feed_step(0, h_here, *sum_a, w["vec_feed"], w)
    sum_a = chips_other(low_a)
    n1_b, r1_b, sl_b, low_b, h1, g, g_o = feed_step(1, h_here, *sum_b, w["vec_feed"], w, [held(x) for x in before])
    sum_b = chips_other(low_b)
    n1_a, n1_b = held(n1_a), held(n1_b)
    n2_a, r2_a, y_a = output_step(n1_a, *sum_a, w["vec_out"])
    n2_b, r2_b, y_b = output_step(n1_b, *sum_b, w["vec_out"])
    kept = ((g, core_other(g_o)), (h1, core_other(h1)), (o, core_other(o_o)), (h, core_other(h)))
    a = (held(lse_a), n1_a, held(r1_a), held(sl_a), held(n2_a), held(r2_a))
    b = (held(lse_b), n1_b, held(r1_b), held(sl_b), held(n2_b), held(r2_b))
    return (y_a, y_b), ((q, kv, kv_other, held(k_t)), (a, b)), kept


def backward(flag, received, own, w, bias, tables, record, hook, after):
    (q, kv, kv_other, k_t), halves = record
    parts, vectors, ubs, before, ds2s = [], [], [], (), []
    for c in range(2):
        lse, n1, r1, sl, n2, r2 = halves[c]
        ds2, low, vec, ub, *before = feed_back_step(
            c, flag, received[c], own, n2, r2, w["gain"][1:2], w, sl, [held(x) for x in before], after if c == 0 else ()
        )
        ds2s.append(held(ds2))
        parts.append(chips_other(low))
        vectors.append(vec)
        ubs.append(ub)
    f, u, u_o = before
    after = hook("feed", (f, core_other(f)), (u, core_other(u_o)))
    before, vectors_1, ds1s, dqs = (), [], [], []
    for c in range(2):
        lse, n1, r1, sl, n2, r2 = halves[c]
        ds1, dq, vec, dkv, send, out = attend_back_step(
            c, ds2s[c], *parts[c], n1, r1, w["gain"][0:1], w, q, kv, kv_other, k_t, bias, lse, before, after
        )
        before = (held(dkv), held(send), held(out)) if c == 0 else ()
        ds1s.append(ds1)
        dqs.append(held(dq))
        vectors_1.append(vec)
        if c == 0:
            after = hook("between", dq, None)
    arrived, dkv = held(core_other(send)), held(dkv)
    after = hook("between", send, None)
    nexts, pbs, before = [], [], ()
    for c in range(2):
        low, pb, *before = qkv_back_step(c, dqs[c], dkv, arrived, tables, w, [held(x) for x in before], after if c == 0 else ())
        nexts.append(chips_other(low))
        pbs.append(pb)
    p, p_o = before
    after = hook("attend", (out, core_other(out)), (p, core_other(p_o)))
    dh = [ds1s[c] + (nexts[c][0].astype(f32) + nexts[c][1].astype(f32)) for c in range(2)]
    vectors = jnp.stack([vectors_1[0] + vectors_1[1], vectors[0] + vectors[1]], axis=1)
    return dh, vectors, ubs[0] + ubs[1], pbs[0] + pbs[1], after


def on_device(tokens, segment, score_grad, qkv_weight, qkv_bias, out_weight, up_weight, up_bias, down_weight, out_bias, norm_gain, norm_shift, proj_weight):
    blocks, share, model = tokens.shape
    wide = 3 * qkv_weight.shape[-1]
    width = wide // 3
    gain, shift, bias = norm_gain[0].astype(f32), norm_shift[0].astype(f32), out_bias[0].astype(f32)
    first = lax.axis_index("section") == 0
    flag = first.astype(jnp.int32).reshape(1, 1)
    device = lax.axis_index("tensor")
    core, chip = device % 2, device // 2
    chips = lax.axis_size("tensor") // 2
    groups = lax.axis_size("dp")
    half = share * chips
    rows = 2 * half
    proj = proj_weight.shape[1]
    entering = [chips_gather(tokens[b], chip) for b in range(2)]

    def both(own):
        return jnp.concatenate([own, core_other(own)], axis=1)

    w = dict(
        qkv=chip_weight(qkv_weight[0].reshape(model, wide), 1), qkv_b=both(qkv_bias[0].reshape(1, wide).astype(f32)),
        out=chip_weight(out_weight[0], 0), up=chip_weight(up_weight[0], 1), up_b=both(up_bias.astype(f32)),
        down=chip_weight(down_weight[0], 0), gain=gain,
        vec_feed=jnp.stack([bias[0], gain[0], shift[0]]),
        vec_out=jnp.stack([gain[0], shift[0], bias[1], gain[1], shift[1]]),
    )

    def own_first(by_token):
        parts = by_token.reshape((chips, 2, share) + by_token.shape[1:])
        even = parts[:, 0].reshape((half,) + by_token.shape[1:])
        odd = parts[:, 1].reshape((half,) + by_token.shape[1:])
        return jnp.concatenate([jnp.where(core == 0, even, odd), jnp.where(core == 0, odd, even)], axis=0)

    index = np.arange(rows)
    tables = [tuple(own_first(jnp.asarray(part))[:half] for part in rope_tables(p)) for p in (index, index % QLEN)]
    segments = [own_first(segment[b]) for b in range(2)]

    def pick(zero, one):
        ids = jnp.where(first, segments[zero], segments[one])
        bias = jnp.where(ids[:, None] == ids[None, :half], 0.0, hidden_score).astype(f32)
        return bias, tuple(jnp.where(first, x, y) for x, y in zip(tables[zero], tables[one]))

    contexts = [pick(0, 0), pick(1, 0), pick(1, 1)]
    received = [jnp.zeros((half // 2, model), bf16)] * 2
    records, kept, outputs = [], [], []
    prelude = [w["vec_feed"], w["vec_out"], w["up_b"]] + [x for bias_of, tables_of in contexts for x in (bias_of, *tables_of)]
    for tick in range(3):
        y, record, keep = forward(flag, entering[min(tick, 1)], received, w, *contexts[tick], prelude if tick == 0 else ())
        records.append(record)
        kept.append(keep)
        outputs.append(y)
        if tick < 2:
            received = [to_section(part, [(0, 1)]) for part in y]

    doc_y, query_y = jnp.concatenate(outputs[1]), jnp.concatenate(outputs[2])
    z = dot(doc_y, proj_weight)
    inverse = lax.rsqrt(jnp.sum(z * z, axis=-1, keepdims=True) + unit_eps)
    doc_units = z * inverse
    units_own = dp_gather(doc_units.astype(bf16))
    units = jnp.stack([units_own, core_other(units_own)], axis=1).reshape(groups * rows, proj)
    alive = dp_gather((segments[0] == 0).astype(f32).reshape(rows // LANES, LANES)).reshape(groups * rows, 1)
    slots = score_grad.shape[0]
    member = (segments[1][:half, None] == jnp.arange(slots)[None, :]).astype(f32)
    grad_t = lax.dot_general(score_grad, member, (((0,), (1,)), ((), ())), precision=lax.Precision.HIGHEST, preferred_element_type=f32)
    query_dz, smooth, query_dy, terms = scores_step(outputs[2], proj_weight, units, alive, grad_t)
    board = lax.dot_general(member, smooth, (((0,), (1,)), ((), ())), precision=lax.Precision.HIGHEST, preferred_element_type=f32)
    terms = terms.reshape(groups, 2, half, proj)
    terms = terms[:, 0] + core_other(terms[:, 1])
    doc_grad = lax.psum_scatter(terms, "dp", scatter_dimension=0)
    doc_dz = (inverse * (doc_grad - doc_units * jnp.sum(doc_grad * doc_units, axis=-1, keepdims=True))).astype(bf16)
    doc_dy = dot(doc_dz, proj_weight, contract_cols)
    proj_grad = dot(doc_y, doc_dz, contract_rows) + dot(query_y, query_dz, contract_rows)
    own = (query_dy, doc_dy, jnp.zeros_like(doc_dy))
    received = [jnp.zeros((half // 2, model), bf16)] * 2
    pairs, sums = {}, {}
    vectors, ub, pb = None, None, None
    input_grads = [None, None]
    after = ()
    line = LineSum() if groups == 4 else None
    chunk_counts = (4, 4, 1, 4)
    plain = []
    board = board + core_other(board)
    proj_grad = dp_sum(proj_grad + core_other(proj_grad))

    for step in range(3):

        def hook(stage, one, two, step=step):
            if stage == "between":
                return line.step((one,)) if line is not None and step == 2 else ()
            done = []
            for place, pair in zip((0, 1) if stage == "feed" else (2, 3), (one, two)):
                pairs[step, place] = pair
                if step == 2:
                    chunks = weight_step(kept[0][place], pair, sums[place], True, chunk_counts[place])
                    if line is not None:
                        line.put(list(chunks))
                    else:
                        plain.append(lax.psum(jnp.concatenate(chunks), "dp").astype(f32))
                    done += chunks[:1]
            if step == 1 and stage == "attend":
                for place in range(4):
                    sums[place] = weight_step(kept[2][place] + kept[1][place], pairs[0, place] + pairs[1, place])
                    done.append(sums[place])
            return tuple(done)

        if step == 2:
            after = tuple(after) + (proj_grad, board)
        dh, vec, ub_now, pb_now, after = backward(flag, received, own[step], w, *contexts[2 - step], records[2 - step], hook, after)
        vectors = vec if vectors is None else vectors + vec
        ub = ub_now if ub is None else ub + ub_now
        pb = pb_now if pb is None else pb + pb_now
        if step < 2:
            received = [to_section(part.astype(bf16), [(1, 0)]) for part in dh]
        if step >= 1:
            input_grads[2 - step] = lax.dynamic_slice_in_dim(jnp.concatenate(dh), chip * share, share, 0)

    if line is not None:
        while line.busy():
            line.step()
        spread, at = [], 0
        for n in chunk_counts:
            spread.append(gathered_line(line.results[at : at + n]))
            at += n
    else:
        spread = plain
    d_down, d_up, d_out, d_qkv = spread
    units_count = up_weight.shape[-1]
    small = jnp.concatenate([vectors.reshape(6, model)], axis=0)
    small = small + core_other(small)
    ub = ub[:, :units_count] + core_other(ub[:, units_count:])
    pb = pb[:, :wide] + core_other(pb[:, wide:])
    vector = dp_sum(jnp.concatenate([ub[0], pb[0], small.reshape(-1)]).reshape(-1, LANES)).reshape(-1)
    ub = vector[:units_count][None]
    pb = vector[units_count : units_count + wide]
    small = vector[units_count + wide :].reshape(6, model)
    stack = jnp.stack(input_grads)
    swap = [(0, 1), (1, 0)]
    mid, docs = model // 2, groups // 2
    sent_input = to_section(stack[:, :, mid:], swap)
    sent_board, sent_proj = to_section((board[:, :docs], proj_grad[:mid]), swap)
    return (
        jnp.where(first, sent_board, board[:, docs:]),
        jnp.where(first, stack[:, :, :mid], sent_input),
        d_qkv.reshape(1, model, 3, width),
        pb.reshape(1, 3, width),
        d_out[None],
        d_up[None],
        ub,
        d_down[None],
        small[0:2][None],
        small[2:4][None],
        small[4:6][None],
        jnp.where(first, sent_proj, proj_grad[mid:]),
    )


def solution(mesh):
    return jax.shard_map(
        on_device,
        mesh=mesh,
        in_specs=(
            P("dp", "tensor", None),
            P("dp", None),
            P("dp", None),
            P("section", None, None, "tensor"),
            P("section", None, "tensor"),
            P("section", "tensor", None),
            P("section", None, "tensor"),
            P("section", "tensor"),
            P("section", "tensor", None),
            P("section", None, None),
            P("section", None, None),
            P("section", None, None),
            P(),
        ),
        out_specs=(
            P("dp", "section"),
            P("dp", "tensor", "section"),
            P("section", None, None, "tensor"),
            P("section", None, "tensor"),
            P("section", "tensor", None),
            P("section", None, "tensor"),
            P("section", "tensor"),
            P("section", "tensor", None),
            P("section", None, None),
            P("section", None, None),
            P("section", None, None),
            P("section", None),
        ),
        check_vma=False,
    )
```

```python
import functools

import jax
import jax.numpy as jnp
import numpy as np
from jax import lax
from jax.experimental import pallas as pl
from jax.experimental.pallas import tpu as pltpu
from jax.sharding import PartitionSpec as P

HD = 64
QLEN = 32
LANES = 128

norm_eps = 1e-05
unit_eps = 1e-06
softness_factor = 0.0625
rope_base = 10000.0
hidden_score = -1000000000.0
contract_rows = (((0,), (0,)), ((), ()))
contract_cols = (((1,), (1,)), ((), ()))
contract_inner = (((1,), (0,)), ((), ()))
bf16 = jnp.bfloat16
f32 = jnp.float32


def dot(left, right, contraction=contract_inner):
    return lax.dot_general(left, right, contraction, preferred_element_type=f32)


def flip(value, bit):
    count = lax.axis_size("tensor")
    return lax.ppermute(value, "tensor", [(i, i ^ (1 << bit)) for i in range(count)])


def chip_bits():
    return range(1, lax.axis_size("tensor").bit_length() - 1)


def core_other(value):
    return flip(value, 0)


def chips_gather(value, chip):
    for bit in chip_bits():
        other = flip(value, bit)
        upper = (chip >> (bit - 1)) % 2 == 1
        value = jnp.concatenate([jnp.where(upper, other, value), jnp.where(upper, value, other)], axis=0)
    return value


def chips_other(low):
    bits = list(chip_bits())
    if not bits:
        return low, jnp.zeros_like(low)
    for bit in bits[:-1]:
        low = (low.astype(f32) + flip(low, bit).astype(f32)).astype(bf16)
    return low, flip(low, bits[-1])


def to_section(value, pairs):
    return lax.ppermute(value, "section", pairs)


def dp_gather(value):
    count = lax.axis_size("dp")
    me = lax.axis_index("dp")
    value = value[None]
    step = 1
    while step < count:
        other = lax.ppermute(value, "dp", [(i, i ^ step) for i in range(count)])
        upper = (me // step) % 2 == 1
        value = jnp.concatenate([jnp.where(upper, other, value), jnp.where(upper, value, other)], axis=0)
        step *= 2
    return value


def dp_sum(value):
    count = lax.axis_size("dp")
    step = 1
    while step < count:
        value = value + lax.ppermute(value, "dp", [(i, i ^ step) for i in range(count)])
        step *= 2
    return value


def slot_kernel(*refs, own, across, next_own, result):
    refs = list(refs)
    end = refs.pop(0)[0, 0] == 1
    take = lambda wanted: refs.pop(0)[...] if wanted else None
    chunk, arrived = take(own), take(own or result)
    side, over = take(across), take(across)
    following = take(next_own)
    finished = take(result)
    total = (side.astype(f32) + over.astype(f32)).astype(bf16) if across else None
    if own:
        refs.pop(0)[...] = (chunk.astype(f32) + arrived.astype(f32)).astype(bf16)
    if across or next_own:
        if not across:
            onward = following
        elif not next_own:
            onward = total
        else:
            onward = jnp.where(end, following, total)
        refs.pop(0)[...] = onward
    if across:
        refs.pop(0)[...] = total
    if result:
        refs.pop(0)[...] = jnp.where(end, arrived, finished).astype(f32)


class LineSum:

    def __init__(self, end, chunks, out_rows):
        self.end, self.chunks, self.count = end, chunks, len(chunks)
        self.k, self.side, self.over, self.total, self.results = 0, None, None, None, []
        self.arrived = []

    def outer(self, value):
        self.arrived.append(lax.ppermute(value, "dp", [(0, 1), (1, 0), (2, 3), (3, 2)]))

    def start(self):
        self.outer(self.chunks[0]())
        self.outer(self.chunks[1]())

    def step(self, after=()):
        k, n = self.k, self.count
        own, across, next_own, result = k < n, 1 <= k <= n, 1 <= k < n - 1, k >= 2
        arrived = self.arrived.pop(0)
        chunk = self.chunks[k]() if own else None
        following = self.chunks[k + 1]() if next_own else None
        ins = [self.end]
        ins += [chunk] if own else []
        ins += [arrived] if own or result else []
        ins += [self.side, self.over] if across else []
        ins += [following] if next_own else []
        ins += [self.total] if result else []
        shape = arrived.shape
        outs = [(shape, bf16)] * (own + (across or next_own) + across) + [(shape, f32)] * result
        got = list(
            call(functools.partial(slot_kernel, own=own, across=across, next_own=next_own, result=result), ins, outs, us=2, after=after, smem=(0,))
        )
        side = got.pop(0) if own else None
        onward = got.pop(0) if across or next_own else None
        self.total = got.pop(0) if across else None
        if result:
            self.results.append(got.pop(0))
        self.side = side
        if own:
            self.over = lax.ppermute(side, "dp", [(1, 2), (2, 1)])
        if onward is not None:
            self.outer(onward)
        self.k += 1
        return (side if own else onward if onward is not None else self.results[-1],)

    def busy(self):
        return self.k <= self.count + 1


class LineSums:

    def __init__(self, end, chunks):
        self.lines = [LineSum(end, chunks[i::2], None) for i in range(2)]
        self.last, self.turn, self.seen = (), 0, []

    def start(self):
        for line in self.lines:
            line.start()

    def step(self, after=()):
        line = self.lines[self.turn]
        self.turn = 1 - self.turn
        if line.busy():
            self.last = line.step(tuple(after) + self.last)
            self.seen.append(self.last)
        return self.last

    def finish(self):
        while any(line.busy() for line in self.lines):
            self.step()
        results = [None] * sum(line.count for line in self.lines)
        for i, line in enumerate(self.lines):
            results[i::2] = line.results
        return results


def rope_tables(positions):
    half = HD // 2
    frequency = np.power(np.float32(rope_base), (-2.0 * np.arange(half) / HD).astype(np.float32)).astype(np.float32)
    angles = (positions.astype(np.float32)[:, None] * frequency[None, :]).astype(np.float32)
    cosine, sine = np.cos(angles), np.sin(angles)
    head = (np.concatenate([cosine, cosine], 1), np.concatenate([-sine, sine], 1))
    return tuple(np.tile(part, (1, LANES // HD)).astype(np.float32) for part in head)


VMEM = pl.BlockSpec(memory_space=pltpu.VMEM)
ANY = pl.BlockSpec(memory_space=pl.ANY)
SMEM = pl.BlockSpec(memory_space=pltpu.SMEM)


pace = {"now": 1.0}
EARLY, LATE = 1.0, 0.3


def cost(us):
    us = us * pace["now"]
    return pl.CostEstimate(flops=int(us * 1.1e9), bytes_accessed=int(us * 1e6), transcendentals=0)


def held(x):
    return pltpu.with_memory_space_constraint(x, pltpu.HBM)


def call(kernel, ins, outs, us, scratch=(), after=(), smem=(), keep=(), limit=16):
    n = len(ins)

    def body(*refs):
        kernel(*refs[:n], *refs[n + len(after) :])

    return pl.pallas_call(
        body,
        in_specs=[SMEM if i in smem else VMEM for i in range(n)] + [ANY] * len(after),
        out_specs=[VMEM] * len(outs),
        out_shape=[pltpu.HBM(*out) if i in keep else jax.ShapeDtypeStruct(*out) for i, out in enumerate(outs)],
        scratch_shapes=list(scratch),
        compiler_params=pltpu.CompilerParams(vmem_limit_bytes=limit * 1024 * 1024),
        cost_estimate=cost(us),
        name=getattr(kernel, "func", kernel).__name__,
    )(*ins, *after)


def load_kernel(own, oth, out, sem, axis):
    size = own.shape[axis]
    places = [out.at[:, :size], out.at[:, size:]] if axis else [out.at[:size], out.at[size:]]
    copies = [pltpu.make_async_copy(x, place, sem.at[i]) for i, (x, place) in enumerate(zip((own, oth), places))]
    for copy in copies:
        copy.start()
    for copy in copies:
        copy.wait()


def chip_weight(own, axis):
    other = core_other(own)
    shape = tuple(2 * n if i == axis else n for i, n in enumerate(own.shape))
    return pl.pallas_call(
        functools.partial(load_kernel, axis=axis),
        in_specs=[ANY, ANY],
        out_specs=VMEM,
        out_shape=pltpu.VMEM(shape, own.dtype),
        cost_estimate=cost(2),
        scratch_shapes=[pltpu.SemaphoreType.DMA((2,))],
        compiler_params=pltpu.CompilerParams(vmem_limit_bytes=16 * 1024 * 1024),
    )(own, other)


def half_rows(ref, c):
    size = ref.shape[0] // 2
    return ref[c * size : (c + 1) * size, :]


def half_lanes(ref, c):
    size = ref.shape[1] // 2
    return ref[:, c * size : (c + 1) * size]


def merge(out, before, value):
    size = value.shape[0]
    out[:size, :] = before[...]
    out[size:, :] = value


def swap_halves(tile):
    lane = lax.broadcasted_iota(jnp.int32, tile.shape, 1)
    return jnp.where(lane % HD < HD // 2, pltpu.roll(tile, LANES - HD // 2, 1), pltpu.roll(tile, HD // 2, 1))


def qkv_kernel(flag, entering, received_a, received_b, w, b, cos, sin, h_ref, q_ref, kv_ref):
    received = jnp.concatenate([received_a[...], received_b[...]], axis=0)
    h = jnp.where(flag[0, 0] == 1, entering[...], received)
    h_ref[...] = h
    width = w.shape[1] // 6
    c, s = cos[...], sin[...]
    for place in range(2):
        at = slice(place * 3 * width, (place + 1) * 3 * width)
        p = dot(h, w[:, at]) + b[:, at]
        for t in range(0, width, LANES):
            at = slice(place * width + t, place * width + t + LANES)
            tile = p[:, t : t + LANES]
            q_ref[:, at] = (tile * c + swap_halves(tile) * s).astype(bf16)
            tile = p[:, width + t : width + t + LANES]
            kv_ref[:, at] = (tile * c + swap_halves(tile) * s).astype(bf16)
        kv_ref[:, 2 * width + place * width : 2 * width + (place + 1) * width] = p[:, 2 * width :].astype(bf16)


def qkv_step(flag, entering, received, w, tables, after=()):
    rows, model = entering.shape
    features = w["qkv"].shape[1] // 3
    return call(
        qkv_kernel,
        [flag, entering, *received, w["qkv"], w["qkv_b"], *tables],
        [((rows, model), bf16), ((rows, features), bf16), ((rows, 2 * features), bf16)],
        after=after,
        smem=(0,),
        keep=(0, 1, 2),
        us=2,
    )


def head_rows(tile, place):
    row = lax.broadcasted_iota(jnp.int32, tile.shape, 0)
    return jnp.where(row // HD == place, tile, 0.0).astype(bf16)


def head_lanes(tile, place):
    lane = lax.broadcasted_iota(jnp.int32, tile.shape, 1)
    return jnp.where(lane // HD == place, tile, 0.0).astype(bf16)


def tile_at(j, features, base=0):
    return slice(base + j * LANES, base + (j + 1) * LANES)


def partner_tile(j, features):
    tiles = features // LANES
    return (j + tiles // 2) % tiles


def partner_base(j, features, base=0):
    return tile_at(partner_tile(j, features), features, base)


def attend_kernel(*refs, c):
    q_ref, kv_own, kv_oth, bias_ref, w = refs[:5]
    if c:
        o_before, v_t, refs = refs[5], refs[6], refs[7:]
        o_own, o_oth, lse_ref, low_ref, o_t, s_all = refs
    else:
        o_first, k_t, v_t, lse_ref, low_ref, o_t, s_all = refs[5:]
    features = q_ref.shape[1]
    rows = kv_own.shape[0]
    some = rows // 2
    q_half = half_rows(q_ref, c)
    for j in range(features // LANES):
        at = tile_at(j, features)
        q_t = q_half[:, at].astype(f32).T * HD ** (-0.5)
        k_here, k_there = kv_own[:, at], kv_oth[:, partner_base(j, features)]
        for place in range(2):
            q_one = head_rows(q_t, place)
            s_all[2 * j + place, :rows, :] = dot(k_here, q_one)
            s_all[2 * j + place, rows:, :] = dot(k_there, q_one)
        if not c:
            v_here, v_there = kv_own[:, tile_at(j, features, features)], kv_oth[:, partner_base(j, features, features)]
            v_t[at, :rows] = v_here.astype(f32).T.astype(bf16)
            v_t[at, rows:] = v_there.astype(f32).T.astype(bf16)
            k_t[at, :rows] = k_here.astype(f32).T.astype(bf16)
            k_t[at, rows:] = k_there.astype(f32).T.astype(bf16)
    bias = bias_ref[:, c * some : (c + 1) * some]
    for h in range(features // HD):
        s = s_all[h] + bias
        peak = jnp.max(s, axis=0, keepdims=True)
        e = jnp.exp(s - peak)
        total = jnp.sum(e, axis=0, keepdims=True)
        s_all[h] = e * (1.0 / total)
        lse_ref[h : h + 1, :] = peak + jnp.log(total)
    for h in range(features // HD):
        o_t[h * HD : (h + 1) * HD, :] = dot(v_t[h * HD : (h + 1) * HD, :], s_all[h].astype(bf16))
    o = o_t[...].T.astype(bf16)
    half = features // 2
    if c:
        merge(o_own, o_before[:, :half], o[:, :half])
        merge(o_oth, o_before[:, half:], o[:, half:])
    else:
        o_first[...] = o
    low_ref[...] = dot(o, w[...]).astype(bf16)


def attend_step(c, q, kv, kv_other, bias, w, before=(), after=()):
    rows, features = q.shape
    model = w["out"].shape[1]
    some = rows // 2
    heads = features // HD
    if c:
        kept = [((rows, features // 2), bf16)] * 2
    else:
        kept = [((some, features), bf16), ((features, 2 * rows), bf16), ((features, 2 * rows), bf16)]
    return call(
        functools.partial(attend_kernel, c=c),
        [q, kv, kv_other, bias, w["out"], *before],
        kept + [((heads, some), f32), ((some, model), bf16)],
        scratch=[pltpu.VMEM((features, some), f32), pltpu.VMEM((heads, 2 * rows, some), f32)],
        after=after,
        keep=(0, 1, 2) if c else (1, 3),
        us=4,
    )


def normed(values):
    centred = values - jnp.mean(values, axis=-1, keepdims=True)
    inverse = lax.rsqrt(jnp.mean(centred * centred, axis=-1, keepdims=True) + norm_eps)
    return centred * inverse, inverse


def norm_back(gradient, n, inverse):
    return inverse * (gradient - jnp.mean(gradient, axis=-1, keepdims=True) - n * jnp.mean(gradient * n, axis=-1, keepdims=True))


def feed_kernel(*refs, c):
    h, low, recv, vec, up, b, down = refs[:7]
    before, refs = (refs[7:10], refs[10:]) if c else (None, refs[7:])
    n_ref, r_ref, sl_ref, low_ref, g_own, rest = refs
    s1 = half_rows(h, c).astype(f32) + (low[...].astype(f32) + recv[...].astype(f32)) + vec[0:1, :]
    n, r = normed(s1)
    n_ref[...] = n
    r_ref[...] = r
    h1 = (n * vec[1:2, :] + vec[2:3, :]).astype(bf16)
    u = dot(h1, up[...]) + b[...]
    phi = 0.5 * (1.0 + lax.erf(u * 0.7071067811865476))
    g = (u * phi).astype(bf16)
    sl_ref[...] = (phi + u * jnp.exp(-0.5 * u * u) * 0.3989422804014327).astype(bf16)
    low_ref[...] = dot(g, down[...]).astype(bf16)
    units = up.shape[1] // 2
    some, model = h1.shape
    if c:
        g_before, rest_before, o_oth = before
        merge(g_own, g_before, g[:, :units])
        rest[:some, :model] = rest_before[:, :model]
        rest[some:, :model] = h1
        rest[:, model : 2 * model] = h[...]
        rest[:some, 2 * model : 2 * model + units] = rest_before[:, model:]
        rest[some:, 2 * model : 2 * model + units] = g[:, units:]
        rest[:, 2 * model + units :] = o_oth[...]
    else:
        g_own[...] = g[:, :units]
        rest[:, :model] = h1
        rest[:, model:] = g[:, units:]


def feed_step(c, h, low, recv, vec, w, before=(), after=()):
    rows, model = h.shape
    units = w["up"].shape[1] // 2
    some = rows // 2
    if c:
        kept = [((rows, units), bf16), ((rows, 2 * model + units + before[-1].shape[1]), bf16)]
    else:
        kept = [((some, units), bf16), ((some, model + units), bf16)]
    return call(
        functools.partial(feed_kernel, c=c),
        [h, low, recv, vec, w["up"], w["up_b"], w["down"], *before],
        [((some, model), f32), ((some, 1), f32), ((some, 2 * units), bf16), ((some, model), bf16)] + kept,
        after=after,
        keep=(0, 1, 2, 4, 5) if c else (0, 1, 2),
        us=4,
    )


def output_kernel(n1, low, recv, vec, n_ref, r_ref, y_ref):
    s2 = n1[...] * vec[0:1, :] + vec[1:2, :] + (low[...].astype(f32) + recv[...].astype(f32)) + vec[2:3, :]
    n, r = normed(s2)
    n_ref[...] = n
    r_ref[...] = r
    y_ref[...] = (n * vec[3:4, :] + vec[4:5, :]).astype(bf16)


def output_step(n1, low, recv, vec, after=()):
    return call(output_kernel, [n1, low, recv, vec], [(n1.shape, f32), ((n1.shape[0], 1), f32), (n1.shape, bf16)], after=after, keep=(0, 1), us=2.3)


def feed_back_head(dy, n, r, gain, ds_ref, vec_ref):
    ds = norm_back(dy * gain, n, r)
    ds_ref[...] = ds
    vec_ref[0:1, :] = jnp.sum(ds, axis=0, keepdims=True)
    vec_ref[1:2, :] = jnp.sum(dy * n, axis=0, keepdims=True)
    vec_ref[2:3, :] = jnp.sum(dy, axis=0, keepdims=True)
    return ds.astype(bf16)


def feed_back_tail(f, up, down, sl, low_ref, ub_ref):
    du = dot(f, down[...], contract_cols) * sl[...].astype(f32)
    ub_ref[...] = jnp.sum(du, axis=0, keepdims=True)
    u = du.astype(bf16)
    low_ref[...] = dot(u, up[...], contract_cols).astype(bf16)
    return u


def feed_back_kernel(*refs, c):
    flag, received, own, n2, r2, gain, up, down, sl = refs[:9]
    before, refs = (refs[9:11], refs[11:]) if c else (None, refs[9:])
    ds_ref, low_ref, vec_ref, ub_ref, u_own, rest = refs
    dy = jnp.where(flag[0, 0] == 1, received[...].astype(f32), own[...])
    f = feed_back_head(dy, n2[...], r2[...], gain[...], ds_ref, vec_ref)
    u = feed_back_tail(f, up, down, sl, low_ref, ub_ref)
    units = up.shape[1] // 2
    some, model = f.shape
    if c:
        merge(u_own, before[0], u[:, :units])
        rest[:some, :] = before[1][...]
        rest[some:, :model] = f
        rest[some:, model:] = u[:, units:]
    else:
        u_own[...] = u[:, :units]
        rest[:, :model] = f
        rest[:, model:] = u[:, units:]


def feed_back_step(c, flag, received, own, n2, r2, gain, w, sl, before=(), after=()):
    some, model = n2.shape
    units = w["up"].shape[1] // 2
    kept = 2 * some if c else some
    return call(
        functools.partial(feed_back_kernel, c=c),
        [flag, received, own, n2, r2, gain, w["up"], w["down"], sl, *before],
        [
            ((some, model), f32), ((some, model), bf16), ((3, model), f32), ((1, 2 * units), f32),
            ((kept, units), bf16), ((kept, model + units), bf16),
        ],
        after=after,
        smem=(0,),
        keep=(0, 2, 3, 4, 5) if c else (0, 2, 3),
        us=5.5,
    )


def first_kernel(rec_a, rec_b, n_a, n_b, r_a, r_b, gain, ds_a, ds_b, vec_a, vec_b, f_ref):
    some = rec_a.shape[0]
    f_ref[:some, :] = feed_back_head(rec_a[...].astype(f32), n_a[...], r_a[...], gain[...], ds_a, vec_a)
    f_ref[some:, :] = feed_back_head(rec_b[...].astype(f32), n_b[...], r_b[...], gain[...], ds_b, vec_b)


def first_step(received, n2, r2, gain, after=()):
    some, model = n2[0].shape
    return call(
        first_kernel,
        [*received, *n2, *r2, gain],
        [((some, model), f32)] * 2 + [((3, model), f32)] * 2 + [((2 * some, model), bf16)],
        after=after,
        keep=(0, 1, 2, 3),
        us=2.5,
    )


def second_kernel(*refs, c):
    f, up, down, sl = refs[:4]
    before, refs = (refs[4:6], refs[6:]) if c else (None, refs[4:])
    low_ref, ub_ref, u_own, u_oth = refs
    u = feed_back_tail(half_rows(f, c), up, down, sl, low_ref, ub_ref)
    units = up.shape[1] // 2
    for place, value in enumerate((u[:, :units], u[:, units:])):
        out = (u_own, u_oth)[place]
        if c:
            merge(out, before[place], value)
        else:
            out[...] = value


def second_step(c, f, w, sl, before=(), after=()):
    rows, model = f.shape
    units = w["up"].shape[1] // 2
    kept = rows if c else rows // 2
    return call(
        functools.partial(second_kernel, c=c),
        [f, w["up"], w["down"], sl, *before],
        [((rows // 2, model), bf16), ((1, 2 * units), f32), ((kept, units), bf16), ((kept, units), bf16)],
        after=after,
        keep=(1, 2, 3) if c else (1,),
        us=4.5,
    )


def attend_back_kernel(*refs, c):
    (ds2, low, recv, n1, r1, gain, w, q_ref, kv_own, kv_oth, k_t, bias_ref, lse_ref), refs = refs[:13], refs[13:]
    if c:
        (own_before, oth_before, out_before), refs = refs[:3], refs[3:]
    ds_ref, dq_ref, vec_ref, dkv_ref, dkv_send, out_ref, dq_t, s_all, d_all, a_all, slopes = refs
    features = q_ref.shape[1]
    rows = kv_own.shape[0]
    some = rows // 2
    dh1 = ds2[...] + (low[...].astype(f32) + recv[...].astype(f32))
    n = n1[...]
    ds1 = norm_back(dh1 * gain[...], n, r1[...])
    ds_ref[...] = ds1
    vec_ref[0:1, :] = jnp.sum(ds1, axis=0, keepdims=True)
    vec_ref[1:2, :] = jnp.sum(dh1 * n, axis=0, keepdims=True)
    vec_ref[2:3, :] = jnp.sum(dh1, axis=0, keepdims=True)
    spread = ds1.astype(bf16)
    if c:
        merge(out_ref, out_before, spread)
    else:
        out_ref[...] = spread
    q_half = half_rows(q_ref, c)
    for j in range(features // LANES):
        at = tile_at(j, features)
        q_t = q_half[:, at].astype(f32).T * HD ** (-0.5)
        k_here, k_there = kv_own[:, at], kv_oth[:, partner_base(j, features)]
        for place in range(2):
            q_one = head_rows(q_t, place)
            s_all[2 * j + place, :rows, :] = dot(k_here, q_one)
            s_all[2 * j + place, rows:, :] = dot(k_there, q_one)
    mixed = dot(spread, w[...], contract_cols).astype(bf16).astype(f32)
    for j in range(features // LANES):
        do_t = mixed[:, tile_at(j, features)].T
        v_here, v_there = kv_own[:, tile_at(j, features, features)], kv_oth[:, partner_base(j, features, features)]
        for place in range(2):
            do_one = head_rows(do_t, place)
            d_all[2 * j + place, :rows, :] = dot(v_here, do_one)
            d_all[2 * j + place, rows:, :] = dot(v_there, do_one)
    bias = bias_ref[:, c * some : (c + 1) * some]
    for h in range(features // HD):
        a = jnp.exp(s_all[h] + bias - lse_ref[h : h + 1, :])
        da = d_all[h]
        slope = a * (da - jnp.sum(da * a, axis=0, keepdims=True))
        slopes[h] = slope.astype(bf16) * jnp.asarray(HD ** (-0.5), bf16)
        a_all[h] = a.astype(bf16)
    for h in range(features // HD):
        dq_t[h * HD : (h + 1) * HD, :] = dot(k_t[h * HD : (h + 1) * HD, :], slopes[h])
    for j in range(features // LANES):
        at, v_at = tile_at(j, features), tile_at(j, features, features)
        theirs, v_theirs = partner_base(j, features), partner_base(j, features, features)
        q, do = q_half[:, at].astype(f32), mixed[:, at]
        dk = dot(slopes[2 * j], head_lanes(q, 0)) + dot(slopes[2 * j + 1], head_lanes(q, 1))
        dv = dot(a_all[2 * j], head_lanes(do, 0)) + dot(a_all[2 * j + 1], head_lanes(do, 1))
        if c:
            dkv_ref[:, at] = dk[:rows] + own_before[:, at]
            dkv_ref[:, v_at] = dv[:rows] + own_before[:, v_at]
            dkv_send[:, theirs] = (dk[rows:] + oth_before[:, theirs]).astype(bf16)
            dkv_send[:, v_theirs] = (dv[rows:] + oth_before[:, v_theirs]).astype(bf16)
        else:
            dkv_ref[:, at] = dk[:rows]
            dkv_ref[:, v_at] = dv[:rows]
            dkv_send[:, theirs] = dk[rows:]
            dkv_send[:, v_theirs] = dv[rows:]
    dq_ref[...] = dq_t[...].T


def attend_back_step(c, ds2, low, recv, n1, r1, gain, w, q, kv, kv_other, k_t, bias, lse, before=(), after=()):
    some, model = ds2.shape
    features = q.shape[1]
    rows = 2 * some
    heads = features // HD
    all_heads = (heads, 2 * rows, some)
    return call(
        functools.partial(attend_back_kernel, c=c),
        [ds2, low, recv, n1, r1, gain, w["out"], q, kv, kv_other, k_t, bias, lse, *before],
        [
            ((some, model), f32), ((some, features), f32), ((3, model), f32),
            ((rows, 2 * features), f32), ((rows, 2 * features), bf16 if c else f32), ((rows if c else some, model), bf16),
        ],
        scratch=[
            pltpu.VMEM((features, some), f32), pltpu.VMEM(all_heads, f32), pltpu.VMEM(all_heads, f32), pltpu.VMEM(all_heads, bf16),
            pltpu.VMEM(all_heads, bf16),
        ],
        after=after,
        keep=(0, 1, 2, 3, 5) if c else (0, 1, 2),
        limit=24,
        us=6.5,
    )


def qkv_back_kernel(*refs, c):
    dq, dkv_ref, arrived_ref, cos, sin, w = refs[:6]
    before, refs = (refs[6:9], refs[9:]) if c else (None, refs[6:])
    low_ref, b_ref, p_own, rest = refs
    some, features = dq.shape
    width = features // 2
    cosine, sine = half_rows(cos, c), half_rows(sin, c)
    dkv = half_rows(dkv_ref, c) + half_rows(arrived_ref, c).astype(f32)
    rows_at = slice(some, 2 * some) if c else slice(0, some)
    model = w.shape[0] if c else 0
    total = None
    for place, p_ref in enumerate((p_own, rest)):
        base = place * 3 * width
        start = place * model
        for t in range(0, width, LANES):
            at = slice(place * width + t, place * width + t + LANES)
            v_at = slice(features + place * width + t, features + place * width + t + LANES)
            gq, gk, gv = dq[:, at], dkv[:, at], dkv[:, v_at]
            gq = gq * cosine - swap_halves(gq) * sine
            gk = gk * cosine - swap_halves(gk) * sine
            for part, g in enumerate((gq, gk, gv)):
                to = part * width + t
                p_ref[rows_at, start + to : start + to + LANES] = g.astype(bf16)
                b_ref[0:1, base + to : base + to + LANES] = jnp.sum(g, axis=0, keepdims=True)
        part = dot(p_ref[rows_at, start : start + 3 * width], w[:, base : base + 3 * width], contract_cols)
        total = part if total is None else total + part
    low_ref[...] = total.astype(bf16)
    if c:
        p_own[:some, :] = before[0][...]
        rest[:some, model:] = before[1][...]
        rest[:, :model] = before[2][...]


def qkv_back_step(c, dq, dkv, arrived, tables, w, before=(), after=()):
    some, features = dq.shape
    model, wide = w["qkv"].shape
    kept = [((2 * some, wide // 2), bf16), ((2 * some, model + wide // 2), bf16)] if c else [((some, wide // 2), bf16)] * 2
    return call(
        functools.partial(qkv_back_kernel, c=c),
        [dq, dkv, arrived, *tables, w["qkv"], *before],
        [((some, model), bf16), ((1, wide), f32)] + kept,
        after=after,
        keep=(1, 2, 3) if c else (1,),
        us=3.4,
    )


def end_kernel(ds, low, recv, out, low_out):
    dh = ds[...] + (low[...].astype(f32) + recv[...].astype(f32))
    out[...] = dh
    low_out[...] = dh.astype(bf16)


def end_step(ds, low, recv, after):
    return call(end_kernel, [ds, low, recv], [(ds.shape, f32), (ds.shape, bf16)], us=1.5, after=after)


def part(array, offset, width):
    return array, offset, width


def weight_kernel(*refs, pieces):
    lefts, rights, outs = refs[:pieces], refs[pieces : 2 * pieces], refs[2 * pieces :]
    left = jnp.concatenate([x[...] for x in lefts], axis=0)
    right = jnp.concatenate([x[...] for x in rights], axis=0)
    total = dot(left, right, contract_rows).astype(bf16)
    for i, out in enumerate(outs):

        @pl.when(pl.program_id(0) == i)
        def _(out=out):
            out[...] = total


def weight_step(lefts, rights, steps):
    shape = (lefts[0][2], rights[0][2])
    steps = min(steps, shape[0] // LANES)
    some = (shape[0] // steps, shape[1])
    specs = [pl.BlockSpec((x.shape[0], some[0]), lambda i, at=offset // some[0]: (0, at + i)) for x, offset, _ in lefts]
    specs += [pl.BlockSpec((x.shape[0], width), lambda i, at=offset // width: (0, at)) for x, offset, width in rights]
    return pl.pallas_call(
        functools.partial(weight_kernel, pieces=len(lefts)),
        grid=(steps,),
        in_specs=specs,
        out_specs=[pl.BlockSpec(some, lambda i: (0, 0))] * steps,
        out_shape=[jax.ShapeDtypeStruct(some, bf16)] * steps,
        cost_estimate=cost(6),
        compiler_params=pltpu.CompilerParams(vmem_limit_bytes=24 * 1024 * 1024),
    )(*[held(x) for x, _, _ in (*lefts, *rights)])


def sum_kernel(x, y, out):
    out[...] = x[...] + y[...]


def sum_after(x, y, after):
    return call(sum_kernel, [x, y], [(x.shape, x.dtype)], us=1, after=after)[0]


def dp_sum_after(value, marks):
    count = lax.axis_size("dp")
    step = 1
    while step < count:
        value = sum_after(value, lax.ppermute(value, "dp", [(i, i ^ step) for i in range(count)]), marks[0])
        marks = marks[1:] or marks
        step *= 2
    return value


def scores_kernel(y_a, y_b, proj, units, alive, grad_t, z_ref, m_ref, dy_a, dy_b, terms_ref, groups):
    low = jnp.concatenate([y_a[...], y_b[...]], axis=0)
    z = dot(low, proj[...])
    inverse = lax.rsqrt(jnp.sum(z * z, axis=-1, keepdims=True) + unit_eps)
    e = z * inverse
    e_low = e.astype(bf16)
    e_t = e_low.astype(f32).T.astype(bf16)
    block = units.shape[0] // groups
    back = None
    for d in range(groups):
        at = slice(d * block, (d + 1) * block)
        docs = units[at, :]
        logits = jnp.where(alive[at, :] > 0, dot(docs, e_t) / softness_factor, hidden_score)
        peak = jnp.max(logits, axis=0, keepdims=True)
        x = jnp.exp(logits - peak)
        total = jnp.sum(x, axis=0, keepdims=True)
        m_ref[d : d + 1, :] = softness_factor * (peak + jnp.log(total))
        pull = (x * (grad_t[d : d + 1, :] / total)).astype(bf16)
        terms_ref[at, :] = dot(pull, e_low)
        part = dot(docs.astype(f32).T.astype(bf16), pull)
        back = part if back is None else back + part
    de = back.T
    dz = (inverse * (de - e * jnp.sum(de * e, axis=-1, keepdims=True))).astype(bf16)
    z_ref[...] = dz
    dy = dot(dz, proj[...], contract_cols)
    some = dy_a.shape[0]
    dy_a[...] = dy[:some]
    dy_b[...] = dy[some:]


def scores_step(y, proj, units, alive, grad_t):
    rows, model = 2 * y[0].shape[0], y[0].shape[1]
    groups, width = grad_t.shape[0], proj.shape[1]
    return call(
        functools.partial(scores_kernel, groups=groups),
        [*y, proj, units, alive, grad_t],
        [((rows, width), bf16), ((groups, rows), f32), ((rows // 2, model), f32), ((rows // 2, model), f32), ((units.shape[0], width), f32)],
        limit=32,
        us=2.6,
    )


def forward(flag, entering, received, w, bias, tables, after=()):
    h, q, kv = qkv_step(flag, entering, received, w, tables, after)
    kv_other = held(core_other(kv))
    h_here, q, kv = held(h), held(q), held(kv)
    o_a, k_t, v_t, lse_a, low_a = attend_step(0, q, kv, kv_other, bias, w)
    sum_a = chips_other(low_a)
    o, o_o, lse_b, low_b = attend_step(1, q, kv, kv_other, bias, w, (o_a, v_t))
    sum_b = chips_other(low_b)
    n1_a, r1_a, sl_a, low_a, *before = feed_step(0, h_here, *sum_a, w["vec_feed"], w)
    sum_a = chips_other(low_a)
    n1_b, r1_b, sl_b, low_b, g, rest = feed_step(1, h_here, *sum_b, w["vec_feed"], w, (*before, held(o_o)))
    sum_b = chips_other(low_b)
    n1_a, n1_b = held(n1_a), held(n1_b)
    n2_a, r2_a, y_a = output_step(n1_a, *sum_a, w["vec_out"])
    n2_b, r2_b, y_b = output_step(n1_b, *sum_b, w["vec_out"], (y_a,))
    there = core_other(rest)
    model, units, width = h.shape[1], g.shape[1], o.shape[1]
    kept = (
        (part(g, 0, units), part(there, 2 * model, units)),
        (part(rest, 0, model), part(there, 0, model)),
        (part(o, 0, width), part(there, 2 * model + units, width)),
        (part(rest, model, model), part(there, model, model)),
    )
    a = (held(lse_a), n1_a, held(r1_a), held(sl_a), held(n2_a), held(r2_a))
    b = (held(lse_b), n1_b, held(r1_b), held(sl_b), held(n2_b), held(r2_b))
    return (y_a, y_b), ((q, kv, kv_other, held(k_t)), (a, b)), kept


def backward(flag, received, own, w, bias, tables, record, hook, last):
    (q, kv, kv_other, k_t), halves = record
    model, units = w["up"].shape[0], w["up"].shape[1] // 2
    parts, vectors, ubs, ds2s, before = [], [], [], [], ()
    after = ()
    if last:
        *ds2s, vec_a, vec_b, f = first_step(received, [x[4] for x in halves], [x[5] for x in halves], w["gain"][1:2])
        ds2s, vectors = [held(x) for x in ds2s], [vec_a, vec_b]
        after = hook(0, (part(f, 0, model), part(core_other(f), 0, model)))
        for c in range(2):
            low, ub, *before = second_step(c, f, w, halves[c][3], before, after)
            parts.append(chips_other(low))
            ubs.append(ub)
            after = ()
        hook("step", low)
        u, u_o = before
        after = hook(1, (part(u, 0, units), part(core_other(u_o), 0, units)))
        after = hook("step", after[0])
    else:
        for c in range(2):
            lse, n1, r1, sl, n2, r2 = halves[c]
            ds2, low, vec, ub, *before = feed_back_step(c, flag, received[c], own[c], n2, r2, w["gain"][1:2], w, sl, before)
            ds2s.append(held(ds2))
            parts.append(chips_other(low))
            vectors.append(vec)
            ubs.append(ub)
        u, rest = before
        there = core_other(rest)
        hook(0, (part(rest, 0, model), part(there, 0, model)))
        hook(1, (part(u, 0, units), part(there, model, units)))
    before, vectors_1, ds1s, dqs = (), [], [], []
    for c in range(2):
        lse, n1, r1, sl, n2, r2 = halves[c]
        ds1, dq, vec, dkv, send, out = attend_back_step(
            c, ds2s[c], *parts[c], n1, r1, w["gain"][0:1], w, q, kv, kv_other, k_t, bias, lse, before, after
        )
        before = (dkv, send, out) if c == 0 else ()
        ds1s.append(ds1)
        dqs.append(held(dq))
        vectors_1.append(vec)
        after = hook("step", dq)
    arrived, dkv = held(core_other(send)), held(dkv)
    nexts, pbs, before = [], [], ()
    for c in range(2):
        low, pb, *before = qkv_back_step(c, dqs[c], dkv, arrived, tables, w, (*before, held(out)) if c else (), after)
        nexts.append(chips_other(low))
        pbs.append(pb)
        after = hook("step", pb)
    p, rest = before
    there = core_other(rest)
    wide = p.shape[1]
    hook(2, (part(rest, 0, model), part(there, 0, model)))
    hook(3, (part(p, 0, wide), part(there, model, wide)))
    after = hook("end", None)
    dh = []
    for c in range(2):
        dh.append(end_step(held(ds1s[c]), *nexts[c], after))
        after = (dh[0][1],)
    vectors = jnp.stack([vectors_1[0] + vectors_1[1], vectors[0] + vectors[1]], axis=1)
    return dh, vectors, ubs[0] + ubs[1], pbs[0] + pbs[1], (parts[1][0], nexts[1][0])


def on_device(tokens, segment, score_grad, qkv_weight, qkv_bias, out_weight, up_weight, up_bias, down_weight, out_bias, norm_gain, norm_shift, proj_weight):
    blocks, share, model = tokens.shape
    pace["now"] = EARLY
    wide = 3 * qkv_weight.shape[-1]
    width = wide // 3
    gain, shift, bias = norm_gain[0].astype(f32), norm_shift[0].astype(f32), out_bias[0].astype(f32)
    first = lax.axis_index("section") == 0
    flag = first.astype(jnp.int32).reshape(1, 1)
    device = lax.axis_index("tensor")
    core, chip = device % 2, device // 2
    chips = lax.axis_size("tensor") // 2
    groups = lax.axis_size("dp")
    half = share * chips
    rows = 2 * half
    proj = proj_weight.shape[1]
    entering = [chips_gather(tokens[b], chip) for b in range(2)]

    def both(own):
        return jnp.concatenate([own, core_other(own)], axis=1)

    w = dict(
        qkv=chip_weight(qkv_weight[0].reshape(model, wide), 1), qkv_b=both(qkv_bias[0].reshape(1, wide).astype(f32)),
        out=chip_weight(out_weight[0], 0), up=chip_weight(up_weight[0], 1), up_b=both(up_bias.astype(f32)),
        down=chip_weight(down_weight[0], 0), gain=gain,
        vec_feed=jnp.stack([bias[0], gain[0], shift[0]]),
        vec_out=jnp.stack([gain[0], shift[0], bias[1], gain[1], shift[1]]),
    )

    def own_first(by_token):
        parts = by_token.reshape((chips, 2, share) + by_token.shape[1:])
        even = parts[:, 0].reshape((half,) + by_token.shape[1:])
        odd = parts[:, 1].reshape((half,) + by_token.shape[1:])
        return jnp.concatenate([jnp.where(core == 0, even, odd), jnp.where(core == 0, odd, even)], axis=0)

    index = np.arange(rows)
    tables = [tuple(own_first(jnp.asarray(part))[:half] for part in rope_tables(p)) for p in (index, index % QLEN)]
    segments = [own_first(segment[b]) for b in range(2)]

    def pick(zero, one):
        ids = jnp.where(first, segments[zero], segments[one])
        bias = jnp.where(ids[:, None] == ids[None, :half], 0.0, hidden_score).astype(f32)
        return bias, tuple(jnp.where(first, x, y) for x, y in zip(tables[zero], tables[one]))

    contexts = [pick(0, 0), pick(1, 0), pick(1, 1)]
    received = [jnp.zeros((half // 2, model), bf16)] * 2
    records, kept, outputs = [], [], []
    prelude = [w["vec_feed"], w["vec_out"], w["up_b"]] + [x for bias_of, tables_of in contexts for x in (bias_of, *tables_of)]
    for tick in range(3):
        y, record, keep = forward(flag, entering[min(tick, 1)], received, w, *contexts[tick], prelude if tick == 0 else ())
        records.append(record)
        kept.append(keep)
        outputs.append(y)
        if tick < 2:
            received = [to_section(part, [(0, 1)]) for part in y]

    doc_y, query_y = jnp.concatenate(outputs[1]), jnp.concatenate(outputs[2])
    z = dot(doc_y, proj_weight)
    inverse = lax.rsqrt(jnp.sum(z * z, axis=-1, keepdims=True) + unit_eps)
    doc_units = z * inverse
    units_own = dp_gather(doc_units.astype(bf16))
    units = jnp.stack([units_own, core_other(units_own)], axis=1).reshape(groups * rows, proj)
    alive = dp_gather((segments[0] == 0).astype(f32).reshape(rows // LANES, LANES)).reshape(groups * rows, 1)
    slots = score_grad.shape[0]
    member = (segments[1][:half, None] == jnp.arange(slots)[None, :]).astype(f32)
    grad_t = lax.dot_general(score_grad, member, (((0,), (1,)), ((), ())), precision=lax.Precision.HIGHEST, preferred_element_type=f32)
    query_dz, smooth, *query_dy, terms = scores_step(outputs[2], proj_weight, units, alive, grad_t)
    board = lax.dot_general(member, smooth, (((0,), (1,)), ((), ())), precision=lax.Precision.HIGHEST, preferred_element_type=f32)
    terms = terms.reshape(groups, 2, half, proj)
    terms = terms[:, 0] + core_other(terms[:, 1])
    doc_grad = lax.psum_scatter(terms, "dp", scatter_dimension=0)
    doc_dz = (inverse * (doc_grad - doc_units * jnp.sum(doc_grad * doc_units, axis=-1, keepdims=True))).astype(bf16)
    doc_dy = dot(doc_dz, proj_weight, contract_cols)
    proj_grad = dot(doc_y, doc_dz, contract_rows) + dot(query_y, query_dz, contract_rows)
    own = (query_dy, (doc_dy[: half // 2], doc_dy[half // 2 :]), [jnp.zeros((half // 2, model), f32)] * 2)
    received = [jnp.zeros((half // 2, model), bf16)] * 2
    pairs = {}
    vectors, ub, pb = None, None, None
    input_grads = [None, None]
    ready = {}
    chunk_counts = (4, 4, 1, 3)
    order = [(place, i) for place in range(4) for i in range(chunk_counts[place])]
    end = ((lax.axis_index("dp") == 0) | (lax.axis_index("dp") == 3)).astype(jnp.int32).reshape(1, 1)
    line = LineSums(end, [lambda key=key: ready[key[0]][key[1]] for key in order]) if groups == 4 else None
    plain, marks = [], []
    board = board + core_other(board)
    mid = model // 2
    lower = core == 0
    proj_half = jnp.where(lower, proj_grad[:mid], proj_grad[mid:])
    proj_half = proj_half + core_other(jnp.where(lower, proj_grad[mid:], proj_grad[:mid]))

    for step in range(3):
        pace["now"] = LATE if step == 2 else EARLY

        def hook(stage, value, step=step):
            if stage == "step":
                return line.step((value,)) if line is not None and step == 2 else ()
            if stage == "end":
                if line is None or step < 2:
                    return ()
                for _ in range(4):
                    line.step()
                return line.last
            pairs[step, stage] = value
            if step < 2:
                return ()
            lefts = kept[2][stage] + kept[1][stage] + kept[0][stage]
            rights = pairs[0, stage] + pairs[1, stage] + value
            if stage == 3:
                lefts, rights = rights, lefts
            ready[stage] = weight_step(lefts, rights, chunk_counts[stage])
            if line is not None and stage == 0:
                line.start()
            if line is None:
                plain.append(lax.psum(jnp.concatenate(ready[stage]), "dp").astype(f32))
            return (ready[stage][0],)

        dh, vec, ub_now, pb_now, marks_now = backward(flag, received, own[step], w, *contexts[2 - step], records[2 - step], hook, step == 2)
        marks.append(marks_now)
        vectors = vec if vectors is None else vectors + vec
        ub = ub_now if ub is None else ub + ub_now
        pb = pb_now if pb is None else pb + pb_now
        if step < 2:
            received = [to_section(low, [(1, 0)]) for _, low in dh]
        if step >= 1:
            input_grads[2 - step] = lax.dynamic_slice_in_dim(jnp.concatenate([x for x, _ in dh]), chip * share, share, 0)

    if line is not None:
        results = line.finish()
        parts, at = [], 0
        for n in chunk_counts:
            parts.append(results[at : at + n])
            at += n
        spread = [jnp.concatenate(p, axis=0) for p in parts[:3]]
        d_qkv = jnp.stack([p.T for p in parts[3]], axis=1)
    else:
        spread = plain[:3]
        d_qkv = plain[3].T.reshape(model, 3, width)
    d_down, d_up, d_out = spread
    units_count = up_weight.shape[-1]
    small = jnp.concatenate([vectors.reshape(6, model)], axis=0)
    small = small + core_other(small)
    ub = ub[:, :units_count] + core_other(ub[:, units_count:])
    pb = pb[:, :wide] + core_other(pb[:, wide:])
    vector = jnp.concatenate([ub[0], pb[0], small.reshape(-1)]).reshape(-1, LANES)
    vector = dp_sum_after(vector, [line.seen[10], line.seen[12]] if line is not None else [()]).reshape(-1)
    proj_half = dp_sum_after(proj_half, [(marks[1][1],), (marks[2][0],)])
    proj_there = core_other(proj_half)
    sent_proj = to_section(jnp.where(lower, proj_half, proj_there), [(1, 0)])
    proj_out = jnp.where(first, sent_proj, jnp.where(lower, proj_there, proj_half))
    ub = vector[:units_count][None]
    pb = vector[units_count : units_count + wide]
    small = vector[units_count + wide :].reshape(6, model)
    stack = jnp.stack(input_grads)
    swap = [(0, 1), (1, 0)]
    docs = groups // 2
    sent_input = to_section(stack[:, :, mid:], swap)
    sent_board = to_section(board[:, :docs], swap)
    return (
        jnp.where(first, sent_board, board[:, docs:]),
        jnp.where(first, stack[:, :, :mid], sent_input),
        d_qkv[None],
        pb.reshape(1, 3, width),
        d_out[None],
        d_up[None],
        ub,
        d_down[None],
        small[0:2][None],
        small[2:4][None],
        small[4:6][None],
        proj_out,
    )


def solution(mesh):
    return jax.shard_map(
        on_device,
        mesh=mesh,
        in_specs=(
            P("dp", "tensor", None),
            P("dp", None),
            P("dp", None),
            P("section", None, None, "tensor"),
            P("section", None, "tensor"),
            P("section", "tensor", None),
            P("section", None, "tensor"),
            P("section", "tensor"),
            P("section", "tensor", None),
            P("section", None, None),
            P("section", None, None),
            P("section", None, None),
            P(),
        ),
        out_specs=(
            P("dp", "section"),
            P("dp", "tensor", "section"),
            P("section", None, None, "tensor"),
            P("section", None, "tensor"),
            P("section", "tensor", None),
            P("section", None, "tensor"),
            P("section", "tensor"),
            P("section", "tensor", None),
            P("section", None, None),
            P("section", None, None),
            P("section", None, None),
            P("section", None),
        ),
        check_vma=False,
    )
```

```python
import functools

import jax
import jax.numpy as jnp
import numpy as np
from jax import lax
from jax.experimental import pallas as pl
from jax.experimental.pallas import tpu as pltpu
from jax.sharding import PartitionSpec as P

HD = 64
QLEN = 32
LANES = 128

norm_eps = 1e-05
unit_eps = 1e-06
softness_factor = 0.0625
rope_base = 10000.0
hidden_score = -1000000000.0
contract_rows = (((0,), (0,)), ((), ()))
contract_cols = (((1,), (1,)), ((), ()))
contract_inner = (((1,), (0,)), ((), ()))
bf16 = jnp.bfloat16
f32 = jnp.float32


def dot(left, right, contraction=contract_inner):
    return lax.dot_general(left, right, contraction, preferred_element_type=f32)


def flip(value, bit):
    count = lax.axis_size("tensor")
    return lax.ppermute(value, "tensor", [(i, i ^ (1 << bit)) for i in range(count)])


def chip_bits():
    return range(1, lax.axis_size("tensor").bit_length() - 1)


def core_other(value):
    return flip(value, 0)


def chips_gather(value, chip):
    for bit in chip_bits():
        other = flip(value, bit)
        upper = (chip >> (bit - 1)) % 2 == 1
        value = jnp.concatenate([jnp.where(upper, other, value), jnp.where(upper, value, other)], axis=0)
    return value


def chips_other(low):
    bits = list(chip_bits())
    if not bits:
        return low, jnp.zeros_like(low)
    for bit in bits[:-1]:
        low = (low.astype(f32) + flip(low, bit).astype(f32)).astype(bf16)
    return low, flip(low, bits[-1])


def to_section(value, pairs):
    return lax.ppermute(value, "section", pairs)


def join_kernel(upper, mine, other, out):
    size = mine.shape[0]
    first = upper[0, 0] == 1
    out[:size, :] = jnp.where(first, other[...], mine[...])
    out[size:, :] = jnp.where(first, mine[...], other[...])


def dp_gather(value, marks):
    count = lax.axis_size("dp")
    me = lax.axis_index("dp")
    step = 1
    while step < count:
        other = lax.ppermute(value, "dp", [(i, i ^ step) for i in range(count)])
        upper = ((me // step) % 2).astype(jnp.int32).reshape(1, 1)
        outs = [((2 * value.shape[0], value.shape[1]), value.dtype)]
        value = call(join_kernel, [upper, value, other], outs, us=1, after=marks[0], smem=(0,))[0]
        marks = marks[1:] or marks
        step *= 2
    return value


def dp_sum(value):
    count = lax.axis_size("dp")
    step = 1
    while step < count:
        value = value + lax.ppermute(value, "dp", [(i, i ^ step) for i in range(count)])
        step *= 2
    return value


def slot_kernel(*refs, own, across, next_own, result):
    refs = list(refs)
    end = refs.pop(0)[0, 0] == 1
    take = lambda wanted: refs.pop(0)[...] if wanted else None
    chunk, arrived = take(own), take(own or result)
    side, over = take(across), take(across)
    following = take(next_own)
    finished = take(result)
    total = (side.astype(f32) + over.astype(f32)).astype(bf16) if across else None
    if own:
        refs.pop(0)[...] = (chunk.astype(f32) + arrived.astype(f32)).astype(bf16)
    if across or next_own:
        if not across:
            onward = following
        elif not next_own:
            onward = total
        else:
            onward = jnp.where(end, following, total)
        refs.pop(0)[...] = onward
    if across:
        refs.pop(0)[...] = total
    if result:
        refs.pop(0)[...] = jnp.where(end, arrived, finished).astype(f32)


class LineSum:

    def __init__(self, end, chunks, there):
        self.end, self.chunks, self.count, self.there = end, chunks, len(chunks), there
        self.k, self.side, self.over, self.total, self.results = 0, None, None, None, []
        self.arrived = []

    def outer(self, value):
        self.arrived.append(lax.ppermute(value, "dp", [(0, 1), (1, 0), (2, 3), (3, 2)]))

    def start(self):
        self.outer(self.chunks[0]())
        self.outer(self.chunks[1]())

    def step(self, after=()):
        k, n = self.k, self.count
        own, across, next_own, result = k < n, 1 <= k <= n, 1 <= k < n - 1, k >= 2
        arrived = self.arrived.pop(0)
        chunk = self.chunks[k]() if own else None
        following = self.chunks[k + 1]() if next_own else None
        ins = [self.end]
        ins += [chunk] if own else []
        ins += [arrived] if own or result else []
        ins += [self.side, self.over] if across else []
        ins += [following] if next_own else []
        ins += [self.total] if result else []
        shape = arrived.shape
        outs = [(shape, bf16)] * (own + (across or next_own) + across) + [(shape, f32)] * result
        got = list(
            call(functools.partial(slot_kernel, own=own, across=across, next_own=next_own, result=result), ins, outs, us=2 * SLOT, after=after, smem=(0,))
        )
        side = got.pop(0) if own else None
        onward = got.pop(0) if across or next_own else None
        self.total = got.pop(0) if across else None
        if result:
            self.results.append(got.pop(0))
        self.side = side
        if own:
            self.over = lax.ppermute(side, "dp", [(1, 2), (2, 1)])
        if onward is not None:
            self.outer(onward)
        self.k += 1
        return (side if own else onward if onward is not None else self.results[-1],)

    def busy(self):
        return self.k <= self.count + 1

    def can_step(self):
        return self.busy() and not (1 <= self.k < self.count - 1 and not self.there(self.k + 1))


class LineSums:

    def __init__(self, end, ready, keys):
        lines = [keys[i::2] for i in range(2)]
        self.lines = [
            LineSum(end, [lambda key=key: ready[key[0]][key[1]] for key in line], lambda k, line=line: line[k][0] in ready) for line in lines
        ]
        self.last, self.turn, self.seen = (), 0, []

    def start(self):
        for line in self.lines:
            line.start()

    def step(self, after=()):
        line = self.lines[self.turn]
        if line.busy() and not line.can_step():
            return self.last
        self.turn = 1 - self.turn
        if line.busy():
            self.last = line.step(tuple(after) + self.last)
            self.seen.append(self.last)
        return self.last

    def finish(self):
        while any(line.busy() for line in self.lines):
            self.step()
        results = [None] * sum(line.count for line in self.lines)
        for i, line in enumerate(self.lines):
            results[i::2] = line.results
        return results


def rope_tables(positions):
    half = HD // 2
    frequency = np.power(np.float32(rope_base), (-2.0 * np.arange(half) / HD).astype(np.float32)).astype(np.float32)
    angles = (positions.astype(np.float32)[:, None] * frequency[None, :]).astype(np.float32)
    cosine, sine = np.cos(angles), np.sin(angles)
    head = (np.concatenate([cosine, cosine], 1), np.concatenate([-sine, sine], 1))
    return tuple(np.tile(part, (1, LANES // HD)).astype(np.float32) for part in head)


VMEM = pl.BlockSpec(memory_space=pltpu.VMEM)
ANY = pl.BlockSpec(memory_space=pl.ANY)
SMEM = pl.BlockSpec(memory_space=pltpu.SMEM)


pace = {"now": 1.0}
EARLY, LATE = 1.2, 0.12
SLOT = 1.0
LINED = (0, 1, 3, 2)


def cost(us):
    us = us * pace["now"]
    return pl.CostEstimate(flops=int(us * 1.1e9), bytes_accessed=int(us * 1e6), transcendentals=0)


def held(x):
    return pltpu.with_memory_space_constraint(x, pltpu.HBM)


def call(kernel, ins, outs, us, scratch=(), after=(), smem=(), keep=(), limit=16):
    n = len(ins)

    def body(*refs):
        kernel(*refs[:n], *refs[n + len(after) :])

    return pl.pallas_call(
        body,
        in_specs=[SMEM if i in smem else VMEM for i in range(n)] + [ANY] * len(after),
        out_specs=[VMEM] * len(outs),
        out_shape=[pltpu.HBM(*out) if i in keep else jax.ShapeDtypeStruct(*out) for i, out in enumerate(outs)],
        scratch_shapes=list(scratch),
        compiler_params=pltpu.CompilerParams(vmem_limit_bytes=limit * 1024 * 1024),
        cost_estimate=cost(us),
        name=getattr(kernel, "func", kernel).__name__,
    )(*ins, *after)


def load_kernel(own, oth, out, sem, axis):
    size = own.shape[axis]
    places = [out.at[:, :size], out.at[:, size:]] if axis else [out.at[:size], out.at[size:]]
    copies = [pltpu.make_async_copy(x, place, sem.at[i]) for i, (x, place) in enumerate(zip((own, oth), places))]
    for copy in copies:
        copy.start()
    for copy in copies:
        copy.wait()


def chip_weight(own, axis):
    other = core_other(own)
    shape = tuple(2 * n if i == axis else n for i, n in enumerate(own.shape))
    return pl.pallas_call(
        functools.partial(load_kernel, axis=axis),
        in_specs=[ANY, ANY],
        out_specs=VMEM,
        out_shape=pltpu.VMEM(shape, own.dtype),
        cost_estimate=cost(2),
        scratch_shapes=[pltpu.SemaphoreType.DMA((2,))],
        compiler_params=pltpu.CompilerParams(vmem_limit_bytes=16 * 1024 * 1024),
    )(own, other)


def half_rows(ref, c):
    size = ref.shape[0] // 2
    return ref[c * size : (c + 1) * size, :]


def half_lanes(ref, c):
    size = ref.shape[1] // 2
    return ref[:, c * size : (c + 1) * size]


def merge(out, before, value):
    size = value.shape[0]
    out[:size, :] = before[...]
    out[size:, :] = value


def swap_halves(tile):
    lane = lax.broadcasted_iota(jnp.int32, tile.shape, 1)
    return jnp.where(lane % HD < HD // 2, pltpu.roll(tile, LANES - HD // 2, 1), pltpu.roll(tile, HD // 2, 1))


def qkv_kernel(flag, entering, received, w, b, cos, sin, h_ref, q_ref, kv_ref):
    h = jnp.where(flag[0, 0] == 1, entering[...], received[...])
    h_ref[...] = h
    width = w.shape[1] // 6
    c, s = cos[...], sin[...]
    for place in range(2):
        at = slice(place * 3 * width, (place + 1) * 3 * width)
        p = dot(h, w[:, at]) + b[:, at]
        for t in range(0, width, LANES):
            at = slice(place * width + t, place * width + t + LANES)
            tile = p[:, t : t + LANES]
            q_ref[:, at] = (tile * c + swap_halves(tile) * s).astype(bf16)
            tile = p[:, width + t : width + t + LANES]
            kv_ref[:, at] = (tile * c + swap_halves(tile) * s).astype(bf16)
        kv_ref[:, 2 * width + place * width : 2 * width + (place + 1) * width] = p[:, 2 * width :].astype(bf16)


def qkv_step(flag, entering, received, w, tables, after=()):
    rows, model = entering.shape
    features = w["qkv"].shape[1] // 3
    return call(
        qkv_kernel,
        [flag, entering, received, w["qkv"], w["qkv_b"], *tables],
        [((rows, model), bf16), ((rows, features), bf16), ((rows, 2 * features), bf16)],
        after=after,
        smem=(0,),
        keep=(0, 1, 2),
        us=2,
    )


def head_rows(tile, place):
    row = lax.broadcasted_iota(jnp.int32, tile.shape, 0)
    return jnp.where(row // HD == place, tile, 0.0).astype(bf16)


def head_lanes(tile, place):
    lane = lax.broadcasted_iota(jnp.int32, tile.shape, 1)
    return jnp.where(lane // HD == place, tile, 0.0).astype(bf16)


def tile_at(j, features, base=0):
    return slice(base + j * LANES, base + (j + 1) * LANES)


def partner_tile(j, features):
    tiles = features // LANES
    return (j + tiles // 2) % tiles


def partner_base(j, features, base=0):
    return tile_at(partner_tile(j, features), features, base)


def attend_kernel(*refs, c):
    q_ref, kv_own, kv_oth, bias_ref, w = refs[:5]
    if c:
        o_before, v_t, refs = refs[5], refs[6], refs[7:]
        o_own, o_oth, lse_ref, low_ref, o_t, s_all = refs
    else:
        o_first, k_t, v_t, lse_ref, low_ref, o_t, s_all = refs[5:]
    features = q_ref.shape[1]
    rows = kv_own.shape[0]
    some = rows // 2
    q_half = half_rows(q_ref, c)
    for j in range(features // LANES):
        at = tile_at(j, features)
        q_t = q_half[:, at].astype(f32).T * HD ** (-0.5)
        k_here, k_there = kv_own[:, at], kv_oth[:, partner_base(j, features)]
        for place in range(2):
            q_one = head_rows(q_t, place)
            s_all[2 * j + place, :rows, :] = dot(k_here, q_one)
            s_all[2 * j + place, rows:, :] = dot(k_there, q_one)
        if not c:
            v_here, v_there = kv_own[:, tile_at(j, features, features)], kv_oth[:, partner_base(j, features, features)]
            v_t[at, :rows] = v_here.astype(f32).T.astype(bf16)
            v_t[at, rows:] = v_there.astype(f32).T.astype(bf16)
            k_t[at, :rows] = k_here.astype(f32).T.astype(bf16)
            k_t[at, rows:] = k_there.astype(f32).T.astype(bf16)
    bias = bias_ref[:, c * some : (c + 1) * some].astype(f32)
    for h in range(features // HD):
        s = s_all[h] + bias
        peak = jnp.max(s, axis=0, keepdims=True)
        e = jnp.exp(s - peak)
        total = jnp.sum(e, axis=0, keepdims=True)
        s_all[h] = e * (1.0 / total)
        lse_ref[h : h + 1, :] = peak + jnp.log(total)
    for h in range(features // HD):
        o_t[h * HD : (h + 1) * HD, :] = dot(v_t[h * HD : (h + 1) * HD, :], s_all[h].astype(bf16))
    o = o_t[...].T.astype(bf16)
    half = features // 2
    if c:
        merge(o_own, o_before[:, :half], o[:, :half])
        merge(o_oth, o_before[:, half:], o[:, half:])
    else:
        o_first[...] = o
    low_ref[...] = dot(o, w[...]).astype(bf16)


def attend_step(c, q, kv, kv_other, bias, w, before=(), after=()):
    rows, features = q.shape
    model = w["out"].shape[1]
    some = rows // 2
    heads = features // HD
    if c:
        kept = [((rows, features // 2), bf16)] * 2
    else:
        kept = [((some, features), bf16), ((features, 2 * rows), bf16), ((features, 2 * rows), bf16)]
    return call(
        functools.partial(attend_kernel, c=c),
        [q, kv, kv_other, bias, w["out"], *before],
        kept + [((heads, some), f32), ((some, model), bf16)],
        scratch=[pltpu.VMEM((features, some), f32), pltpu.VMEM((heads, 2 * rows, some), f32)],
        after=after,
        keep=(0, 1, 2) if c else (1, 3),
        us=4,
    )


def normed(values):
    centred = values - jnp.mean(values, axis=-1, keepdims=True)
    inverse = lax.rsqrt(jnp.mean(centred * centred, axis=-1, keepdims=True) + norm_eps)
    return centred * inverse, inverse


def norm_back(gradient, n, inverse):
    return inverse * (gradient - jnp.mean(gradient, axis=-1, keepdims=True) - n * jnp.mean(gradient * n, axis=-1, keepdims=True))


def feed_kernel(*refs, c):
    h, low, recv, vec, up, b, down = refs[:7]
    before, refs = (refs[7:10], refs[10:]) if c else (None, refs[7:])
    n_ref, r_ref, sl_ref, low_ref, g_own, rest = refs
    s1 = half_rows(h, c).astype(f32) + (low[...].astype(f32) + recv[...].astype(f32)) + vec[0:1, :]
    n, r = normed(s1)
    n_ref[...] = n
    r_ref[...] = r
    h1 = (n * vec[1:2, :] + vec[2:3, :]).astype(bf16)
    u = dot(h1, up[...]) + b[...]
    phi = 0.5 * (1.0 + lax.erf(u * 0.7071067811865476))
    g = (u * phi).astype(bf16)
    sl_ref[...] = (phi + u * jnp.exp(-0.5 * u * u) * 0.3989422804014327).astype(bf16)
    low_ref[...] = dot(g, down[...]).astype(bf16)
    units = up.shape[1] // 2
    some, model = h1.shape
    if c:
        g_before, rest_before, o_oth = before
        merge(g_own, g_before, g[:, :units])
        rest[:some, :model] = rest_before[:, :model]
        rest[some:, :model] = h1
        rest[:, model : 2 * model] = h[...]
        rest[:some, 2 * model : 2 * model + units] = rest_before[:, model:]
        rest[some:, 2 * model : 2 * model + units] = g[:, units:]
        rest[:, 2 * model + units :] = o_oth[...]
    else:
        g_own[...] = g[:, :units]
        rest[:, :model] = h1
        rest[:, model:] = g[:, units:]


def feed_step(c, h, low, recv, vec, w, before=(), after=()):
    rows, model = h.shape
    units = w["up"].shape[1] // 2
    some = rows // 2
    if c:
        kept = [((rows, units), bf16), ((rows, 2 * model + units + before[-1].shape[1]), bf16)]
    else:
        kept = [((some, units), bf16), ((some, model + units), bf16)]
    return call(
        functools.partial(feed_kernel, c=c),
        [h, low, recv, vec, w["up"], w["up_b"], w["down"], *before],
        [((some, model), f32), ((some, 1), f32), ((some, 2 * units), bf16), ((some, model), bf16)] + kept,
        after=after,
        keep=(0, 1, 2, 4, 5) if c else (0, 1, 2),
        us=4,
    )


def output_kernel(*refs, c):
    n1, low, recv, vec = refs[:4]
    before, (n_ref, r_ref, y_ref) = (refs[4], refs[5:]) if c else (None, refs[4:])
    s2 = n1[...] * vec[0:1, :] + vec[1:2, :] + (low[...].astype(f32) + recv[...].astype(f32)) + vec[2:3, :]
    n, r = normed(s2)
    n_ref[...] = n
    r_ref[...] = r
    y = (n * vec[3:4, :] + vec[4:5, :]).astype(bf16)
    if c:
        merge(y_ref, before, y)
    else:
        y_ref[...] = y


def output_step(c, n1, low, recv, vec, before=()):
    some, model = n1.shape
    return call(
        functools.partial(output_kernel, c=c),
        [n1, low, recv, vec, *before],
        [((some, model), f32), ((some, 1), f32), ((2 * some if c else some, model), bf16)],
        keep=(0, 1),
        us=2.3,
    )


def feed_back_head(dy, n, r, gain, ds_ref, vec_ref):
    ds = norm_back(dy * gain, n, r)
    ds_ref[...] = ds
    vec_ref[0:1, :] = jnp.sum(ds, axis=0, keepdims=True)
    vec_ref[1:2, :] = jnp.sum(dy * n, axis=0, keepdims=True)
    vec_ref[2:3, :] = jnp.sum(dy, axis=0, keepdims=True)
    return ds.astype(bf16)


def feed_back_tail(f, up, down, sl, low_ref, ub_ref):
    du = dot(f, down[...], contract_cols) * sl[...].astype(f32)
    ub_ref[...] = jnp.sum(du, axis=0, keepdims=True)
    u = du.astype(bf16)
    low_ref[...] = dot(u, up[...], contract_cols).astype(bf16)
    return u


def feed_back_kernel(*refs, c):
    flag, received, own, n2, r2, gain, up, down, sl = refs[:9]
    before, refs = (refs[9:11], refs[11:]) if c else (None, refs[9:])
    ds_ref, low_ref, vec_ref, ub_ref, u_own, rest = refs
    dy = jnp.where(flag[0, 0] == 1, received[...].astype(f32), own[...])
    f = feed_back_head(dy, n2[...], r2[...], gain[...], ds_ref, vec_ref)
    u = feed_back_tail(f, up, down, sl, low_ref, ub_ref)
    units = up.shape[1] // 2
    some, model = f.shape
    if c:
        merge(u_own, before[0], u[:, :units])
        rest[:some, :] = before[1][...]
        rest[some:, :model] = f
        rest[some:, model:] = u[:, units:]
    else:
        u_own[...] = u[:, :units]
        rest[:, :model] = f
        rest[:, model:] = u[:, units:]


def feed_back_step(c, flag, received, own, n2, r2, gain, w, sl, before=(), after=()):
    some, model = n2.shape
    units = w["up"].shape[1] // 2
    kept = 2 * some if c else some
    return call(
        functools.partial(feed_back_kernel, c=c),
        [flag, received, own, n2, r2, gain, w["up"], w["down"], sl, *before],
        [
            ((some, model), f32), ((some, model), bf16), ((3, model), f32), ((1, 2 * units), f32),
            ((kept, units), bf16), ((kept, model + units), bf16),
        ],
        after=after,
        smem=(0,),
        keep=(0, 2, 3, 4, 5) if c else (0, 2, 3),
        us=5.5,
    )


def first_kernel(rec_a, rec_b, n_a, n_b, r_a, r_b, gain, ds_a, ds_b, vec_a, vec_b, f_ref):
    some = n_a.shape[0]
    f_ref[:some, :] = feed_back_head(rec_a[...].astype(f32), n_a[...], r_a[...], gain[...], ds_a, vec_a)
    f_ref[some:, :] = feed_back_head(rec_b[...].astype(f32), n_b[...], r_b[...], gain[...], ds_b, vec_b)


def first_step(received, n2, r2, gain, after=()):
    some, model = n2[0].shape
    return call(
        first_kernel,
        [*received, *n2, *r2, gain],
        [((some, model), f32)] * 2 + [((3, model), f32)] * 2 + [((2 * some, model), bf16)],
        after=after,
        keep=(0, 1, 2, 3),
        us=2.5,
    )


def second_kernel(*refs, c):
    f, up, down, sl = refs[:4]
    before, refs = (refs[4:6], refs[6:]) if c else (None, refs[4:])
    low_ref, ub_ref, u_own, u_oth = refs
    u = feed_back_tail(half_rows(f, c), up, down, sl, low_ref, ub_ref)
    units = up.shape[1] // 2
    for place, value in enumerate((u[:, :units], u[:, units:])):
        out = (u_own, u_oth)[place]
        if c:
            merge(out, before[place], value)
        else:
            out[...] = value


def second_step(c, f, w, sl, before=(), after=()):
    rows, model = f.shape
    units = w["up"].shape[1] // 2
    kept = rows if c else rows // 2
    return call(
        functools.partial(second_kernel, c=c),
        [f, w["up"], w["down"], sl, *before],
        [((rows // 2, model), bf16), ((1, 2 * units), f32), ((kept, units), bf16), ((kept, units), bf16)],
        after=after,
        keep=(1, 2, 3) if c else (1,),
        us=4.5,
    )


def attend_back_kernel(*refs, c):
    (ds2, low, recv, n1, r1, gain, w, q_ref, kv_own, kv_oth, k_t, bias_ref, lse_ref), refs = refs[:13], refs[13:]
    if c:
        (own_before, oth_before, out_before), refs = refs[:3], refs[3:]
    ds_ref, dq_ref, vec_ref, dkv_ref, dkv_send, out_ref, dq_t, s_all, d_all, a_all, slopes = refs
    features = q_ref.shape[1]
    rows = kv_own.shape[0]
    some = rows // 2
    dh1 = ds2[...] + (low[...].astype(f32) + recv[...].astype(f32))
    n = n1[...]
    ds1 = norm_back(dh1 * gain[...], n, r1[...])
    ds_ref[...] = ds1
    vec_ref[0:1, :] = jnp.sum(ds1, axis=0, keepdims=True)
    vec_ref[1:2, :] = jnp.sum(dh1 * n, axis=0, keepdims=True)
    vec_ref[2:3, :] = jnp.sum(dh1, axis=0, keepdims=True)
    spread = ds1.astype(bf16)
    if c:
        merge(out_ref, out_before, spread)
    else:
        out_ref[...] = spread
    q_half = half_rows(q_ref, c)
    for j in range(features // LANES):
        at = tile_at(j, features)
        q_t = q_half[:, at].astype(f32).T * HD ** (-0.5)
        k_here, k_there = kv_own[:, at], kv_oth[:, partner_base(j, features)]
        for place in range(2):
            q_one = head_rows(q_t, place)
            s_all[2 * j + place, :rows, :] = dot(k_here, q_one)
            s_all[2 * j + place, rows:, :] = dot(k_there, q_one)
    mixed = dot(spread, w[...], contract_cols).astype(bf16).astype(f32)
    for j in range(features // LANES):
        do_t = mixed[:, tile_at(j, features)].T
        v_here, v_there = kv_own[:, tile_at(j, features, features)], kv_oth[:, partner_base(j, features, features)]
        for place in range(2):
            do_one = head_rows(do_t, place)
            d_all[2 * j + place, :rows, :] = dot(v_here, do_one)
            d_all[2 * j + place, rows:, :] = dot(v_there, do_one)
    bias = bias_ref[:, c * some : (c + 1) * some].astype(f32)
    for h in range(features // HD):
        a = jnp.exp(s_all[h] + bias - lse_ref[h : h + 1, :])
        da = d_all[h]
        slope = a * (da - jnp.sum(da * a, axis=0, keepdims=True))
        slopes[h] = slope.astype(bf16) * jnp.asarray(HD ** (-0.5), bf16)
        a_all[h] = a.astype(bf16)
    for h in range(features // HD):
        dq_t[h * HD : (h + 1) * HD, :] = dot(k_t[h * HD : (h + 1) * HD, :], slopes[h])
    for j in range(features // LANES):
        at, v_at = tile_at(j, features), tile_at(j, features, features)
        theirs, v_theirs = partner_base(j, features), partner_base(j, features, features)
        q, do = q_half[:, at].astype(f32), mixed[:, at]
        dk = dot(slopes[2 * j], head_lanes(q, 0)) + dot(slopes[2 * j + 1], head_lanes(q, 1))
        dv = dot(a_all[2 * j], head_lanes(do, 0)) + dot(a_all[2 * j + 1], head_lanes(do, 1))
        if c:
            dkv_ref[:, at] = dk[:rows] + own_before[:, at]
            dkv_ref[:, v_at] = dv[:rows] + own_before[:, v_at]
            dkv_send[:, theirs] = (dk[rows:] + oth_before[:, theirs]).astype(bf16)
            dkv_send[:, v_theirs] = (dv[rows:] + oth_before[:, v_theirs]).astype(bf16)
        else:
            dkv_ref[:, at] = dk[:rows]
            dkv_ref[:, v_at] = dv[:rows]
            dkv_send[:, theirs] = dk[rows:]
            dkv_send[:, v_theirs] = dv[rows:]
    dq_ref[...] = dq_t[...].T


def attend_back_step(c, ds2, low, recv, n1, r1, gain, w, q, kv, kv_other, k_t, bias, lse, before=(), after=()):
    some, model = ds2.shape
    features = q.shape[1]
    rows = 2 * some
    heads = features // HD
    all_heads = (heads, 2 * rows, some)
    return call(
        functools.partial(attend_back_kernel, c=c),
        [ds2, low, recv, n1, r1, gain, w["out"], q, kv, kv_other, k_t, bias, lse, *before],
        [
            ((some, model), f32), ((some, features), f32), ((3, model), f32),
            ((rows, 2 * features), f32), ((rows, 2 * features), bf16 if c else f32), ((rows if c else some, model), bf16),
        ],
        scratch=[
            pltpu.VMEM((features, some), f32), pltpu.VMEM(all_heads, f32), pltpu.VMEM(all_heads, f32), pltpu.VMEM(all_heads, bf16),
            pltpu.VMEM(all_heads, bf16),
        ],
        after=after,
        keep=(0, 1, 2, 3, 5) if c else (0, 1, 2),
        limit=24,
        us=6.5,
    )


def qkv_back_kernel(*refs, c):
    dq, dkv_ref, arrived_ref, cos, sin, w = refs[:6]
    before, refs = (refs[6:9], refs[9:]) if c else (None, refs[6:])
    low_ref, b_ref, p_own, rest = refs
    some, features = dq.shape
    width = features // 2
    cosine, sine = half_rows(cos, c), half_rows(sin, c)
    dkv = half_rows(dkv_ref, c) + half_rows(arrived_ref, c).astype(f32)
    rows_at = slice(some, 2 * some) if c else slice(0, some)
    model = w.shape[0] if c else 0
    total = None
    for place, p_ref in enumerate((p_own, rest)):
        base = place * 3 * width
        start = place * model
        for t in range(0, width, LANES):
            at = slice(place * width + t, place * width + t + LANES)
            v_at = slice(features + place * width + t, features + place * width + t + LANES)
            gq, gk, gv = dq[:, at], dkv[:, at], dkv[:, v_at]
            gq = gq * cosine - swap_halves(gq) * sine
            gk = gk * cosine - swap_halves(gk) * sine
            for part, g in enumerate((gq, gk, gv)):
                to = part * width + t
                p_ref[rows_at, start + to : start + to + LANES] = g.astype(bf16)
                b_ref[0:1, base + to : base + to + LANES] = jnp.sum(g, axis=0, keepdims=True)
        part = dot(p_ref[rows_at, start : start + 3 * width], w[:, base : base + 3 * width], contract_cols)
        total = part if total is None else total + part
    low_ref[...] = total.astype(bf16)
    if c:
        p_own[:some, :] = before[0][...]
        rest[:some, model:] = before[1][...]
        rest[:, :model] = before[2][...]


def qkv_back_step(c, dq, dkv, arrived, tables, w, before=(), after=()):
    some, features = dq.shape
    model, wide = w["qkv"].shape
    kept = [((2 * some, wide // 2), bf16), ((2 * some, model + wide // 2), bf16)] if c else [((some, wide // 2), bf16)] * 2
    return call(
        functools.partial(qkv_back_kernel, c=c),
        [dq, dkv, arrived, *tables, w["qkv"], *before],
        [((some, model), bf16), ((1, wide), f32)] + kept,
        after=after,
        keep=(1, 2, 3) if c else (1,),
        us=3.4,
    )


def end_kernel(ds, low, recv, out, low_out):
    dh = ds[...] + (low[...].astype(f32) + recv[...].astype(f32))
    out[...] = dh
    low_out[...] = dh.astype(bf16)


def end_step(ds, low, recv, after):
    return call(end_kernel, [ds, low, recv], [(ds.shape, f32), (ds.shape, bf16)], us=1.5, after=after)


def part(array, offset, width):
    return array, offset, width


def weight_kernel(*refs, pieces):
    lefts, rights, outs = refs[:pieces], refs[pieces : 2 * pieces], refs[2 * pieces :]
    left = jnp.concatenate([x[...] for x in lefts], axis=0)
    right = jnp.concatenate([x[...] for x in rights], axis=0)
    total = dot(left, right, contract_rows).astype(bf16)
    for i, out in enumerate(outs):

        @pl.when(pl.program_id(0) == i)
        def _(out=out):
            out[...] = total


def weight_step(lefts, rights, steps):
    shape = (lefts[0][2], rights[0][2])
    steps = min(steps, shape[0] // LANES)
    some = (shape[0] // steps, shape[1])
    specs = [pl.BlockSpec((x.shape[0], some[0]), lambda i, at=offset // some[0]: (0, at + i)) for x, offset, _ in lefts]
    specs += [pl.BlockSpec((x.shape[0], width), lambda i, at=offset // width: (0, at)) for x, offset, width in rights]
    return pl.pallas_call(
        functools.partial(weight_kernel, pieces=len(lefts)),
        grid=(steps,),
        in_specs=specs,
        out_specs=[pl.BlockSpec(some, lambda i: (0, 0))] * steps,
        out_shape=[jax.ShapeDtypeStruct(some, bf16)] * steps,
        cost_estimate=cost(6),
        compiler_params=pltpu.CompilerParams(vmem_limit_bytes=24 * 1024 * 1024),
    )(*[held(x) for x, _, _ in (*lefts, *rights)])


def sum_kernel(x, y, out):
    out[...] = x[...] + y[...]


def sum_after(x, y, after):
    return call(sum_kernel, [x, y], [(x.shape, x.dtype)], us=1, after=after)[0]


def dp_sum_after(value, marks):
    count = lax.axis_size("dp")
    step = 1
    while step < count:
        value = sum_after(value, lax.ppermute(value, "dp", [(i, i ^ step) for i in range(count)]), marks[0])
        marks = marks[1:] or marks
        step *= 2
    return value


def embed_kernel(y, proj, alive, units_ref, inverse_ref, payload):
    z = dot(y[...], proj[...])
    inverse = lax.rsqrt(jnp.sum(z * z, axis=-1, keepdims=True) + unit_eps)
    units = z * inverse
    units_ref[...] = units
    inverse_ref[...] = inverse
    width = units.shape[1]
    payload[:, :width] = units.astype(bf16)
    payload[:, width:] = alive[...]


def embed_step(y, proj, alive, after):
    rows, width = alive.shape
    return call(embed_kernel, [y, proj, alive], [((rows, width), f32), ((rows, 1), f32), ((rows, 2 * width), bf16)], us=1.5, after=after)


def scores_kernel(y, proj, docs_own, docs_oth, grad_t, z_ref, m_ref, dy_a, dy_b, terms_own, terms_oth, groups):
    z = dot(y[...], proj[...])
    inverse = lax.rsqrt(jnp.sum(z * z, axis=-1, keepdims=True) + unit_eps)
    e = z * inverse
    e_low = e.astype(bf16)
    e_t = e_low.astype(f32).T.astype(bf16)
    half, width = e.shape
    back = None
    for d in range(groups):
        at = slice(d * half, (d + 1) * half)
        docs = jnp.concatenate([docs_own[at, :width], docs_oth[at, :width]], axis=0)
        alive = jnp.concatenate([docs_own[at, width : width + 1], docs_oth[at, width : width + 1]], axis=0).astype(f32)
        logits = jnp.where(alive > 0, dot(docs, e_t) / softness_factor, hidden_score)
        peak = jnp.max(logits, axis=0, keepdims=True)
        x = jnp.exp(logits - peak)
        total = jnp.sum(x, axis=0, keepdims=True)
        m_ref[d : d + 1, :] = softness_factor * (peak + jnp.log(total))
        pull = (x * (grad_t[d : d + 1, :] / total)).astype(bf16)
        terms = dot(pull, e_low)
        terms_own[at, :] = terms[:half]
        terms_oth[at, :] = terms[half:]
        part = dot(docs.astype(f32).T.astype(bf16), pull)
        back = part if back is None else back + part
    de = back.T
    dz = (inverse * (de - e * jnp.sum(de * e, axis=-1, keepdims=True))).astype(bf16)
    z_ref[...] = dz
    dy = dot(dz, proj[...], contract_cols)
    some = dy_a.shape[0]
    dy_a[...] = dy[:some]
    dy_b[...] = dy[some:]


def scores_step(y, proj, docs_own, docs_oth, grad_t):
    rows, model = y.shape
    groups, width = grad_t.shape[0], proj.shape[1]
    return call(
        functools.partial(scores_kernel, groups=groups),
        [y, proj, docs_own, docs_oth, grad_t],
        [
            ((rows, width), bf16), ((groups, rows), f32), ((rows // 2, model), f32), ((rows // 2, model), f32),
            ((groups * rows, width), f32), ((groups * rows, width), f32),
        ],
        limit=32,
        us=2.6,
    )


def forward(flag, entering, received, w, bias, tables, after=()):
    h, q, kv = qkv_step(flag, entering, received, w, tables, after)
    kv_other = held(core_other(kv))
    h_here, q, kv = held(h), held(q), held(kv)
    o_a, k_t, v_t, lse_a, low_a = attend_step(0, q, kv, kv_other, bias, w)
    sum_a = chips_other(low_a)
    o, o_o, lse_b, low_b = attend_step(1, q, kv, kv_other, bias, w, (o_a, v_t))
    sum_b = chips_other(low_b)
    n1_a, r1_a, sl_a, low_a, *before = feed_step(0, h_here, *sum_a, w["vec_feed"], w)
    sum_a = chips_other(low_a)
    n1_b, r1_b, sl_b, low_b, g, rest = feed_step(1, h_here, *sum_b, w["vec_feed"], w, (*before, held(o_o)))
    sum_b = chips_other(low_b)
    n1_a, n1_b = held(n1_a), held(n1_b)
    n2_a, r2_a, y_a = output_step(0, n1_a, *sum_a, w["vec_out"])
    n2_b, r2_b, y = output_step(1, n1_b, *sum_b, w["vec_out"], (y_a,))
    there = core_other(rest)
    model, units, width = h.shape[1], g.shape[1], o.shape[1]
    kept = (
        (part(g, 0, units), part(there, 2 * model, units)),
        (part(rest, 0, model), part(there, 0, model)),
        (part(o, 0, width), part(there, 2 * model + units, width)),
        (part(rest, model, model), part(there, model, model)),
    )
    a = (held(lse_a), n1_a, held(r1_a), held(sl_a), held(n2_a), held(r2_a))
    b = (held(lse_b), n1_b, held(r1_b), held(sl_b), held(n2_b), held(r2_b))
    return y, ((q, kv, kv_other, held(k_t)), (a, b)), kept, ((o,), (rest,))


def backward(flag, received, own, w, bias, tables, record, hook, last):
    (q, kv, kv_other, k_t), halves = record
    model, units = w["up"].shape[0], w["up"].shape[1] // 2
    parts, vectors, ubs, ds2s, before = [], [], [], [], ()
    after = ()
    if last:
        *ds2s, vec_a, vec_b, f = first_step(received, [x[4] for x in halves], [x[5] for x in halves], w["gain"][1:2])
        ds2s, vectors = [held(x) for x in ds2s], [vec_a, vec_b]
        after = hook(0, (part(f, 0, model), part(core_other(f), 0, model)))
        for c in range(2):
            low, ub, *before = second_step(c, f, w, halves[c][3], before, after)
            parts.append(chips_other(low))
            ubs.append(ub)
            after = ()
        hook("step", low)
        u, u_o = before
        after = hook(1, (part(u, 0, units), part(core_other(u_o), 0, units)))
        after = hook("step", after[0])
    else:
        for c in range(2):
            lse, n1, r1, sl, n2, r2 = halves[c]
            ds2, low, vec, ub, *before = feed_back_step(c, flag, received[c], own[c], n2, r2, w["gain"][1:2], w, sl, before)
            ds2s.append(held(ds2))
            parts.append(chips_other(low))
            vectors.append(vec)
            ubs.append(ub)
        u, rest = before
        there = core_other(rest)
        hook(0, (part(rest, 0, model), part(there, 0, model)))
        hook(1, (part(u, 0, units), part(there, model, units)))
    before, vectors_1, ds1s, dqs = (), [], [], []
    for c in range(2):
        lse, n1, r1, sl, n2, r2 = halves[c]
        ds1, dq, vec, dkv, send, out = attend_back_step(
            c, ds2s[c], *parts[c], n1, r1, w["gain"][0:1], w, q, kv, kv_other, k_t, bias, lse, before, after
        )
        before = (dkv, send, out) if c == 0 else ()
        ds1s.append(ds1)
        dqs.append(held(dq))
        vectors_1.append(vec)
        after = hook("step", dq)
    arrived, dkv = held(core_other(send)), held(dkv)
    nexts, pbs, before = [], [], ()
    for c in range(2):
        low, pb, *before = qkv_back_step(c, dqs[c], dkv, arrived, tables, w, (*before, held(out)) if c else (), after)
        nexts.append(chips_other(low))
        pbs.append(pb)
        after = hook("step", pb)
    p, rest = before
    there = core_other(rest)
    wide = p.shape[1]
    hook(2, (part(rest, 0, model), part(there, 0, model)))
    hook(3, (part(p, 0, wide), part(there, model, wide)))
    after = hook("end", None)
    dh, dh_low = [], []
    for c in range(2):
        out_c, low = end_step(held(ds1s[c]), *nexts[c], after)
        dh.append(out_c)
        dh_low.append(low)
        after = (low,)
    vectors = jnp.stack([vectors_1[0] + vectors_1[1], vectors[0] + vectors[1]], axis=1)
    return dh, dh_low, vectors, ubs[0] + ubs[1], pbs[0] + pbs[1], (parts[1][0], nexts[1][0])


def on_device(tokens, segment, score_grad, qkv_weight, qkv_bias, out_weight, up_weight, up_bias, down_weight, out_bias, norm_gain, norm_shift, proj_weight):
    blocks, share, model = tokens.shape
    pace["now"] = EARLY
    wide = 3 * qkv_weight.shape[-1]
    width = wide // 3
    gain, shift, bias = norm_gain[0].astype(f32), norm_shift[0].astype(f32), out_bias[0].astype(f32)
    first = lax.axis_index("section") == 0
    flag = first.astype(jnp.int32).reshape(1, 1)
    device = lax.axis_index("tensor")
    core, chip = device % 2, device // 2
    chips = lax.axis_size("tensor") // 2
    groups = lax.axis_size("dp")
    half = share * chips
    rows = 2 * half
    proj = proj_weight.shape[1]
    entering = [chips_gather(tokens[b], chip) for b in range(2)]

    def both(own):
        return jnp.concatenate([own, core_other(own)], axis=1)

    w = dict(
        qkv=chip_weight(qkv_weight[0].reshape(model, wide), 1), qkv_b=both(qkv_bias[0].reshape(1, wide).astype(f32)),
        out=chip_weight(out_weight[0], 0), up=chip_weight(up_weight[0], 1), up_b=both(up_bias.astype(f32)),
        down=chip_weight(down_weight[0], 0), gain=gain,
        vec_feed=jnp.stack([bias[0], gain[0], shift[0]]),
        vec_out=jnp.stack([gain[0], shift[0], bias[1], gain[1], shift[1]]),
    )

    def own_first(by_token):
        parts = by_token.reshape((chips, 2, share) + by_token.shape[1:])
        even = parts[:, 0].reshape((half,) + by_token.shape[1:])
        odd = parts[:, 1].reshape((half,) + by_token.shape[1:])
        return jnp.concatenate([jnp.where(core == 0, even, odd), jnp.where(core == 0, odd, even)], axis=0)

    index = np.arange(rows)
    tables = [tuple(own_first(jnp.asarray(part))[:half] for part in rope_tables(p)) for p in (index, index % QLEN)]
    segments = [own_first(segment[b]) for b in range(2)]

    def pick(zero, one):
        ids = jnp.where(first, segments[zero], segments[one])
        bias = jnp.where(ids[:, None] == ids[None, :half], 0.0, hidden_score).astype(bf16)
        return held(bias), tuple(jnp.where(first, x, y) for x, y in zip(tables[zero], tables[one]))

    contexts = [pick(0, 0), pick(1, 0), pick(1, 1)]
    received = jnp.zeros((half, model), bf16)
    records, kept, outputs = [], [], []
    alive_here = jnp.broadcast_to((segments[0][:half] == 0).astype(bf16)[:, None], (half, proj))
    slots = score_grad.shape[0]
    member = (segments[1][:half, None] == jnp.arange(slots)[None, :]).astype(f32)
    grad_t = lax.dot_general(score_grad, member, (((0,), (1,)), ((), ())), precision=lax.Precision.HIGHEST, preferred_element_type=f32)
    prelude = [w["vec_feed"], w["vec_out"], w["up_b"], alive_here, grad_t]
    prelude += [x for bias_of, tables_of in contexts for x in (bias_of, *tables_of)]
    for tick in range(3):
        y, record, keep, marks_2 = forward(flag, entering[min(tick, 1)], received, w, *contexts[tick], prelude if tick == 0 else ())
        records.append(record)
        kept.append(keep)
        outputs.append(y)
        if tick == 2:
            break
        received = to_section(y, [(0, 1)])

    doc_y, query_y = outputs[1], outputs[2]
    doc_units, inverse, payload = embed_step(doc_y, proj_weight, alive_here, (records[2][0][0],))
    docs_own = dp_gather(payload, marks_2)
    docs_oth = core_other(docs_own)
    query_dz, smooth, *query_dy, terms, terms_there = scores_step(query_y, proj_weight, docs_own, docs_oth, grad_t)
    board = lax.dot_general(member, smooth, (((0,), (1,)), ((), ())), precision=lax.Precision.HIGHEST, preferred_element_type=f32)
    terms = (terms + core_other(terms_there)).reshape(groups, half, proj)
    doc_grad = lax.psum_scatter(terms, "dp", scatter_dimension=0)
    doc_dz = (inverse * (doc_grad - doc_units * jnp.sum(doc_grad * doc_units, axis=-1, keepdims=True))).astype(bf16)
    doc_dy = dot(doc_dz, proj_weight, contract_cols)
    proj_grad = dot(doc_y, doc_dz, contract_rows) + dot(query_y, query_dz, contract_rows)
    own = (query_dy, (doc_dy[: half // 2], doc_dy[half // 2 :]), [jnp.zeros((half // 2, model), f32)] * 2)
    received = [jnp.zeros((half // 2, model), bf16)] * 2
    pairs = {}
    vectors, ub, pb = None, None, None
    input_grads = [None, None]
    ready = {}
    chunk_counts = (4, 4, 1, 3)
    order = [(place, i) for place in LINED for i in range(chunk_counts[place])]
    end = ((lax.axis_index("dp") == 0) | (lax.axis_index("dp") == 3)).astype(jnp.int32).reshape(1, 1)
    line = LineSums(end, ready, order) if groups == 4 else None
    plain, marks = {}, []
    board = board + core_other(board)
    mid = model // 2
    lower = core == 0
    proj_half = jnp.where(lower, proj_grad[:mid], proj_grad[mid:])
    proj_half = proj_half + core_other(jnp.where(lower, proj_grad[mid:], proj_grad[:mid]))

    for step in range(3):
        pace["now"] = LATE if step == 2 else EARLY

        def hook(stage, value, step=step):
            if stage == "step":
                return line.step((value,)) if line is not None and step == 2 else ()
            if stage == "end":
                if line is None or step < 2:
                    return ()
                for _ in range(4 if len(LINED) == 4 else 2):
                    line.step()
                return line.last
            pairs[step, stage] = value
            if step < 2:
                return ()
            lefts = kept[2][stage] + kept[1][stage] + kept[0][stage]
            rights = pairs[0, stage] + pairs[1, stage] + value
            if stage == 3:
                lefts, rights = rights, lefts
            if stage == 0:
                size = lefts[0][2] // chunk_counts[0]
                ready[stage] = list(weight_step([(x, offset, size) for x, offset, _ in lefts], rights, 1))
                ready[stage] += weight_step([(x, offset + size, n - size) for x, offset, n in lefts], rights, chunk_counts[0] - 1)
            else:
                ready[stage] = weight_step(lefts, rights, chunk_counts[stage])
            if line is not None and stage == LINED[0]:
                line.start()
            if line is None or stage not in LINED:
                plain[stage] = lax.psum(jnp.concatenate(ready[stage]), "dp").astype(f32)
            return (ready[stage][0],)

        dh, dh_low, vec, ub_now, pb_now, marks_now = backward(flag, received, own[step], w, *contexts[2 - step], records[2 - step], hook, step == 2)
        marks.append(marks_now)
        vectors = vec if vectors is None else vectors + vec
        ub = ub_now if ub is None else ub + ub_now
        pb = pb_now if pb is None else pb + pb_now
        if step < 2:
            received = [to_section(x, [(1, 0)]) for x in dh_low]
        if step >= 1:
            input_grads[2 - step] = lax.dynamic_slice_in_dim(jnp.concatenate(dh), chip * share, share, 0)

    if line is not None:
        results = dict(zip(order, line.finish()))
        parts = {place: [results[place, i] for i in range(chunk_counts[place])] for place in LINED}
        spread = [jnp.concatenate(parts[place], axis=0) if place in parts else plain[place] for place in range(3)]
        d_qkv = jnp.stack([p.T for p in parts[3]], axis=1)
    else:
        spread = [plain[place] for place in range(3)]
        d_qkv = plain[3].T.reshape(model, 3, width)
    d_down, d_up, d_out = spread
    units_count = up_weight.shape[-1]
    small = jnp.concatenate([vectors.reshape(6, model)], axis=0)
    small = small + core_other(small)
    ub = ub[:, :units_count] + core_other(ub[:, units_count:])
    pb = pb[:, :wide] + core_other(pb[:, wide:])
    vector = jnp.concatenate([ub[0], pb[0], small.reshape(-1)]).reshape(-1, LANES)
    vector = dp_sum_after(vector, [line.seen[-6], line.seen[-1]] if line is not None else [()]).reshape(-1)
    proj_half = dp_sum_after(proj_half, [(marks[1][1],), (marks[2][0],)])
    proj_there = core_other(proj_half)
    sent_proj = to_section(jnp.where(lower, proj_half, proj_there), [(1, 0)])
    proj_out = jnp.where(first, sent_proj, jnp.where(lower, proj_there, proj_half))
    ub = vector[:units_count][None]
    pb = vector[units_count : units_count + wide]
    small = vector[units_count + wide :].reshape(6, model)
    stack = jnp.stack(input_grads)
    swap = [(0, 1), (1, 0)]
    docs = groups // 2
    sent_input = to_section(stack[:, :, mid:], swap)
    sent_board = to_section(board[:, :docs], swap)
    return (
        jnp.where(first, sent_board, board[:, docs:]),
        jnp.where(first, stack[:, :, :mid], sent_input),
        d_qkv[None],
        pb.reshape(1, 3, width),
        d_out[None],
        d_up[None],
        ub,
        d_down[None],
        small[0:2][None],
        small[2:4][None],
        small[4:6][None],
        proj_out,
    )


def solution(mesh):
    return jax.shard_map(
        on_device,
        mesh=mesh,
        in_specs=(
            P("dp", "tensor", None),
            P("dp", None),
            P("dp", None),
            P("section", None, None, "tensor"),
            P("section", None, "tensor"),
            P("section", "tensor", None),
            P("section", None, "tensor"),
            P("section", "tensor"),
            P("section", "tensor", None),
            P("section", None, None),
            P("section", None, None),
            P("section", None, None),
            P(),
        ),
        out_specs=(
            P("dp", "section"),
            P("dp", "tensor", "section"),
            P("section", None, None, "tensor"),
            P("section", None, "tensor"),
            P("section", "tensor", None),
            P("section", None, "tensor"),
            P("section", "tensor"),
            P("section", "tensor", None),
            P("section", None, None),
            P("section", None, None),
            P("section", None, None),
            P("section", None),
        ),
        check_vma=False,
    )
```

```python
import functools

import jax
import jax.numpy as jnp
import numpy as np
from jax import lax
from jax.experimental import pallas as pl
from jax.experimental.pallas import tpu as pltpu
from jax.sharding import PartitionSpec as P

HD = 64
QLEN = 32
LANES = 128

norm_eps = 1e-05
unit_eps = 1e-06
softness_factor = 0.0625
rope_base = 10000.0
hidden_score = -1000000000.0
contract_rows = (((0,), (0,)), ((), ()))
contract_cols = (((1,), (1,)), ((), ()))
contract_inner = (((1,), (0,)), ((), ()))
bf16 = jnp.bfloat16
f32 = jnp.float32


def dot(left, right, contraction=contract_inner):
    return lax.dot_general(left, right, contraction, preferred_element_type=f32)


def flip(value, bit):
    count = lax.axis_size("tensor")
    return lax.ppermute(value, "tensor", [(i, i ^ (1 << bit)) for i in range(count)])


def chip_bits():
    return range(1, lax.axis_size("tensor").bit_length() - 1)


def core_other(value):
    return flip(value, 0)


def chips_gather(value, chip):
    for bit in chip_bits():
        other = flip(value, bit)
        upper = (chip >> (bit - 1)) % 2 == 1
        value = jnp.concatenate([jnp.where(upper, other, value), jnp.where(upper, value, other)], axis=0)
    return value


def chips_other(low):
    bits = list(chip_bits())
    if not bits:
        return low, jnp.zeros_like(low)
    for bit in bits[:-1]:
        low = (low.astype(f32) + flip(low, bit).astype(f32)).astype(bf16)
    return low, flip(low, bits[-1])


def to_section(value, pairs):
    return lax.ppermute(value, "section", pairs)


def join_kernel(upper, mine, other, out):
    size = mine.shape[0]
    first = upper[0, 0] == 1
    out[:size, :] = jnp.where(first, other[...], mine[...])
    out[size:, :] = jnp.where(first, mine[...], other[...])


def dp_gather(value, marks):
    count = lax.axis_size("dp")
    me = lax.axis_index("dp")
    step = 1
    while step < count:
        other = lax.ppermute(value, "dp", [(i, i ^ step) for i in range(count)])
        upper = ((me // step) % 2).astype(jnp.int32).reshape(1, 1)
        outs = [((2 * value.shape[0], value.shape[1]), value.dtype)]
        value = call(join_kernel, [upper, value, other], outs, us=1, after=marks[0], smem=(0,))[0]
        marks = marks[1:] or marks
        step *= 2
    return value


def dp_sum(value):
    count = lax.axis_size("dp")
    step = 1
    while step < count:
        value = value + lax.ppermute(value, "dp", [(i, i ^ step) for i in range(count)])
        step *= 2
    return value


def slot_kernel(*refs, own, across, next_own, result):
    refs = list(refs)
    end = refs.pop(0)[0, 0] == 1
    take = lambda wanted: refs.pop(0)[...] if wanted else None
    chunk, arrived = take(own), take(own or result)
    side, over = take(across), take(across)
    following = take(next_own)
    finished = take(result)
    total = (side.astype(f32) + over.astype(f32)).astype(bf16) if across else None
    if own:
        refs.pop(0)[...] = (chunk.astype(f32) + arrived.astype(f32)).astype(bf16)
    if across or next_own:
        if not across:
            onward = following
        elif not next_own:
            onward = total
        else:
            onward = jnp.where(end, following, total)
        refs.pop(0)[...] = onward
    if across:
        refs.pop(0)[...] = total
    if result:
        refs.pop(0)[...] = jnp.where(end, arrived, finished).astype(f32)


class LineSum:

    def __init__(self, end, chunks, there):
        self.end, self.chunks, self.count, self.there = end, chunks, len(chunks), there
        self.k, self.side, self.over, self.total, self.results = 0, None, None, None, []
        self.arrived = []

    def outer(self, value):
        self.arrived.append(lax.ppermute(value, "dp", [(0, 1), (1, 0), (2, 3), (3, 2)]))

    def start(self):
        self.outer(self.chunks[0]())
        self.outer(self.chunks[1]())

    def step(self, after=()):
        k, n = self.k, self.count
        own, across, next_own, result = k < n, 1 <= k <= n, 1 <= k < n - 1, k >= 2
        arrived = self.arrived.pop(0)
        chunk = self.chunks[k]() if own else None
        following = self.chunks[k + 1]() if next_own else None
        ins = [self.end]
        ins += [chunk] if own else []
        ins += [arrived] if own or result else []
        ins += [self.side, self.over] if across else []
        ins += [following] if next_own else []
        ins += [self.total] if result else []
        shape = arrived.shape
        outs = [(shape, bf16)] * (own + (across or next_own) + across) + [(shape, f32)] * result
        got = list(
            call(functools.partial(slot_kernel, own=own, across=across, next_own=next_own, result=result), ins, outs, us=2 * SLOT, after=after, smem=(0,))
        )
        side = got.pop(0) if own else None
        onward = got.pop(0) if across or next_own else None
        self.total = got.pop(0) if across else None
        if result:
            self.results.append(got.pop(0))
        self.side = side
        if own:
            self.over = lax.ppermute(side, "dp", [(1, 2), (2, 1)])
        if onward is not None:
            self.outer(onward)
        self.k += 1
        return (side if own else onward if onward is not None else self.results[-1],)

    def busy(self):
        return self.k <= self.count + 1

    def can_step(self):
        return self.busy() and not (1 <= self.k < self.count - 1 and not self.there(self.k + 1))


class LineSums:

    def __init__(self, end, ready, keys):
        lines = [keys[i::2] for i in range(2)]
        self.lines = [
            LineSum(end, [lambda key=key: ready[key[0]][key[1]] for key in line], lambda k, line=line: line[k][0] in ready) for line in lines
        ]
        self.last, self.turn, self.seen = (), 0, []

    def start(self):
        for line in self.lines:
            line.start()

    def step(self, after=()):
        line = self.lines[self.turn]
        if line.busy() and not line.can_step():
            return self.last
        self.turn = 1 - self.turn
        if line.busy():
            self.last = line.step(tuple(after) + self.last)
            self.seen.append(self.last)
        return self.last

    def finish(self):
        while any(line.busy() for line in self.lines):
            self.step()
        results = [None] * sum(line.count for line in self.lines)
        for i, line in enumerate(self.lines):
            results[i::2] = line.results
        return results


def rope_tables(positions):
    half = HD // 2
    frequency = np.power(np.float32(rope_base), (-2.0 * np.arange(half) / HD).astype(np.float32)).astype(np.float32)
    angles = (positions.astype(np.float32)[:, None] * frequency[None, :]).astype(np.float32)
    cosine, sine = np.cos(angles), np.sin(angles)
    head = (np.concatenate([cosine, cosine], 1), np.concatenate([-sine, sine], 1))
    return tuple(np.tile(part, (1, LANES // HD)).astype(np.float32) for part in head)


VMEM = pl.BlockSpec(memory_space=pltpu.VMEM)
ANY = pl.BlockSpec(memory_space=pl.ANY)
SMEM = pl.BlockSpec(memory_space=pltpu.SMEM)


pace = {"now": 1.0}
EARLY, LATE = 1.0, 0.6
SLOT = 0.2
LINED = (0, 1, 3, 2)


def cost(us):
    us = us * pace["now"]
    return pl.CostEstimate(flops=int(us * 1.1e9), bytes_accessed=int(us * 1e6), transcendentals=0)


def held(x):
    return pltpu.with_memory_space_constraint(x, pltpu.HBM)


def call(kernel, ins, outs, us, scratch=(), after=(), smem=(), keep=(), limit=16):
    n = len(ins)

    def body(*refs):
        kernel(*refs[:n], *refs[n + len(after) :])

    return pl.pallas_call(
        body,
        in_specs=[SMEM if i in smem else VMEM for i in range(n)] + [ANY] * len(after),
        out_specs=[VMEM] * len(outs),
        out_shape=[pltpu.HBM(*out) if i in keep else jax.ShapeDtypeStruct(*out) for i, out in enumerate(outs)],
        scratch_shapes=list(scratch),
        compiler_params=pltpu.CompilerParams(vmem_limit_bytes=limit * 1024 * 1024),
        cost_estimate=cost(us),
        name=getattr(kernel, "func", kernel).__name__,
    )(*ins, *after)


def load_kernel(own, oth, out, sem, axis):
    size = own.shape[axis]
    places = [out.at[:, :size], out.at[:, size:]] if axis else [out.at[:size], out.at[size:]]
    copies = [pltpu.make_async_copy(x, place, sem.at[i]) for i, (x, place) in enumerate(zip((own, oth), places))]
    for copy in copies:
        copy.start()
    for copy in copies:
        copy.wait()


def chip_weight(own, axis):
    other = core_other(own)
    shape = tuple(2 * n if i == axis else n for i, n in enumerate(own.shape))
    return pl.pallas_call(
        functools.partial(load_kernel, axis=axis),
        in_specs=[ANY, ANY],
        out_specs=VMEM,
        out_shape=pltpu.VMEM(shape, own.dtype),
        cost_estimate=cost(2),
        scratch_shapes=[pltpu.SemaphoreType.DMA((2,))],
        compiler_params=pltpu.CompilerParams(vmem_limit_bytes=16 * 1024 * 1024),
    )(own, other)


def half_rows(ref, c):
    size = ref.shape[0] // 2
    return ref[c * size : (c + 1) * size, :]


def half_lanes(ref, c):
    size = ref.shape[1] // 2
    return ref[:, c * size : (c + 1) * size]


def merge(out, before, value):
    size = value.shape[0]
    out[:size, :] = before[...]
    out[size:, :] = value


def swap_halves(tile):
    lane = lax.broadcasted_iota(jnp.int32, tile.shape, 1)
    return jnp.where(lane % HD < HD // 2, pltpu.roll(tile, LANES - HD // 2, 1), pltpu.roll(tile, HD // 2, 1))


def qkv_kernel(flag, entering, received, w, b, cos, sin, h_ref, q_ref, kv_ref):
    h = jnp.where(flag[0, 0] == 1, entering[...], received[...])
    h_ref[...] = h
    width = w.shape[1] // 6
    c, s = cos[...], sin[...]
    for place in range(2):
        at = slice(place * 3 * width, (place + 1) * 3 * width)
        p = dot(h, w[:, at]) + b[:, at]
        for t in range(0, width, LANES):
            at = slice(place * width + t, place * width + t + LANES)
            tile = p[:, t : t + LANES]
            q_ref[:, at] = (tile * c + swap_halves(tile) * s).astype(bf16)
            tile = p[:, width + t : width + t + LANES]
            kv_ref[:, at] = (tile * c + swap_halves(tile) * s).astype(bf16)
        kv_ref[:, 2 * width + place * width : 2 * width + (place + 1) * width] = p[:, 2 * width :].astype(bf16)


def qkv_step(flag, entering, received, w, tables, after=()):
    rows, model = entering.shape
    features = w["qkv"].shape[1] // 3
    return call(
        qkv_kernel,
        [flag, entering, received, w["qkv"], w["qkv_b"], *tables],
        [((rows, model), bf16), ((rows, features), bf16), ((rows, 2 * features), bf16)],
        after=after,
        smem=(0,),
        keep=(0, 1, 2),
        us=2,
    )


def head_rows(tile, place):
    row = lax.broadcasted_iota(jnp.int32, tile.shape, 0)
    return jnp.where(row // HD == place, tile, 0.0).astype(bf16)


def head_lanes(tile, place):
    lane = lax.broadcasted_iota(jnp.int32, tile.shape, 1)
    return jnp.where(lane // HD == place, tile, 0.0).astype(bf16)


def tile_at(j, features, base=0):
    return slice(base + j * LANES, base + (j + 1) * LANES)


def partner_tile(j, features):
    tiles = features // LANES
    return (j + tiles // 2) % tiles


def partner_base(j, features, base=0):
    return tile_at(partner_tile(j, features), features, base)


def attend_kernel(*refs, c):
    q_ref, kv_own, kv_oth, bias_ref, w = refs[:5]
    if c:
        o_before, v_t, refs = refs[5], refs[6], refs[7:]
        o_own, o_oth, lse_ref, low_ref, o_t, s_all = refs
    else:
        o_first, k_t, v_t, lse_ref, low_ref, o_t, s_all = refs[5:]
    features = q_ref.shape[1]
    rows = kv_own.shape[0]
    some = rows // 2
    q_half = half_rows(q_ref, c)
    for j in range(features // LANES):
        at = tile_at(j, features)
        q_t = q_half[:, at].astype(f32).T * HD ** (-0.5)
        k_here, k_there = kv_own[:, at], kv_oth[:, partner_base(j, features)]
        for place in range(2):
            q_one = head_rows(q_t, place)
            s_all[2 * j + place, :rows, :] = dot(k_here, q_one)
            s_all[2 * j + place, rows:, :] = dot(k_there, q_one)
        if not c:
            v_here, v_there = kv_own[:, tile_at(j, features, features)], kv_oth[:, partner_base(j, features, features)]
            v_t[at, :rows] = v_here.astype(f32).T.astype(bf16)
            v_t[at, rows:] = v_there.astype(f32).T.astype(bf16)
            k_t[at, :rows] = k_here.astype(f32).T.astype(bf16)
            k_t[at, rows:] = k_there.astype(f32).T.astype(bf16)
    bias = bias_ref[:, c * some : (c + 1) * some].astype(f32)
    for h in range(features // HD):
        s = s_all[h] + bias
        peak = jnp.max(s, axis=0, keepdims=True)
        e = jnp.exp(s - peak)
        total = jnp.sum(e, axis=0, keepdims=True)
        s_all[h] = e * (1.0 / total)
        lse_ref[h : h + 1, :] = peak + jnp.log(total)
    for h in range(features // HD):
        o_t[h * HD : (h + 1) * HD, :] = dot(v_t[h * HD : (h + 1) * HD, :], s_all[h].astype(bf16))
    o = o_t[...].T.astype(bf16)
    half = features // 2
    if c:
        merge(o_own, o_before[:, :half], o[:, :half])
        merge(o_oth, o_before[:, half:], o[:, half:])
    else:
        o_first[...] = o
    low_ref[...] = dot(o, w[...]).astype(bf16)


def attend_step(c, q, kv, kv_other, bias, w, before=(), after=()):
    rows, features = q.shape
    model = w["out"].shape[1]
    some = rows // 2
    heads = features // HD
    if c:
        kept = [((rows, features // 2), bf16)] * 2
    else:
        kept = [((some, features), bf16), ((features, 2 * rows), bf16), ((features, 2 * rows), bf16)]
    return call(
        functools.partial(attend_kernel, c=c),
        [q, kv, kv_other, bias, w["out"], *before],
        kept + [((heads, some), f32), ((some, model), bf16)],
        scratch=[pltpu.VMEM((features, some), f32), pltpu.VMEM((heads, 2 * rows, some), f32)],
        after=after,
        keep=(0, 1, 2) if c else (1, 3),
        us=4,
    )


def normed(values):
    centred = values - jnp.mean(values, axis=-1, keepdims=True)
    inverse = lax.rsqrt(jnp.mean(centred * centred, axis=-1, keepdims=True) + norm_eps)
    return centred * inverse, inverse


def norm_back(gradient, n, inverse):
    return inverse * (gradient - jnp.mean(gradient, axis=-1, keepdims=True) - n * jnp.mean(gradient * n, axis=-1, keepdims=True))


def feed_kernel(*refs, c):
    h, low, recv, vec, up, b, down = refs[:7]
    before, refs = (refs[7:10], refs[10:]) if c else (None, refs[7:])
    n_ref, r_ref, sl_ref, low_ref, g_own, rest = refs
    s1 = half_rows(h, c).astype(f32) + (low[...].astype(f32) + recv[...].astype(f32)) + vec[0:1, :]
    n, r = normed(s1)
    n_ref[...] = n
    r_ref[...] = r
    h1 = (n * vec[1:2, :] + vec[2:3, :]).astype(bf16)
    u = dot(h1, up[...]) + b[...]
    phi = 0.5 * (1.0 + lax.erf(u * 0.7071067811865476))
    g = (u * phi).astype(bf16)
    sl_ref[...] = (phi + u * jnp.exp(-0.5 * u * u) * 0.3989422804014327).astype(bf16)
    low_ref[...] = dot(g, down[...]).astype(bf16)
    units = up.shape[1] // 2
    some, model = h1.shape
    if c:
        g_before, rest_before, o_oth = before
        merge(g_own, g_before, g[:, :units])
        rest[:some, :model] = rest_before[:, :model]
        rest[some:, :model] = h1
        rest[:, model : 2 * model] = h[...]
        rest[:some, 2 * model : 2 * model + units] = rest_before[:, model:]
        rest[some:, 2 * model : 2 * model + units] = g[:, units:]
        rest[:, 2 * model + units :] = o_oth[...]
    else:
        g_own[...] = g[:, :units]
        rest[:, :model] = h1
        rest[:, model:] = g[:, units:]


def feed_step(c, h, low, recv, vec, w, before=(), after=()):
    rows, model = h.shape
    units = w["up"].shape[1] // 2
    some = rows // 2
    if c:
        kept = [((rows, units), bf16), ((rows, 2 * model + units + before[-1].shape[1]), bf16)]
    else:
        kept = [((some, units), bf16), ((some, model + units), bf16)]
    return call(
        functools.partial(feed_kernel, c=c),
        [h, low, recv, vec, w["up"], w["up_b"], w["down"], *before],
        [((some, model), f32), ((some, 1), f32), ((some, 2 * units), bf16), ((some, model), bf16)] + kept,
        after=after,
        keep=(0, 1, 2, 4, 5) if c else (0, 1, 2),
        us=4,
    )


def output_kernel(*refs, c):
    n1, low, recv, vec = refs[:4]
    before, (n_ref, r_ref, y_ref) = (refs[4], refs[5:]) if c else (None, refs[4:])
    s2 = n1[...] * vec[0:1, :] + vec[1:2, :] + (low[...].astype(f32) + recv[...].astype(f32)) + vec[2:3, :]
    n, r = normed(s2)
    n_ref[...] = n
    r_ref[...] = r
    y = (n * vec[3:4, :] + vec[4:5, :]).astype(bf16)
    if c:
        merge(y_ref, before, y)
    else:
        y_ref[...] = y


def output_step(c, n1, low, recv, vec, before=()):
    some, model = n1.shape
    return call(
        functools.partial(output_kernel, c=c),
        [n1, low, recv, vec, *before],
        [((some, model), f32), ((some, 1), f32), ((2 * some if c else some, model), bf16)],
        keep=(0, 1),
        us=2.3,
    )


def feed_back_head(dy, n, r, gain, ds_ref, vec_ref):
    ds = norm_back(dy * gain, n, r)
    ds_ref[...] = ds
    vec_ref[0:1, :] = jnp.sum(ds, axis=0, keepdims=True)
    vec_ref[1:2, :] = jnp.sum(dy * n, axis=0, keepdims=True)
    vec_ref[2:3, :] = jnp.sum(dy, axis=0, keepdims=True)
    return ds.astype(bf16)


def feed_back_tail(f, up, down, sl, low_ref, ub_ref):
    du = dot(f, down[...], contract_cols) * sl[...].astype(f32)
    ub_ref[...] = jnp.sum(du, axis=0, keepdims=True)
    u = du.astype(bf16)
    low_ref[...] = dot(u, up[...], contract_cols).astype(bf16)
    return u


def feed_back_kernel(*refs, c):
    flag, received, own, n2, r2, gain, up, down, sl = refs[:9]
    before, refs = (refs[9:11], refs[11:]) if c else (None, refs[9:])
    ds_ref, low_ref, vec_ref, ub_ref, u_own, rest = refs
    dy = jnp.where(flag[0, 0] == 1, received[...].astype(f32), own[...])
    f = feed_back_head(dy, n2[...], r2[...], gain[...], ds_ref, vec_ref)
    u = feed_back_tail(f, up, down, sl, low_ref, ub_ref)
    units = up.shape[1] // 2
    some, model = f.shape
    if c:
        merge(u_own, before[0], u[:, :units])
        rest[:some, :] = before[1][...]
        rest[some:, :model] = f
        rest[some:, model:] = u[:, units:]
    else:
        u_own[...] = u[:, :units]
        rest[:, :model] = f
        rest[:, model:] = u[:, units:]


def feed_back_step(c, flag, received, own, n2, r2, gain, w, sl, before=(), after=()):
    some, model = n2.shape
    units = w["up"].shape[1] // 2
    kept = 2 * some if c else some
    return call(
        functools.partial(feed_back_kernel, c=c),
        [flag, received, own, n2, r2, gain, w["up"], w["down"], sl, *before],
        [
            ((some, model), f32), ((some, model), bf16), ((3, model), f32), ((1, 2 * units), f32),
            ((kept, units), bf16), ((kept, model + units), bf16),
        ],
        after=after,
        smem=(0,),
        keep=(0, 2, 3, 4, 5) if c else (0, 2, 3),
        us=5.5,
    )


def first_kernel(rec_a, rec_b, n_a, n_b, r_a, r_b, gain, ds_a, ds_b, vec_a, vec_b, f_ref):
    some = n_a.shape[0]
    f_ref[:some, :] = feed_back_head(rec_a[...].astype(f32), n_a[...], r_a[...], gain[...], ds_a, vec_a)
    f_ref[some:, :] = feed_back_head(rec_b[...].astype(f32), n_b[...], r_b[...], gain[...], ds_b, vec_b)


def first_step(received, n2, r2, gain, after=()):
    some, model = n2[0].shape
    return call(
        first_kernel,
        [*received, *n2, *r2, gain],
        [((some, model), f32)] * 2 + [((3, model), f32)] * 2 + [((2 * some, model), bf16)],
        after=after,
        keep=(0, 1, 2, 3),
        us=2.5,
    )


def second_kernel(*refs, c):
    f, up, down, sl = refs[:4]
    before, refs = (refs[4:6], refs[6:]) if c else (None, refs[4:])
    low_ref, ub_ref, u_own, u_oth = refs
    u = feed_back_tail(half_rows(f, c), up, down, sl, low_ref, ub_ref)
    units = up.shape[1] // 2
    for place, value in enumerate((u[:, :units], u[:, units:])):
        out = (u_own, u_oth)[place]
        if c:
            merge(out, before[place], value)
        else:
            out[...] = value


def second_step(c, f, w, sl, before=(), after=()):
    rows, model = f.shape
    units = w["up"].shape[1] // 2
    kept = rows if c else rows // 2
    return call(
        functools.partial(second_kernel, c=c),
        [f, w["up"], w["down"], sl, *before],
        [((rows // 2, model), bf16), ((1, 2 * units), f32), ((kept, units), bf16), ((kept, units), bf16)],
        after=after,
        keep=(1, 2, 3) if c else (1,),
        us=4.5,
    )


def attend_back_kernel(*refs, c):
    (ds2, low, recv, n1, r1, gain, w, q_ref, kv_own, kv_oth, k_t, bias_ref, lse_ref), refs = refs[:13], refs[13:]
    if c:
        (own_before, oth_before, out_before), refs = refs[:3], refs[3:]
    ds_ref, dq_ref, vec_ref, dkv_ref, dkv_send, out_ref, dq_t, s_all, d_all, a_all, slopes = refs
    features = q_ref.shape[1]
    rows = kv_own.shape[0]
    some = rows // 2
    dh1 = ds2[...] + (low[...].astype(f32) + recv[...].astype(f32))
    n = n1[...]
    ds1 = norm_back(dh1 * gain[...], n, r1[...])
    ds_ref[...] = ds1
    vec_ref[0:1, :] = jnp.sum(ds1, axis=0, keepdims=True)
    vec_ref[1:2, :] = jnp.sum(dh1 * n, axis=0, keepdims=True)
    vec_ref[2:3, :] = jnp.sum(dh1, axis=0, keepdims=True)
    spread = ds1.astype(bf16)
    if c:
        merge(out_ref, out_before, spread)
    else:
        out_ref[...] = spread
    q_half = half_rows(q_ref, c)
    for j in range(features // LANES):
        at = tile_at(j, features)
        q_t = q_half[:, at].astype(f32).T * HD ** (-0.5)
        k_here, k_there = kv_own[:, at], kv_oth[:, partner_base(j, features)]
        for place in range(2):
            q_one = head_rows(q_t, place)
            s_all[2 * j + place, :rows, :] = dot(k_here, q_one)
            s_all[2 * j + place, rows:, :] = dot(k_there, q_one)
    mixed = dot(spread, w[...], contract_cols).astype(bf16).astype(f32)
    for j in range(features // LANES):
        do_t = mixed[:, tile_at(j, features)].T
        v_here, v_there = kv_own[:, tile_at(j, features, features)], kv_oth[:, partner_base(j, features, features)]
        for place in range(2):
            do_one = head_rows(do_t, place)
            d_all[2 * j + place, :rows, :] = dot(v_here, do_one)
            d_all[2 * j + place, rows:, :] = dot(v_there, do_one)
    bias = bias_ref[:, c * some : (c + 1) * some].astype(f32)
    for h in range(features // HD):
        a = jnp.exp(s_all[h] + bias - lse_ref[h : h + 1, :])
        da = d_all[h]
        slope = a * (da - jnp.sum(da * a, axis=0, keepdims=True))
        slopes[h] = slope.astype(bf16) * jnp.asarray(HD ** (-0.5), bf16)
        a_all[h] = a.astype(bf16)
    for h in range(features // HD):
        dq_t[h * HD : (h + 1) * HD, :] = dot(k_t[h * HD : (h + 1) * HD, :], slopes[h])
    for j in range(features // LANES):
        at, v_at = tile_at(j, features), tile_at(j, features, features)
        theirs, v_theirs = partner_base(j, features), partner_base(j, features, features)
        q, do = q_half[:, at].astype(f32), mixed[:, at]
        dk = dot(slopes[2 * j], head_lanes(q, 0)) + dot(slopes[2 * j + 1], head_lanes(q, 1))
        dv = dot(a_all[2 * j], head_lanes(do, 0)) + dot(a_all[2 * j + 1], head_lanes(do, 1))
        if c:
            dkv_ref[:, at] = dk[:rows] + own_before[:, at]
            dkv_ref[:, v_at] = dv[:rows] + own_before[:, v_at]
            dkv_send[:, theirs] = (dk[rows:] + oth_before[:, theirs]).astype(bf16)
            dkv_send[:, v_theirs] = (dv[rows:] + oth_before[:, v_theirs]).astype(bf16)
        else:
            dkv_ref[:, at] = dk[:rows]
            dkv_ref[:, v_at] = dv[:rows]
            dkv_send[:, theirs] = dk[rows:]
            dkv_send[:, v_theirs] = dv[rows:]
    dq_ref[...] = dq_t[...].T


def attend_back_step(c, ds2, low, recv, n1, r1, gain, w, q, kv, kv_other, k_t, bias, lse, before=(), after=()):
    some, model = ds2.shape
    features = q.shape[1]
    rows = 2 * some
    heads = features // HD
    all_heads = (heads, 2 * rows, some)
    return call(
        functools.partial(attend_back_kernel, c=c),
        [ds2, low, recv, n1, r1, gain, w["out"], q, kv, kv_other, k_t, bias, lse, *before],
        [
            ((some, model), f32), ((some, features), f32), ((3, model), f32),
            ((rows, 2 * features), f32), ((rows, 2 * features), bf16 if c else f32), ((rows if c else some, model), bf16),
        ],
        scratch=[
            pltpu.VMEM((features, some), f32), pltpu.VMEM(all_heads, f32), pltpu.VMEM(all_heads, f32), pltpu.VMEM(all_heads, bf16),
            pltpu.VMEM(all_heads, bf16),
        ],
        after=after,
        keep=(0, 1, 2, 3, 5) if c else (0, 1, 2),
        limit=24,
        us=6.5,
    )


def qkv_back_kernel(*refs, c):
    dq, dkv_ref, arrived_ref, cos, sin, w = refs[:6]
    before, refs = (refs[6:9], refs[9:]) if c else (None, refs[6:])
    low_ref, b_ref, p_own, rest = refs
    some, features = dq.shape
    width = features // 2
    cosine, sine = half_rows(cos, c), half_rows(sin, c)
    dkv = half_rows(dkv_ref, c) + half_rows(arrived_ref, c).astype(f32)
    rows_at = slice(some, 2 * some) if c else slice(0, some)
    model = w.shape[0] if c else 0
    total = None
    for place, p_ref in enumerate((p_own, rest)):
        base = place * 3 * width
        start = place * model
        for t in range(0, width, LANES):
            at = slice(place * width + t, place * width + t + LANES)
            v_at = slice(features + place * width + t, features + place * width + t + LANES)
            gq, gk, gv = dq[:, at], dkv[:, at], dkv[:, v_at]
            gq = gq * cosine - swap_halves(gq) * sine
            gk = gk * cosine - swap_halves(gk) * sine
            for part, g in enumerate((gq, gk, gv)):
                to = part * width + t
                p_ref[rows_at, start + to : start + to + LANES] = g.astype(bf16)
                b_ref[0:1, base + to : base + to + LANES] = jnp.sum(g, axis=0, keepdims=True)
        part = dot(p_ref[rows_at, start : start + 3 * width], w[:, base : base + 3 * width], contract_cols)
        total = part if total is None else total + part
    low_ref[...] = total.astype(bf16)
    if c:
        p_own[:some, :] = before[0][...]
        rest[:some, model:] = before[1][...]
        rest[:, :model] = before[2][...]


def qkv_back_step(c, dq, dkv, arrived, tables, w, before=(), after=()):
    some, features = dq.shape
    model, wide = w["qkv"].shape
    kept = [((2 * some, wide // 2), bf16), ((2 * some, model + wide // 2), bf16)] if c else [((some, wide // 2), bf16)] * 2
    return call(
        functools.partial(qkv_back_kernel, c=c),
        [dq, dkv, arrived, *tables, w["qkv"], *before],
        [((some, model), bf16), ((1, wide), f32)] + kept,
        after=after,
        keep=(1, 2, 3) if c else (1,),
        us=3.4,
    )


def end_kernel(ds, low, recv, out, low_out):
    dh = ds[...] + (low[...].astype(f32) + recv[...].astype(f32))
    out[...] = dh
    low_out[...] = dh.astype(bf16)


def end_step(ds, low, recv, after):
    return call(end_kernel, [ds, low, recv], [(ds.shape, f32), (ds.shape, bf16)], us=1.5, after=after)


def part(array, offset, width):
    return array, offset, width


def weight_kernel(*refs, pieces):
    lefts, rights, outs = refs[:pieces], refs[pieces : 2 * pieces], refs[2 * pieces :]
    left = jnp.concatenate([x[...] for x in lefts], axis=0)
    right = jnp.concatenate([x[...] for x in rights], axis=0)
    total = dot(left, right, contract_rows).astype(bf16)
    for i, out in enumerate(outs):

        @pl.when(pl.program_id(0) == i)
        def _(out=out):
            out[...] = total


def weight_step(lefts, rights, steps):
    shape = (lefts[0][2], rights[0][2])
    steps = min(steps, shape[0] // LANES)
    some = (shape[0] // steps, shape[1])
    specs = [pl.BlockSpec((x.shape[0], some[0]), lambda i, at=offset // some[0]: (0, at + i)) for x, offset, _ in lefts]
    specs += [pl.BlockSpec((x.shape[0], width), lambda i, at=offset // width: (0, at)) for x, offset, width in rights]
    return pl.pallas_call(
        functools.partial(weight_kernel, pieces=len(lefts)),
        grid=(steps,),
        in_specs=specs,
        out_specs=[pl.BlockSpec(some, lambda i: (0, 0))] * steps,
        out_shape=[jax.ShapeDtypeStruct(some, bf16)] * steps,
        cost_estimate=cost(6),
        compiler_params=pltpu.CompilerParams(vmem_limit_bytes=24 * 1024 * 1024),
    )(*[held(x) for x, _, _ in (*lefts, *rights)])


def sum_kernel(x, y, out):
    out[...] = x[...] + y[...]


def sum_after(x, y, after):
    return call(sum_kernel, [x, y], [(x.shape, x.dtype)], us=1, after=after)[0]


def dp_sum_after(value, marks):
    count = lax.axis_size("dp")
    step = 1
    while step < count:
        value = sum_after(value, lax.ppermute(value, "dp", [(i, i ^ step) for i in range(count)]), marks[0])
        marks = marks[1:] or marks
        step *= 2
    return value


def embed_kernel(y, proj, alive, units_ref, inverse_ref, payload):
    z = dot(y[...], proj[...])
    inverse = lax.rsqrt(jnp.sum(z * z, axis=-1, keepdims=True) + unit_eps)
    units = z * inverse
    units_ref[...] = units
    inverse_ref[...] = inverse
    width = units.shape[1]
    payload[:, :width] = units.astype(bf16)
    payload[:, width:] = alive[...]


def embed_step(y, proj, alive, after):
    rows, width = alive.shape
    return call(embed_kernel, [y, proj, alive], [((rows, width), f32), ((rows, 1), f32), ((rows, 2 * width), bf16)], us=1.5, after=after)


def scores_kernel(y, proj, docs_own, docs_oth, grad_t, z_ref, m_ref, dy_a, dy_b, terms_own, terms_oth, groups):
    z = dot(y[...], proj[...])
    inverse = lax.rsqrt(jnp.sum(z * z, axis=-1, keepdims=True) + unit_eps)
    e = z * inverse
    e_low = e.astype(bf16)
    e_t = e_low.astype(f32).T.astype(bf16)
    half, width = e.shape
    back = None
    for d in range(groups):
        at = slice(d * half, (d + 1) * half)
        docs = jnp.concatenate([docs_own[at, :width], docs_oth[at, :width]], axis=0)
        alive = jnp.concatenate([docs_own[at, width : width + 1], docs_oth[at, width : width + 1]], axis=0).astype(f32)
        logits = jnp.where(alive > 0, dot(docs, e_t) / softness_factor, hidden_score)
        peak = jnp.max(logits, axis=0, keepdims=True)
        x = jnp.exp(logits - peak)
        total = jnp.sum(x, axis=0, keepdims=True)
        m_ref[d : d + 1, :] = softness_factor * (peak + jnp.log(total))
        pull = (x * (grad_t[d : d + 1, :] / total)).astype(bf16)
        terms = dot(pull, e_low)
        terms_own[at, :] = terms[:half]
        terms_oth[at, :] = terms[half:]
        part = dot(docs.astype(f32).T.astype(bf16), pull)
        back = part if back is None else back + part
    de = back.T
    dz = (inverse * (de - e * jnp.sum(de * e, axis=-1, keepdims=True))).astype(bf16)
    z_ref[...] = dz
    dy = dot(dz, proj[...], contract_cols)
    some = dy_a.shape[0]
    dy_a[...] = dy[:some]
    dy_b[...] = dy[some:]


def scores_step(y, proj, docs_own, docs_oth, grad_t):
    rows, model = y.shape
    groups, width = grad_t.shape[0], proj.shape[1]
    return call(
        functools.partial(scores_kernel, groups=groups),
        [y, proj, docs_own, docs_oth, grad_t],
        [
            ((rows, width), bf16), ((groups, rows), f32), ((rows // 2, model), f32), ((rows // 2, model), f32),
            ((groups * rows, width), f32), ((groups * rows, width), f32),
        ],
        limit=32,
        us=2.6,
    )


def forward(flag, entering, received, w, bias, tables, after=()):
    h, q, kv = qkv_step(flag, entering, received, w, tables, after)
    kv_other = held(core_other(kv))
    h_here, q, kv = held(h), held(q), held(kv)
    o_a, k_t, v_t, lse_a, low_a = attend_step(0, q, kv, kv_other, bias, w)
    sum_a = chips_other(low_a)
    o, o_o, lse_b, low_b = attend_step(1, q, kv, kv_other, bias, w, (o_a, v_t))
    sum_b = chips_other(low_b)
    n1_a, r1_a, sl_a, low_a, *before = feed_step(0, h_here, *sum_a, w["vec_feed"], w)
    sum_a = chips_other(low_a)
    n1_b, r1_b, sl_b, low_b, g, rest = feed_step(1, h_here, *sum_b, w["vec_feed"], w, (*before, held(o_o)))
    sum_b = chips_other(low_b)
    n1_a, n1_b = held(n1_a), held(n1_b)
    n2_a, r2_a, y_a = output_step(0, n1_a, *sum_a, w["vec_out"])
    n2_b, r2_b, y = output_step(1, n1_b, *sum_b, w["vec_out"], (y_a,))
    there = core_other(rest)
    model, units, width = h.shape[1], g.shape[1], o.shape[1]
    kept = (
        (part(g, 0, units), part(there, 2 * model, units)),
        (part(rest, 0, model), part(there, 0, model)),
        (part(o, 0, width), part(there, 2 * model + units, width)),
        (part(rest, model, model), part(there, model, model)),
    )
    a = (held(lse_a), n1_a, held(r1_a), held(sl_a), held(n2_a), held(r2_a))
    b = (held(lse_b), n1_b, held(r1_b), held(sl_b), held(n2_b), held(r2_b))
    return y, ((q, kv, kv_other, held(k_t)), (a, b)), kept, ((o,), (rest,))


def backward(flag, received, own, w, bias, tables, record, hook, last):
    (q, kv, kv_other, k_t), halves = record
    model, units = w["up"].shape[0], w["up"].shape[1] // 2
    parts, vectors, ubs, ds2s, before = [], [], [], [], ()
    after = ()
    if last:
        *ds2s, vec_a, vec_b, f = first_step(received, [x[4] for x in halves], [x[5] for x in halves], w["gain"][1:2])
        ds2s, vectors = [held(x) for x in ds2s], [vec_a, vec_b]
        after = hook(0, (part(f, 0, model), part(core_other(f), 0, model)))
        for c in range(2):
            low, ub, *before = second_step(c, f, w, halves[c][3], before, after)
            parts.append(chips_other(low))
            ubs.append(ub)
            after = ()
        hook("step", low)
        u, u_o = before
        after = hook(1, (part(u, 0, units), part(core_other(u_o), 0, units)))
        after = hook("step", after[0])
    else:
        for c in range(2):
            lse, n1, r1, sl, n2, r2 = halves[c]
            ds2, low, vec, ub, *before = feed_back_step(c, flag, received[c], own[c], n2, r2, w["gain"][1:2], w, sl, before)
            ds2s.append(held(ds2))
            parts.append(chips_other(low))
            vectors.append(vec)
            ubs.append(ub)
        u, rest = before
        there = core_other(rest)
        hook(0, (part(rest, 0, model), part(there, 0, model)))
        hook(1, (part(u, 0, units), part(there, model, units)))
    before, vectors_1, ds1s, dqs = (), [], [], []
    for c in range(2):
        lse, n1, r1, sl, n2, r2 = halves[c]
        ds1, dq, vec, dkv, send, out = attend_back_step(
            c, ds2s[c], *parts[c], n1, r1, w["gain"][0:1], w, q, kv, kv_other, k_t, bias, lse, before, after
        )
        before = (dkv, send, out) if c == 0 else ()
        ds1s.append(ds1)
        dqs.append(held(dq))
        vectors_1.append(vec)
        after = ()
    hook("step", send)
    after = hook("step", send)
    arrived, dkv = held(core_other(send)), held(dkv)
    nexts, pbs, before = [], [], ()
    for c in range(2):
        low, pb, *before = qkv_back_step(c, dqs[c], dkv, arrived, tables, w, (*before, held(out)) if c else (), after)
        nexts.append(chips_other(low))
        pbs.append(pb)
        after = ()
    hook("step", pb)
    hook("step", pb)
    p, rest = before
    there = core_other(rest)
    wide = p.shape[1]
    hook(2, (part(rest, 0, model), part(there, 0, model)))
    hook(3, (part(p, 0, wide), part(there, model, wide)))
    after = hook("end", None)
    dh, dh_low = [], []
    for c in range(2):
        out_c, low = end_step(held(ds1s[c]), *nexts[c], after)
        dh.append(out_c)
        dh_low.append(low)
        after = (low,)
    vectors = jnp.stack([vectors_1[0] + vectors_1[1], vectors[0] + vectors[1]], axis=1)
    return dh, dh_low, vectors, ubs[0] + ubs[1], pbs[0] + pbs[1], (parts[1][0], nexts[1][0])


def on_device(tokens, segment, score_grad, qkv_weight, qkv_bias, out_weight, up_weight, up_bias, down_weight, out_bias, norm_gain, norm_shift, proj_weight):
    blocks, share, model = tokens.shape
    pace["now"] = EARLY
    wide = 3 * qkv_weight.shape[-1]
    width = wide // 3
    gain, shift, bias = norm_gain[0].astype(f32), norm_shift[0].astype(f32), out_bias[0].astype(f32)
    first = lax.axis_index("section") == 0
    flag = first.astype(jnp.int32).reshape(1, 1)
    device = lax.axis_index("tensor")
    core, chip = device % 2, device // 2
    chips = lax.axis_size("tensor") // 2
    groups = lax.axis_size("dp")
    half = share * chips
    rows = 2 * half
    proj = proj_weight.shape[1]
    entering = [chips_gather(tokens[b], chip) for b in range(2)]

    def both(own):
        return jnp.concatenate([own, core_other(own)], axis=1)

    w = dict(
        qkv=chip_weight(qkv_weight[0].reshape(model, wide), 1), qkv_b=both(qkv_bias[0].reshape(1, wide).astype(f32)),
        out=chip_weight(out_weight[0], 0), up=chip_weight(up_weight[0], 1), up_b=both(up_bias.astype(f32)),
        down=chip_weight(down_weight[0], 0), gain=gain,
        vec_feed=jnp.stack([bias[0], gain[0], shift[0]]),
        vec_out=jnp.stack([gain[0], shift[0], bias[1], gain[1], shift[1]]),
    )

    def own_first(by_token):
        parts = by_token.reshape((chips, 2, share) + by_token.shape[1:])
        even = parts[:, 0].reshape((half,) + by_token.shape[1:])
        odd = parts[:, 1].reshape((half,) + by_token.shape[1:])
        return jnp.concatenate([jnp.where(core == 0, even, odd), jnp.where(core == 0, odd, even)], axis=0)

    index = np.arange(rows)
    tables = [tuple(own_first(jnp.asarray(part))[:half] for part in rope_tables(p)) for p in (index, index % QLEN)]
    segments = [own_first(segment[b]) for b in range(2)]

    def pick(zero, one):
        ids = jnp.where(first, segments[zero], segments[one])
        bias = jnp.where(ids[:, None] == ids[None, :half], 0.0, hidden_score).astype(bf16)
        return held(bias), tuple(jnp.where(first, x, y) for x, y in zip(tables[zero], tables[one]))

    contexts = [pick(0, 0), pick(1, 0), pick(1, 1)]
    received = jnp.zeros((half, model), bf16)
    records, kept, outputs = [], [], []
    alive_here = jnp.broadcast_to((segments[0][:half] == 0).astype(bf16)[:, None], (half, proj))
    slots = score_grad.shape[0]
    member = (segments[1][:half, None] == jnp.arange(slots)[None, :]).astype(f32)
    grad_t = lax.dot_general(score_grad, member, (((0,), (1,)), ((), ())), precision=lax.Precision.HIGHEST, preferred_element_type=f32)
    prelude = [w["vec_feed"], w["vec_out"], w["up_b"], alive_here, grad_t]
    prelude += [x for bias_of, tables_of in contexts for x in (bias_of, *tables_of)]
    for tick in range(3):
        y, record, keep, marks_2 = forward(flag, entering[min(tick, 1)], received, w, *contexts[tick], prelude if tick == 0 else ())
        records.append(record)
        kept.append(keep)
        outputs.append(y)
        if tick == 2:
            break
        received = to_section(y, [(0, 1)])

    doc_y, query_y = outputs[1], outputs[2]
    doc_units, inverse, payload = embed_step(doc_y, proj_weight, alive_here, (records[2][0][0],))
    docs_own = dp_gather(payload, marks_2)
    docs_oth = core_other(docs_own)
    query_dz, smooth, *query_dy, terms, terms_there = scores_step(query_y, proj_weight, docs_own, docs_oth, grad_t)
    board = lax.dot_general(member, smooth, (((0,), (1,)), ((), ())), precision=lax.Precision.HIGHEST, preferred_element_type=f32)
    terms = (terms + core_other(terms_there)).reshape(groups, half, proj)
    doc_grad = lax.psum_scatter(terms, "dp", scatter_dimension=0)
    doc_dz = (inverse * (doc_grad - doc_units * jnp.sum(doc_grad * doc_units, axis=-1, keepdims=True))).astype(bf16)
    doc_dy = dot(doc_dz, proj_weight, contract_cols)
    proj_grad = dot(doc_y, doc_dz, contract_rows) + dot(query_y, query_dz, contract_rows)
    own = (query_dy, (doc_dy[: half // 2], doc_dy[half // 2 :]), [jnp.zeros((half // 2, model), f32)] * 2)
    received = [jnp.zeros((half // 2, model), bf16)] * 2
    pairs = {}
    vectors, ub, pb = None, None, None
    input_grads = [None, None]
    ready = {}
    chunk_counts = (4, 4, 1, 3)
    order = [(place, i) for place in LINED for i in range(chunk_counts[place])]
    end = ((lax.axis_index("dp") == 0) | (lax.axis_index("dp") == 3)).astype(jnp.int32).reshape(1, 1)
    line = LineSums(end, ready, order) if groups == 4 else None
    plain, marks = {}, []
    board = board + core_other(board)
    mid = model // 2
    lower = core == 0
    proj_half = jnp.where(lower, proj_grad[:mid], proj_grad[mid:])
    proj_half = proj_half + core_other(jnp.where(lower, proj_grad[mid:], proj_grad[:mid]))

    for step in range(3):
        pace["now"] = LATE if step == 2 else EARLY

        def hook(stage, value, step=step):
            if stage == "step":
                return line.step((value,)) if line is not None and step == 2 else ()
            if stage == "end":
                if line is None or step < 2:
                    return ()
                for _ in range(4 if len(LINED) == 4 else 2):
                    line.step()
                return line.last
            pairs[step, stage] = value
            if step < 2:
                return ()
            lefts = kept[2][stage] + kept[1][stage] + kept[0][stage]
            rights = pairs[0, stage] + pairs[1, stage] + value
            if stage == 3:
                lefts, rights = rights, lefts
            if stage == 0:
                size = lefts[0][2] // chunk_counts[0]
                ready[stage] = list(weight_step([(x, offset, size) for x, offset, _ in lefts], rights, 1))
                ready[stage] += weight_step([(x, offset + size, n - size) for x, offset, n in lefts], rights, chunk_counts[0] - 1)
            else:
                ready[stage] = weight_step(lefts, rights, chunk_counts[stage])
            if line is not None and stage == LINED[0]:
                line.start()
            if line is None or stage not in LINED:
                plain[stage] = lax.psum(jnp.concatenate(ready[stage]), "dp").astype(f32)
            return (ready[stage][0],)

        dh, dh_low, vec, ub_now, pb_now, marks_now = backward(flag, received, own[step], w, *contexts[2 - step], records[2 - step], hook, step == 2)
        marks.append(marks_now)
        vectors = vec if vectors is None else vectors + vec
        ub = ub_now if ub is None else ub + ub_now
        pb = pb_now if pb is None else pb + pb_now
        if step < 2:
            received = [to_section(x, [(1, 0)]) for x in dh_low]
        if step >= 1:
            input_grads[2 - step] = lax.dynamic_slice_in_dim(jnp.concatenate(dh), chip * share, share, 0)

    if line is not None:
        results = dict(zip(order, line.finish()))
        parts = {place: [results[place, i] for i in range(chunk_counts[place])] for place in LINED}
        spread = [jnp.concatenate(parts[place], axis=0) if place in parts else plain[place] for place in range(3)]
        d_qkv = jnp.stack([p.T for p in parts[3]], axis=1)
    else:
        spread = [plain[place] for place in range(3)]
        d_qkv = plain[3].T.reshape(model, 3, width)
    d_down, d_up, d_out = spread
    units_count = up_weight.shape[-1]
    small = jnp.concatenate([vectors.reshape(6, model)], axis=0)
    small = small + core_other(small)
    ub = ub[:, :units_count] + core_other(ub[:, units_count:])
    pb = pb[:, :wide] + core_other(pb[:, wide:])
    vector = jnp.concatenate([ub[0], pb[0], small.reshape(-1)]).reshape(-1, LANES)
    vector = dp_sum_after(vector, [line.seen[-6], line.seen[-1]] if line is not None else [()]).reshape(-1)
    proj_half = dp_sum_after(proj_half, [(marks[1][1],), (marks[2][0],)])
    proj_there = core_other(proj_half)
    sent_proj = to_section(jnp.where(lower, proj_half, proj_there), [(1, 0)])
    proj_out = jnp.where(first, sent_proj, jnp.where(lower, proj_there, proj_half))
    ub = vector[:units_count][None]
    pb = vector[units_count : units_count + wide]
    small = vector[units_count + wide :].reshape(6, model)
    stack = jnp.stack(input_grads)
    swap = [(0, 1), (1, 0)]
    docs = groups // 2
    sent_input = to_section(stack[:, :, mid:], swap)
    sent_board = to_section(board[:, :docs], swap)
    return (
        jnp.where(first, sent_board, board[:, docs:]),
        jnp.where(first, stack[:, :, :mid], sent_input),
        d_qkv[None],
        pb.reshape(1, 3, width),
        d_out[None],
        d_up[None],
        ub,
        d_down[None],
        small[0:2][None],
        small[2:4][None],
        small[4:6][None],
        proj_out,
    )


def solution(mesh):
    return jax.shard_map(
        on_device,
        mesh=mesh,
        in_specs=(
            P("dp", "tensor", None),
            P("dp", None),
            P("dp", None),
            P("section", None, None, "tensor"),
            P("section", None, "tensor"),
            P("section", "tensor", None),
            P("section", None, "tensor"),
            P("section", "tensor"),
            P("section", "tensor", None),
            P("section", None, None),
            P("section", None, None),
            P("section", None, None),
            P(),
        ),
        out_specs=(
            P("dp", "section"),
            P("dp", "tensor", "section"),
            P("section", None, None, "tensor"),
            P("section", None, "tensor"),
            P("section", "tensor", None),
            P("section", None, "tensor"),
            P("section", "tensor"),
            P("section", "tensor", None),
            P("section", None, None),
            P("section", None, None),
            P("section", None, None),
            P("section", None),
        ),
        check_vma=False,
    )
```
